32 devices in a mesh: dp: 8 (over z, x), field: 4 (over y, core).
Axes of the slice: x: 2, y: 2, z: 4, core: 2. Of those that a mesh axis runs over, the one named last changes fastest.
Arguments:
- examples: float32 [16384, 512], P('dp', 'field'), may hold values from -6 to 6
- domain: int32 [16384], P('dp'), may hold values from 0 to 15
- labels: int32 [16384, 3], P('dp'), may hold values from 0 to 1
- row_counts: int32 [8], P('dp'), may hold values from 1 to 2048, as said below
- gate_weight: float32 [3, 512, 8], P(None, 'field'), may hold values from -0.25 to 0.25
- gate_bias: float32 [16, 24], replicated, may hold values from -1.5 to 1.5
- w_first: float32 [8, 512, 256], P(None, 'field'), may hold values from -0.25 to 0.25
- b_first: float32 [8, 256], replicated, may hold values from -1.5 to 1.5
- w_second: float32 [8, 256, 256], replicated, may hold values from -0.375 to 0.375
- b_second: float32 [8, 256], replicated, may hold values from -1.5 to 1.5
- tower_first: float32 [3, 256, 128], replicated, may hold values from -0.375 to 0.375
- tower_bias: float32 [3, 128], replicated, may hold values from -1.5 to 1.5
- tower_out: float32 [3, 128], replicated, may hold values from -0.5 to 0.5
- tower_out_bias: float32 [3], replicated, may hold values from -2 to 2
Outputs:
- loss: float32 [], replicated
- grad_examples: float32 [16384, 512], P('dp', 'field')
- grad_gate_weight: float32 [3, 512, 8], P(None, 'field')
- grad_gate_bias: float32 [16, 24], replicated
- grad_w_first: float32 [8, 512, 256], P(None, 'field')
- grad_b_first: float32 [8, 256], replicated
- grad_w_second: float32 [8, 256, 256], replicated
- grad_b_second: float32 [8, 256], replicated
- grad_tower_first: float32 [3, 256, 128], replicated
- grad_tower_bias: float32 [3, 128], replicated
- grad_tower_out: float32 [3, 128], replicated
- grad_tower_out_bias: float32 [3], replicated
The draws below stay inside these ranges and needn't reach their ends.
Inputs may be any that keep to these rules, and one draw needn't show every extreme that they name: `row_counts`: the live rows of an index of dp are the first ones of its block; the last index of dp has all 2048 live.
All inputs are finite; a program needn't handle non-finite values.
Results may differ from the reference program's by a relative error of at most 0.00017.
Values sent between devices are 32-bit elements; how exact they have to be, the bound alone decides.
No kernel may reach another device: no remote copies, remote signals or barrier semaphores. Data moves between devices by JAX's collectives and lax.ppermute only.
A program may use at most 192 MiB of HBM per device.

```python
import math
import jax
import jax.numpy as jnp
import numpy as np
from jax import lax

D_IN = 512
EXPERTS = 8
HIDDEN_SIZE = 256
TASKS = 3
TOWER = 128
DOMAINS = 16
TOK_DEV = 2048
TOKENS = 16384
N_DP = 8


def draw_row_counts(key, part):
    key = jax.random.fold_in(key, 5)
    indices = jnp.arange(N_DP, dtype=jnp.int32)
    lowest = TOK_DEV // 3
    rising = lowest + indices * (TOK_DEV - lowest) // max(N_DP - 1, 1)
    jitter = jax.random.randint(key, (N_DP,), 0, max(TOK_DEV // 8, 2), dtype=jnp.int32)
    counts = jnp.where(indices == N_DP - 1, TOK_DEV, rising - jitter)
    return jnp.clip(counts, 1, TOK_DEV).astype(jnp.int32)


def set_ends(array, own_key, least, top_value):
    place = [jax.random.randint(jax.random.fold_in(own_key, axis), (), 0, length) for axis, length in enumerate(array.shape)]
    longest = array.shape.index(max(array.shape))
    next_to = place[:longest] + [(place[longest] + 1) % array.shape[longest]] + place[longest + 1:]
    return array.at[tuple(place)].set(least).at[tuple(next_to)].set(top_value)


def steps_of(own_key, dims, pieces, smallest, largest):
    gain = 1.0
    for dim, blocks in pieces:
        heights = jax.random.uniform(jax.random.fold_in(jax.random.fold_in(own_key, 6), dim), (blocks,), jnp.float32, smallest / len(pieces), largest / len(pieces))
        gain = gain * jnp.repeat(jnp.exp(heights), dims[dim] // blocks).reshape((-1,) + (1,) * (len(dims) - 1 - dim))
    return gain


def rank_bounds(count, lean):
    weights = [(1 << 20) // math.isqrt(rank ** lean) + 1 for rank in range(1, count + 1)]
    spread = 1 + sum(weights) // (1 << 30)
    return np.cumsum(np.array([max(1, weight // spread) for weight in weights]))


def ranked(rng, shape, count, skew):
    listing = rank_bounds(count, skew)
    pick = jax.random.randint(jax.random.fold_in(rng, 1), shape, 0, int(listing[count - 1]))
    standing = jnp.searchsorted(jnp.asarray(listing, jnp.int32), pick, side="right")
    return jax.random.permutation(jax.random.fold_in(rng, 2), count)[standing].astype(jnp.int32)


def scatter_about(stream_key, extent, deviation, most, shards=(), kind=jnp.bfloat16):
    drawn = jax.random.normal(stream_key, extent, jnp.float32) * deviation
    if len(shards) > 0:
        drawn = steps_of(stream_key, extent, shards, -0.22, 0.18) * drawn
    return jnp.clip(drawn, min=-most, max=most).astype(kind)


def setup_inputs(seed: int = 0) -> dict:
    splits = jax.random.split(jax.random.key(seed), 15)
    return {
        "examples": scatter_about(splits[0], (TOKENS, D_IN), 1.0, 6.0, ((0, 8), (1, 4)), jnp.float32),
        "domain": set_ends(ranked(splits[1], (TOKENS,), DOMAINS, 2), jax.random.fold_in(splits[1], 3), 0, DOMAINS - 1).astype(jnp.int32),
        "labels": set_ends(jax.random.randint(splits[2], (TOKENS, TASKS), 0, 2), jax.random.fold_in(splits[2], 1), 0, 1).astype(jnp.int32),
        "row_counts": draw_row_counts(jax.random.fold_in(splits[14], 71), 0),
        "gate_weight": scatter_about(splits[4], (TASKS, D_IN, EXPERTS), D_IN ** -0.5, 0.25, ((1, 4),), jnp.float32),
        "gate_bias": scatter_about(splits[5], (DOMAINS, TASKS * EXPERTS), 0.3, 1.5, (), jnp.float32),
        "w_first": scatter_about(splits[6], (EXPERTS, D_IN, HIDDEN_SIZE), D_IN ** -0.5, 0.25, ((1, 4),), jnp.float32),
        "b_first": scatter_about(splits[7], (EXPERTS, HIDDEN_SIZE), 0.3, 1.5, (), jnp.float32),
        "w_second": scatter_about(splits[8], (EXPERTS, HIDDEN_SIZE, HIDDEN_SIZE), HIDDEN_SIZE ** -0.5, 0.375, (), jnp.float32),
        "b_second": scatter_about(splits[9], (EXPERTS, HIDDEN_SIZE), 0.3, 1.5, (), jnp.float32),
        "tower_first": scatter_about(splits[10], (TASKS, HIDDEN_SIZE, TOWER), HIDDEN_SIZE ** -0.5, 0.375, (), jnp.float32),
        "tower_bias": scatter_about(splits[11], (TASKS, TOWER), 0.3, 1.5, (), jnp.float32),
        "tower_out": scatter_about(splits[12], (TASKS, TOWER), TOWER ** -0.5, 0.5, (), jnp.float32),
        "tower_out_bias": scatter_about(splits[13], (TASKS,), 0.5, 2.0, (), jnp.float32),
    }


HIGHEST = lax.Precision.HIGHEST

def gelu_exact(values):
    return jax.nn.gelu(values, approximate=False)

def forward(examples, gate_weight, gate_bias, w_first, b_first, w_second, b_second, tower_first, tower_bias, tower_out, tower_out_bias, onehot, targets, weights_live):
    first = jnp.einsum('tc,ech->teh', examples, w_first, precision=HIGHEST) + b_first
    hidden = gelu_exact(first)
    expert_out = jnp.einsum('teh,ehj->tej', hidden, w_second, precision=HIGHEST) + b_second
    logits = jnp.einsum('tc,kce->tke', examples, gate_weight, precision=HIGHEST)
    logits = logits + jnp.dot(onehot, gate_bias, precision=HIGHEST).reshape(logits.shape)
    gates = jax.nn.softmax(logits, axis=-1)
    mixture = jnp.einsum('tke,tej->tkj', gates, expert_out, precision=HIGHEST)
    tower_pre = jnp.einsum('tkj,kjm->tkm', mixture, tower_first, precision=HIGHEST) + tower_bias
    tower_act = gelu_exact(tower_pre)
    score = jnp.einsum('tkm,km->tk', tower_act, tower_out, precision=HIGHEST) + tower_out_bias
    per_item = jax.nn.softplus(score) - targets * score
    return jnp.sum(per_item * weights_live[:, None]) / jnp.sum(weights_live)

def reference(examples, domain, labels, row_counts, gate_weight, gate_bias, w_first, b_first, w_second, b_second, tower_first, tower_bias, tower_out, tower_out_bias):
    positions = jnp.arange(TOKENS, dtype=jnp.int32)
    blocks = positions // TOK_DEV
    weights_live = (positions % TOK_DEV < row_counts[blocks]).astype(jnp.float32)
    onehot = (domain[:, None] == jnp.arange(DOMAINS, dtype=jnp.int32)[None, :]).astype(jnp.float32)
    targets = labels.astype(jnp.float32)

    def objective(examples, gate_weight, gate_bias, w_first, b_first, w_second, b_second, tower_first, tower_bias, tower_out, tower_out_bias):
        return forward(examples, gate_weight, gate_bias, w_first, b_first, w_second, b_second, tower_first, tower_bias, tower_out, tower_out_bias, onehot, targets, weights_live)
    loss, pullback = jax.vjp(objective, examples, gate_weight, gate_bias, w_first, b_first, w_second, b_second, tower_first, tower_bias, tower_out, tower_out_bias)
    grads = pullback(jnp.ones_like(loss))
    return (loss, grads[0], grads[1], grads[2], grads[3], grads[4], grads[5], grads[6], grads[7], grads[8], grads[9], grads[10])
```

```python
import functools

import jax
import jax.numpy as jnp
from jax import lax
from jax.experimental import pallas as pl
from jax.experimental.pallas import tpu as pltpu
from jax.sharding import PartitionSpec as P

F32 = jnp.float32
BF16 = jnp.bfloat16
ROOT_HALF = 0.7071067811865476
DENSITY = 0.3989422804014327
VMEM = pltpu.VMEM
PARAMS = pltpu.CompilerParams(vmem_limit_bytes=58 * 1024 * 1024)
NN, TN, NT = (1, 0), (0, 0), (1, 1)


def split(x):
    high = x.astype(BF16)
    return high, (x - high.astype(F32)).astype(BF16)


def one_dot(a, b, dims):
    return lax.dot_general(a, b, (((dims[0],), (dims[1],)), ((), ())), preferred_element_type=F32)


def dot3(a, b, dims):
    return one_dot(a[0], b[0], dims) + (one_dot(a[0], b[1], dims) + one_dot(a[1], b[0], dims))


def gelu_parts(v):
    cdf = 0.5 + 0.5 * lax.erf(v * ROOT_HALF)
    return v * cdf, cdf + v * (DENSITY * jnp.exp(-0.5 * v * v))


def pick(matrix, index):
    lane = lax.broadcasted_iota(jnp.int32, matrix.shape, 1)
    return jnp.sum(jnp.where(lane == index, matrix, 0.0), axis=1, keepdims=True)


def middle_kernel(
    place,
    factor,
    out_bias,
    x0,
    x1,
    x2,
    x3,
    w0,
    w1,
    w2,
    w3,
    domain,
    labels,
    gate_bias,
    b_first,
    w_second,
    b_second,
    t_first,
    t_bias,
    t_out,
    xt_high,
    xt_low,
    gf_high,
    gf_low,
    gate_rows,
    glog_out,
    s_keep,
    s_send,
    hid_high,
    hid_low,
    slope,
    e_out,
    gates,
    mix,
    gmix,
    ggate,
    b1_cols,
    b2_cols,
    summed,
    rest,
    sems,
):
    experts = w_second.shape[0]
    tasks, width, tower = t_first.shape
    hidden = w_second.shape[1]
    rows = domain.shape[1]
    domains = gate_bias.shape[1]
    cols = w0.shape[1]
    start, count, me, field = place[0], place[1], place[2], place[3]

    for k, ref in enumerate((x0, x1, x2, x3)):
        block = slice(k * cols, (k + 1) * cols)
        high, low = split(ref[0:rows, :].T)
        xt_high[block, :] = high
        xt_low[block, :] = low
        gate_rows[:, block] = ref[rows : rows + tasks * experts, :]
    hot = lax.broadcasted_iota(jnp.int32, (domains, rows), 0) == domain[...]
    onehot = jnp.where(hot, 1.0, 0.0).astype(BF16)
    bias_high, bias_low = split(gate_bias[...])
    logits = dot3(split(gate_rows[...]), (xt_high[...], xt_low[...]), NN)
    logits = logits + (one_dot(bias_high, onehot, NN) + one_dot(bias_low, onehot, NN))
    logits = logits.reshape(tasks, experts, rows)
    raised = jnp.exp(logits - jnp.max(logits, axis=1, keepdims=True))
    soft = raised / jnp.sum(raised, axis=1, keepdims=True)
    gates[...] = soft.reshape(tasks * experts, rows)
    mix[...] = jnp.zeros_like(mix)
    b1_cols[...] = jnp.zeros_like(b1_cols)
    b2_cols[...] = jnp.zeros_like(b2_cols)

    @pl.loop(0, experts)
    def _(e):
        weight = jnp.concatenate([w0[e], w1[e], w2[e], w3[e]], axis=0)
        pre = dot3(split(weight), (xt_high[...], xt_low[...]), TN) + pick(b_first[...], e)
        value, steep = gelu_parts(pre)
        slope[e] = steep
        value = split(value)
        hid_high[e], hid_low[e] = value
        result = dot3(split(w_second[e]), value, TN) + pick(b_second[...], e)
        e_out[e] = result
        for k in range(tasks):
            mix[k] += gates[pl.ds(k * experts + e, 1), :] * result

    position = start + lax.broadcasted_iota(jnp.int32, (1, rows), 1)
    live = jnp.where(position < count, 1.0, 0.0)
    loss = jnp.zeros((1, 1), F32)
    rest[...] = jnp.zeros_like(rest)
    small = width + tower + 4 * tasks * experts
    ones = jnp.ones((8, rows), BF16)
    row_of = lax.broadcasted_iota(jnp.int32, (8, rows), 0)
    lane_of = lax.broadcasted_iota(jnp.int32, (1, tower), 1)
    scalars = jnp.zeros((1, tower), F32)
    for k in range(tasks):
        mixed = split(mix[k])
        weight = split(t_first[k])
        pre = dot3(weight, mixed, TN) + t_bias[:, k : k + 1]
        value, steep = gelu_parts(pre)
        out_column = t_out[:, k : k + 1]
        score = jnp.sum(value * out_column, axis=0, keepdims=True) + out_bias[k]
        target = labels[k : k + 1, :].astype(F32)
        per_item = jnp.maximum(score, 0.0) + jnp.log1p(jnp.exp(-jnp.abs(score))) - target * score
        loss = loss + jnp.sum(per_item * live, axis=1, keepdims=True)
        gscore = live * (jax.nn.sigmoid(score) - target) * factor[0]
        gpre = split(gscore * out_column * steep)
        gweight = dot3(mixed, gpre, NT)
        gbias = one_dot(ones, gpre[0], NT) + one_dot(ones, gpre[1], NT)
        spread = split(jnp.where(row_of == 0, gscore, 0.0))
        gout = dot3(spread, split(value), NT)
        if k < 2:
            rest[0:width, k * tower : (k + 1) * tower] = gweight
        else:
            rest[width : width + tower, 0:tower] = gweight[0:tower]
            rest[width : width + tower, tower:] = gweight[tower:]
        misc = rest.shape[0] - 8
        at = k
        rest[misc + at // 2 : misc + at // 2 + 1, (at % 2) * tower : (at % 2 + 1) * tower] = gbias[0:1]
        at = tasks + k
        rest[misc + at // 2 : misc + at // 2 + 1, (at % 2) * tower : (at % 2 + 1) * tower] = gout[0:1]
        scalars = scalars + jnp.where(lane_of == k, jnp.sum(gscore, axis=1, keepdims=True), 0.0)
        gmix[k] = dot3(weight, gpre, NN)
    scalars = scalars + jnp.where(lane_of == tasks, loss, 0.0)
    rest[misc + tasks : misc + tasks + 1, 0:tower] = scalars

    @pl.loop(0, experts)
    def _(e):
        result = e_out[e]
        total = jnp.zeros_like(result)
        for k in range(tasks):
            down = gmix[k]
            ggate[pl.ds(k * experts + e, 1), :] = jnp.sum(down * result, axis=0, keepdims=True)
            total = total + gates[pl.ds(k * experts + e, 1), :] * down
        lane = lax.broadcasted_iota(jnp.int32, b1_cols.shape, 1)
        b2_cols[...] += jnp.where(lane == e, jnp.sum(total, axis=1, keepdims=True), 0.0)
        total = split(total)
        gweight = dot3((hid_high[e], hid_low[e]), total, NT)
        piece = hidden // 4
        for i in range(4):
            slot = (4 * e + i) ^ me
            summed[slot, 0:piece, :] = gweight[i * piece : (i + 1) * piece]
        gfirst = dot3(split(w_second[e]), total, NN) * slope[e]
        b1_cols[...] += jnp.where(lane == e, jnp.sum(gfirst, axis=1, keepdims=True), 0.0)
        high, low = split(gfirst)
        gf_high[e] = high
        gf_low[e] = low

    soft = gates[...].reshape(tasks, experts, rows)
    gsoft = ggate[...].reshape(tasks, experts, rows)
    glog = soft * (gsoft - jnp.sum(soft * gsoft, axis=1, keepdims=True))
    glog = glog.reshape(tasks * experts, rows)
    glog_out[...] = glog
    glog_parts = split(glog)
    ggw = dot3(glog_parts, (xt_high[...], xt_low[...]), NT)
    base = width + tower
    for k in range(4):
        rest[pl.ds(pl.multiple_of(base + (field ^ k) * tasks * experts, 8), tasks * experts), 0:tower] = ggw[
            :, k * cols : (k + 1) * cols
        ]
    b1_rows = b1_cols[...].T
    b2_rows = b2_cols[...].T
    rest[base : base + 8, tower:] = b1_rows[0:8, 0:tower]
    rest[base + 8 : base + 16, tower:] = b1_rows[0:8, tower:]
    base = base + 4 * tasks * experts
    rest[base : base + 8, :] = b2_rows[0:8]
    base = base + 8
    rest[base : base + domains, 0 : tasks * experts] = one_dot(onehot, glog_parts[0], NT) + one_dot(
        onehot, glog_parts[1], NT
    )
    tail = rest.shape[0] // 32
    for p in range(32):
        slot = p ^ me
        summed[slot, hidden // 4 :, :] = rest[p * tail : (p + 1) * tail, :]
    keep = pltpu.make_async_copy(summed.at[0:16], s_keep, sems.at[0])
    send = pltpu.make_async_copy(summed.at[16:32], s_send, sems.at[1])
    send.start()
    keep.start()
    send.wait()
    keep.wait()


def first_kernel(
    place, xt_high, xt_low, gf_high, gf_low, w0, w1, w2, w3, carried, *rest, first, last
):
    if last:
        keep, send, g0, g1, g2, g3, total = rest
    else:
        keep, send, total_out, total = rest
    step = pl.program_id(0)
    cols = w0.shape[1]
    piece = keep.shape[1] // 8
    halves = cols // piece
    me = place[0]
    parts = (gf_high[0], gf_low[0])
    weight = jnp.concatenate([w0[0], w1[0], w2[0], w3[0]], axis=0)
    gweight = dot3((xt_high[...], xt_low[...]), parts, NT)
    for k in range(4):
        target = (keep, send)[k % 2]
        for i in range(halves):
            slot = (halves * step + i) ^ me
            target[k // 2, pl.ds(pl.multiple_of(slot * piece, 8), piece), :] = gweight[
                k * cols + i * piece : k * cols + (i + 1) * piece
            ]

    @pl.when(step == 0)
    def _():
        if first:
            total[...] = dot3(split(carried[0][...]), split(carried[1][...]), TN)
        else:
            total[...] = carried[...]

    total[...] += dot3(split(weight), parts, NN)

    @pl.when(step == pl.num_programs(0) - 1)
    def _():
        if last:
            for k, ref in enumerate((g0, g1, g2, g3)):
                ref[...] = total[k * cols : (k + 1) * cols, :].T
        else:
            total_out[...] = total[...]


def finish_second_kernel(place, s0, s1, gw2, gtf, ggw, ggb, gb1, gb2, gtb, gto, scal, rest):
    me, field = place[0], place[1]
    hidden = gw2.shape[1]
    piece = hidden // 4
    tasks, width, tower = gtf.shape
    cols, experts = ggw.shape[1], ggw.shape[2]
    domains = ggb.shape[0]
    tail = rest.shape[0] // 32
    for p in range(32):
        slot = p ^ me
        low = slot % 16
        value = jnp.where(slot < 16, s0[low], s1[low])
        gw2[p // 4, (p % 4) * piece : (p % 4 + 1) * piece, :] = value[0:piece]
        rest[p * tail : (p + 1) * tail, :] = value[piece:]
    gtf[0] = rest[0:width, 0:tower]
    gtf[1] = rest[0:width, tower:]
    gtf[2, 0:tower] = rest[width : width + tower, 0:tower]
    gtf[2, tower:] = rest[width : width + tower, tower:]
    base = width + tower
    mine = rest[pl.ds(pl.multiple_of(base + field * tasks * experts, 8), tasks * experts), 0:tower]
    for k in range(tasks):
        ggw[k] = mine[k * experts : (k + 1) * experts].T
    gb1[:, 0:tower] = rest[base : base + 8, tower:]
    gb1[:, tower:] = rest[base + 8 : base + 16, tower:]
    base = base + 4 * tasks * experts
    gb2[...] = rest[base : base + 8, :]
    base = base + 8
    ggb[...] = rest[base : base + domains, 0 : tasks * experts]
    misc = rest.shape[0] - 8
    for k in range(tasks):
        at = k
        gtb[k : k + 1] = rest[misc + at // 2 : misc + at // 2 + 1, (at % 2) * tower : (at % 2 + 1) * tower]
        at = tasks + k
        gto[k : k + 1] = rest[misc + at // 2 : misc + at // 2 + 1, (at % 2) * tower : (at % 2 + 1) * tower]
    scal[...] = rest[misc + tasks : misc + tasks + 1, 0:tower]


def finish_first_kernel(place, a0, a1, b0, b1, out):
    me = place[0]
    half = out.shape[0] // 2
    cols = out.shape[1]
    piece = a0.shape[1]
    for c, (low_ref, high_ref) in enumerate(((a0, a1), (b0, b1))):
        for p in range(8):
            slot = p ^ me
            value = jnp.where(slot < 4, low_ref[slot % 4], high_ref[slot % 4])
            row = p * piece
            out[c * half + row // cols, row % cols : row % cols + piece, :] = value


def finish_inputs_kernel(place, g0, g1, g2, g3, out):
    field = place[0]
    rows = g0.shape[0]
    for k, ref in enumerate((g0, g1, g2, g3)):
        out[pl.ds(pl.multiple_of((field ^ k) * rows, 8), rows), :] = ref[...]


def whole():
    return pl.BlockSpec(memory_space=VMEM)


def scalars():
    return pl.BlockSpec(memory_space=pltpu.SMEM)


def like(shape, dtype=F32):
    return jax.ShapeDtypeStruct(shape, dtype)


def per_device(
    n_dp,
    examples,
    domain,
    labels,
    row_counts,
    gate_weight,
    gate_bias,
    w_first,
    b_first,
    w_second,
    b_second,
    tower_first,
    tower_bias,
    tower_out,
    tower_out_bias,
):
    all_rows, cols = examples.shape
    rows = all_rows // 4
    experts, _, hidden = w_first.shape
    tasks = gate_weight.shape[0]
    width = w_second.shape[2]
    tower = tower_first.shape[2]
    domains = gate_bias.shape[0]
    field = lax.axis_index("field").astype(jnp.int32)
    group = lax.axis_index("dp").astype(jnp.int32)

    def over_field(value, mask):
        return lax.ppermute(value, "field", [(d, d ^ mask) for d in range(4)])

    def over_dp(value, mask):
        return lax.ppermute(value, "dp", [(d, d ^ mask) for d in range(n_dp)])

    core, chip_y = field & 1, field >> 1
    chip_x, z_low, z_high = group & 1, (group >> 1) & 1, (group >> 2) & 1
    me5 = core * 16 + chip_x * 8 + chip_y * 4 + z_low * 2 + z_high
    me3 = chip_x * 4 + z_low * 2 + z_high

    count = row_counts[0]
    total = jnp.minimum(count, all_rows).astype(F32).reshape(1)
    mask = 1
    while mask < n_dp:
        total = total + over_dp(total, mask)
        mask *= 2
    factor = 1.0 / total

    gate_rows = jnp.transpose(gate_weight, (0, 2, 1)).reshape(tasks * experts, cols)
    blocks = []
    for k in range(4):
        mine = lax.dynamic_slice(examples, ((field ^ k) * rows, 0), (rows, cols))
        blocks.append(jnp.concatenate([mine, gate_rows], axis=0))
    blocks = [blocks[0]] + [over_field(blocks[k], k) for k in (1, 2, 3)]
    first_near = over_field(w_first, 1)
    first_far = over_field(w_first, 2)
    first_last = over_field(first_far, 1)
    firsts = (w_first, first_near, first_far, first_last)

    my_domain = lax.dynamic_slice(domain, (field * rows,), (rows,)).reshape(1, rows)
    my_labels = lax.dynamic_slice(labels, (field * rows, 0), (rows, tasks)).T

    units = experts * hidden
    place = jnp.stack([field * rows, count, me5, field]).astype(jnp.int32)
    outs = pl.pallas_call(
        middle_kernel,
        name="middle",
        out_shape=(
            like((4 * cols, rows), BF16),
            like((4 * cols, rows), BF16),
            like((experts, hidden, rows), BF16),
            like((experts, hidden, rows), BF16),
            like((tasks * experts, 4 * cols)),
            like((tasks * experts, rows)),
            like((16, 80, width)),
            like((16, 80, width)),
        ),
        in_specs=[scalars()] * 3 + [whole()] * 17,
        out_specs=[whole()] * 6 + [pl.BlockSpec(memory_space=pl.ANY)] * 2,
        scratch_shapes=[
            VMEM((experts, hidden, rows), BF16),
            VMEM((experts, hidden, rows), BF16),
            VMEM((experts, hidden, rows), F32),
            VMEM((experts, width, rows), F32),
            VMEM((tasks * experts, rows), F32),
            VMEM((tasks, width, rows), F32),
            VMEM((tasks, width, rows), F32),
            VMEM((tasks * experts, rows), F32),
            VMEM((hidden, 128), F32),
            VMEM((width, 128), F32),
            VMEM((32, 80, width), F32),
            VMEM((512, width), F32),
            pltpu.SemaphoreType.DMA((2,)),
        ],
        compiler_params=PARAMS,
        cost_estimate=pl.CostEstimate(
            flops=6 * rows * units * (4 * cols + 3 * width), bytes_accessed=24 << 20, transcendentals=2 * rows * units
        ),
    )(
        place,
        factor,
        tower_out_bias,
        *blocks,
        *firsts,
        my_domain,
        my_labels,
        gate_bias.T,
        b_first.T,
        w_second,
        b_second.T,
        tower_first,
        tower_bias.T,
        tower_out.T,
    )
    xt_high, xt_low, gf_high, gf_low, gate_all, glog, s_keep, s_send = outs

    half = experts // 2
    chunk_rows = half * cols
    place3 = me3.reshape(1)

    def first_call(index, carried):
        last = index == 1
        expert = lambda i: (i + index * half, 0, 0)
        tail_shapes = tuple(like((rows, cols)) for _ in range(4)) if last else (like((4 * cols, rows)),)
        n_carried = 1 if last else 2

        def body(place_ref, *refs):
            ins, others = refs[:8], refs[8:]
            given = others[:n_carried]
            first_kernel(
                place_ref,
                *ins,
                given[0] if last else given,
                *others[n_carried:],
                first=not last,
                last=last,
            )

        return pl.pallas_call(
            body,
            name="first_%d" % index,
            grid=(half,),
            out_shape=(like((2, chunk_rows, hidden)), like((2, chunk_rows, hidden))) + tail_shapes,
            in_specs=[scalars(), whole(), whole()]
            + [pl.BlockSpec((1, hidden, rows), expert)] * 2
            + [pl.BlockSpec((1, cols, hidden), expert)] * 4
            + [whole()] * n_carried,
            out_specs=[whole()] * (2 + len(tail_shapes)),
            scratch_shapes=[VMEM((4 * cols, rows), F32)],
            compiler_params=PARAMS,
            cost_estimate=pl.CostEstimate(
                flops=12 * rows * half * hidden * 4 * cols, bytes_accessed=12 << 20, transcendentals=0
            ),
        )(place3, xt_high, xt_low, gf_high, gf_low, *firsts, *carried)

    def over_rest(value):
        mask = 8
        while mask < n_dp:
            value = value + over_dp(value, mask)
            mask *= 2
        return value

    def halve(kept, got, move, mask):
        n = kept.shape[0] // 2
        send = kept[n:] + got[n:]
        stay = kept[:n] + got[:n]
        return stay, move(send, mask)

    def double(value, move, mask):
        return jnp.concatenate([value, move(value, mask)], axis=0)

    kept, got = s_keep, over_field(s_send, 1)
    kept, got = halve(kept, got, over_dp, 1)
    kept, got = halve(kept, got, over_field, 2)
    kept, got = halve(kept, got, over_dp, 2)
    kept, got = halve(kept, got, over_dp, 4)
    value = over_rest(kept + got)
    value = double(value, over_dp, 4)
    value = double(value, over_dp, 2)
    value = double(value, over_field, 2)
    value = double(value, over_dp, 1)
    other = over_field(value, 1)

    seconds = pl.pallas_call(
        finish_second_kernel,
        name="finish_second",
        out_shape=(
            like((experts, hidden, width)),
            like((tasks, width, tower)),
            like((tasks, cols, experts)),
            like((domains, tasks * experts)),
            like((experts, hidden)),
            like((experts, width)),
            like((tasks, tower)),
            like((tasks, tower)),
            like((1, tower)),
        ),
        in_specs=[scalars()] + [whole()] * 2,
        out_specs=[whole()] * 9,
        scratch_shapes=[VMEM((512, width), F32)],
        compiler_params=PARAMS,
    )(jnp.stack([me5, field]), value, other)
    grad_w_second, grad_tower_first, grad_gate_weight, grad_gate_bias = seconds[:4]
    grad_b_first, grad_b_second, grad_tower_bias, grad_tower_out, scal = seconds[4:]

    def sum_first(keep, send):
        got = over_field(send, 1)
        far = keep[1] + got[1]
        near = keep[0] + got[0]
        kept, got = near.reshape(8, -1, hidden), over_field(far, 2).reshape(8, -1, hidden)
        kept, got = halve(kept, got, over_dp, 1)
        kept, got = halve(kept, got, over_dp, 2)
        kept, got = halve(kept, got, over_dp, 4)
        value = over_rest(kept + got)
        value = double(value, over_dp, 4)
        value = double(value, over_dp, 2)
        return value, over_dp(value, 1)

    keep, send, carried = first_call(0, (gate_all, glog))
    pair_a = sum_first(keep, send)
    keep, send, g0, g1, g2, g3 = first_call(1, (carried,))
    pair_b = sum_first(keep, send)
    grad_w_first = pl.pallas_call(
        finish_first_kernel,
        name="finish_first",
        out_shape=like((experts, cols, hidden)),
        in_specs=[scalars()] + [whole()] * 4,
        out_specs=whole(),
        compiler_params=PARAMS,
    )(place3, *pair_a, *pair_b)

    back = [g0] + [over_field(g, k) for k, g in ((1, g1), (2, g2), (3, g3))]
    grad_examples = pl.pallas_call(
        finish_inputs_kernel,
        name="finish_inputs",
        out_shape=like((all_rows, cols)),
        in_specs=[scalars()] + [whole()] * 4,
        out_specs=whole(),
        compiler_params=PARAMS,
    )(field.reshape(1), *back)

    loss = scal[0, tasks] / total[0]
    return (
        loss,
        grad_examples,
        grad_gate_weight,
        grad_gate_bias,
        grad_w_first,
        grad_b_first,
        grad_w_second,
        grad_b_second,
        grad_tower_first,
        grad_tower_bias,
        grad_tower_out,
        scal[0, :tasks],
    )


def solution(mesh):
    placed = (
        P("dp", "field"),
        P("dp"),
        P("dp", None),
        P("dp"),
        P(None, "field", None),
        P(),
        P(None, "field", None),
        P(),
        P(),
        P(),
        P(),
        P(),
        P(),
        P(),
    )
    return jax.shard_map(
        functools.partial(per_device, mesh.shape["dp"]),
        mesh=mesh,
        in_specs=placed,
        out_specs=(
            P(),
            P("dp", "field"),
            P(None, "field", None),
            P(),
            P(None, "field", None),
            P(),
            P(),
            P(),
            P(),
            P(),
            P(),
            P(),
        ),
        check_vma=False,
    )
```

```python
import functools

import jax
import jax.numpy as jnp
from jax import lax
from jax.experimental import pallas as pl
from jax.experimental.pallas import tpu as pltpu
from jax.sharding import PartitionSpec as P

F32 = jnp.float32
BF16 = jnp.bfloat16
ROOT_HALF = 0.7071067811865476
DENSITY = 0.3989422804014327
VMEM = pltpu.VMEM
PARAMS = pltpu.CompilerParams(vmem_limit_bytes=58 * 1024 * 1024)
NN, TN, NT = (1, 0), (0, 0), (1, 1)


def split(x):
    high = x.astype(BF16)
    return high, (x - high.astype(F32)).astype(BF16)


def one_dot(a, b, dims):
    return lax.dot_general(a, b, (((dims[0],), (dims[1],)), ((), ())), preferred_element_type=F32)


def dot3(a, b, dims):
    return one_dot(a[0], b[0], dims) + (one_dot(a[0], b[1], dims) + one_dot(a[1], b[0], dims))


def gelu_parts(v):
    cdf = 0.5 + 0.5 * lax.erf(v * ROOT_HALF)
    return v * cdf, cdf + v * (DENSITY * jnp.exp(-0.5 * v * v))


def pick(matrix, index):
    lane = lax.broadcasted_iota(jnp.int32, matrix.shape, 1)
    return jnp.sum(jnp.where(lane == index, matrix, 0.0), axis=1, keepdims=True)


def middle_kernel(
    place,
    out_bias,
    x0,
    x1,
    x2,
    x3,
    gate_rows,
    near0,
    near1,
    fa0,
    fa1,
    fa2,
    fa3,
    fb0,
    fb1,
    fb2,
    fb3,
    domain,
    labels,
    gate_bias,
    b_first,
    w_second,
    b_second,
    t_first,
    t_bias,
    t_out,
    xt_high_out,
    xt_low_out,
    gf_high_out,
    gf_low_out,
    w_high_out,
    w_low_out,
    gate_all,
    glog_out,
    s_keep,
    s_send,
    w_in,
    w2_in,
    xt_high,
    xt_low,
    gf_high,
    gf_low,
    w_high,
    w_low,
    hid_high,
    hid_low,
    slope,
    e_out,
    gates,
    mix,
    gmix,
    ggate,
    b1_cols,
    b2_cols,
    summed,
    rest,
    sems,
):
    experts = w_second.shape[0]
    tasks, width, tower = t_first.shape
    hidden = w_second.shape[1]
    rows = domain.shape[1]
    domains = gate_bias.shape[0]
    cols = near0.shape[1]
    start, count, me, field, corner = place[0], place[1], place[2], place[3], place[4]
    units = tasks * experts
    quarter = experts // 4
    order = [(r ^ corner) * quarter + i for r in range(4) for i in range(quarter)]

    loads = []
    for n, e in enumerate(order):
        far_a, far_b = ((fa0, fb0), (fa1, fb1), (fa2, fb2), (fa3, fb3))[n // quarter]
        sources = (near0.at[e], near1.at[e], far_a.at[n % quarter], far_b.at[n % quarter])
        for k, source in enumerate(sources):
            target = w_in.at[n, k * cols : (k + 1) * cols]
            loads.append(pltpu.make_async_copy(source, target, sems.at[5 * n + k]))
        loads.append(pltpu.make_async_copy(w_second.at[e], w2_in.at[n], sems.at[5 * n + 4]))
    for load in loads:
        load.start()

    for k, ref in enumerate((x0, x1, x2, x3)):
        block = slice(k * cols, (k + 1) * cols)
        high, low = split(ref[0:rows, :].T)
        xt_high[block, :] = high
        xt_low[block, :] = low
        gate_all[:, block] = gate_rows[...] if k == 0 else ref[rows : rows + units, :]
    hot = lax.broadcasted_iota(jnp.int32, (domains, rows), 0) == domain[...]
    onehot = jnp.where(hot, 1.0, 0.0).astype(BF16)
    bias_high, bias_low = split(gate_bias[...])
    logits = dot3(split(gate_all[...]), (xt_high[...], xt_low[...]), NN)
    logits = logits + (one_dot(bias_high, onehot, TN) + one_dot(bias_low, onehot, TN))
    logits = logits.reshape(tasks, experts, rows)
    raised = jnp.exp(logits - jnp.max(logits, axis=1, keepdims=True))
    soft = raised / jnp.sum(raised, axis=1, keepdims=True)
    gates[...] = soft.reshape(units, rows)
    mix[...] = jnp.zeros_like(mix)
    b1_cols[...] = jnp.zeros_like(b1_cols)
    b2_cols[...] = jnp.zeros_like(b2_cols)
    b1_in = b_first[...].T
    b2_in = b_second[...].T
    rest[...] = jnp.zeros_like(rest)
    for load in loads:
        load.wait()

    def first_layer(n):
        weight = split(w_in[n])
        w_high[n], w_low[n] = weight
        return dot3(weight, (xt_high[...], xt_low[...]), TN)

    pre = first_layer(0)
    value = None
    for n in range(experts + 1):
        following = first_layer(n + 1) if n + 1 < experts else None
        if n < experts:
            raw, steep = gelu_parts(pre + pick(b1_in, order[n]))
            slope[n] = steep
        if n > 0:
            e = order[n - 1]
            result = dot3(split(w2_in[n - 1]), value, TN) + pick(b2_in, e)
            e_out[n - 1] = result
            for k in range(tasks):
                mix[k] += gates[pl.ds(k * experts + e, 1), :] * result
        if n < experts:
            value = split(raw)
            hid_high[n], hid_low[n] = value
        pre = following

    stores = [
        pltpu.make_async_copy(xt_high, xt_high_out, sems.at[0]),
        pltpu.make_async_copy(xt_low, xt_low_out, sems.at[1]),
    ]
    for n, e in enumerate(order):
        stores.append(pltpu.make_async_copy(w_high.at[n], w_high_out.at[e], sems.at[2 + 2 * n]))
        stores.append(pltpu.make_async_copy(w_low.at[n], w_low_out.at[e], sems.at[3 + 2 * n]))
    for store in stores:
        store.start()

    position = start + lax.broadcasted_iota(jnp.int32, (1, rows), 1)
    live = jnp.where(position < count, 1.0, 0.0)
    loss = jnp.zeros((1, 1), F32)
    ones = jnp.ones((8, rows), BF16)
    row_of = lax.broadcasted_iota(jnp.int32, (8, rows), 0)
    lane_of = lax.broadcasted_iota(jnp.int32, (1, tower), 1)
    scalars = jnp.where(lane_of == tasks + 1, jnp.sum(live, axis=1, keepdims=True), 0.0)
    eye = lax.broadcasted_iota(jnp.int32, (tasks, tower), 0) == lax.broadcasted_iota(jnp.int32, (tasks, tower), 1)
    eye = jnp.where(eye, 1.0, 0.0)
    tb_in = lax.dot_general(t_bias[...], eye, (((0,), (0,)), ((), ())), precision=lax.Precision.HIGHEST)
    to_in = lax.dot_general(t_out[...], eye, (((0,), (0,)), ((), ())), precision=lax.Precision.HIGHEST)
    misc = rest.shape[0] - 8
    for k in range(tasks):
        mixed = split(mix[k])
        weight = split(t_first[k])
        pre = dot3(weight, mixed, TN) + tb_in[:, k : k + 1]
        value, steep = gelu_parts(pre)
        out_column = to_in[:, k : k + 1]
        score = jnp.sum(value * out_column, axis=0, keepdims=True) + out_bias[k]
        target = labels[k : k + 1, :].astype(F32)
        per_item = jnp.maximum(score, 0.0) + jnp.log1p(jnp.exp(-jnp.abs(score))) - target * score
        loss = loss + jnp.sum(per_item * live, axis=1, keepdims=True)
        gscore = live * (jax.nn.sigmoid(score) - target)
        gpre = split(gscore * out_column * steep)
        gweight = dot3(mixed, gpre, NT)
        gbias = one_dot(ones, gpre[0], NT) + one_dot(ones, gpre[1], NT)
        spread = split(jnp.where(row_of == 0, gscore, 0.0))
        gout = dot3(spread, split(value), NT)
        if k < 2:
            rest[0:width, k * tower : (k + 1) * tower] = gweight
        else:
            rest[width : width + tower, 0:tower] = gweight[0:tower]
            rest[width : width + tower, tower:] = gweight[tower:]
        at = k
        rest[misc + at // 2 : misc + at // 2 + 1, (at % 2) * tower : (at % 2 + 1) * tower] = gbias[0:1]
        at = tasks + k
        rest[misc + at // 2 : misc + at // 2 + 1, (at % 2) * tower : (at % 2 + 1) * tower] = gout[0:1]
        scalars = scalars + jnp.where(lane_of == k, jnp.sum(gscore, axis=1, keepdims=True), 0.0)
        gmix[k] = dot3(weight, gpre, NN)
    scalars = scalars + jnp.where(lane_of == tasks, loss, 0.0)
    rest[misc + tasks : misc + tasks + 1, 0:tower] = scalars

    grads = []
    for n, e in enumerate(order):
        result = e_out[n]
        total = None
        for k in range(tasks):
            down = gmix[k]
            ggate[pl.ds(k * experts + e, 1), :] = jnp.sum(down * result, axis=0, keepdims=True)
            part = gates[pl.ds(k * experts + e, 1), :] * down
            total = part if total is None else total + part
        lane = lax.broadcasted_iota(jnp.int32, b1_cols.shape, 1)
        b2_cols[...] += jnp.where(lane == e, jnp.sum(total, axis=1, keepdims=True), 0.0)
        total = split(total)
        gweight = dot3((hid_high[n], hid_low[n]), total, NT)
        piece = hidden // 4
        for i in range(4):
            slot = (4 * e + i) ^ me
            summed[slot, 0:piece, :] = gweight[i * piece : (i + 1) * piece]
        gfirst = dot3(split(w2_in[n]), total, NN) * slope[n]
        b1_cols[...] += jnp.where(lane == e, jnp.sum(gfirst, axis=1, keepdims=True), 0.0)
        high, low = split(gfirst)
        gf_high[n] = high
        gf_low[n] = low
        grads.append(pltpu.make_async_copy(gf_high.at[n], gf_high_out.at[e], sems.at[20 + 2 * n]))
        grads.append(pltpu.make_async_copy(gf_low.at[n], gf_low_out.at[e], sems.at[21 + 2 * n]))
        if n % 4 == 3:
            for copy in grads[-8:]:
                copy.start()

    soft = gates[...].reshape(tasks, experts, rows)
    gsoft = ggate[...].reshape(tasks, experts, rows)
    glog = soft * (gsoft - jnp.sum(soft * gsoft, axis=1, keepdims=True))
    glog = glog.reshape(units, rows)
    glog_out[...] = glog
    glog_parts = split(glog)
    ggw = dot3(glog_parts, (xt_high[...], xt_low[...]), NT)
    base = width + tower
    for k in range(4):
        at = pl.multiple_of(base + (field ^ k) * units, 8)
        rest[pl.ds(at, units), 0:tower] = ggw[:, k * cols : (k + 1) * cols]
    b1_rows = b1_cols[...].T
    b2_rows = b2_cols[...].T
    rest[base : base + 8, tower:] = b1_rows[0:8, 0:tower]
    rest[base + 8 : base + 16, tower:] = b1_rows[0:8, tower:]
    base = base + 4 * units
    rest[base : base + 8, :] = b2_rows[0:8]
    base = base + 8
    rest[base : base + domains, 0:units] = one_dot(onehot, glog_parts[0], NT) + one_dot(onehot, glog_parts[1], NT)
    tail = rest.shape[0] // 32
    for p in range(32):
        slot = p ^ me
        summed[slot, hidden // 4 :, :] = rest[p * tail : (p + 1) * tail, :]
    last = [
        pltpu.make_async_copy(summed.at[16:32], s_send, sems.at[36]),
        pltpu.make_async_copy(summed.at[0:16], s_keep, sems.at[37]),
    ]
    for copy in last:
        copy.start()
    for copy in stores + grads + last:
        copy.wait()


def first_kernel(
    place, xt_high, xt_low, gate_all, glog, gf_high, gf_low, w_high, w_low, keep, send, g0, g1, g2, g3, total
):
    step = pl.program_id(0)
    cols = keep.shape[2]
    parts = (gf_high[0], gf_low[0])
    gweight = dot3((xt_high[...], xt_low[...]), parts, NT)
    slot = step ^ place[0]
    for k in range(4):
        target = (keep, send)[k % 2]
        target[k // 2, slot] = gweight[k * cols : (k + 1) * cols]

    @pl.when(step == 0)
    def _():
        total[...] = dot3(split(gate_all[...]), split(glog[...]), TN)

    total[...] += dot3((w_high[0], w_low[0]), parts, NN)

    @pl.when(step == pl.num_programs(0) - 1)
    def _():
        for k, ref in enumerate((g0, g1, g2, g3)):
            ref[...] = total[k * cols : (k + 1) * cols, :].T


def finish_second_kernel(
    place, a0, a1, a2, a3, b0, b1, b2, b3, gw2, gtf, ggw, ggb, gb1, gb2, gtb, gto, gtob, loss, factor_out, rest
):
    me, field = place[0], place[1]
    hidden = gw2.shape[1]
    piece = hidden // 4
    tasks, width, tower = gtf.shape
    experts = ggw.shape[1]
    units = tasks * experts
    domains = ggb.shape[0]
    tail = rest.shape[0] // 32
    held = (a0, a1, a2, a3, b0, b1, b2, b3)
    for s, ref in enumerate(held):
        for z in range(4):
            p = (s * 4 + z) ^ me
            rest[pl.ds(pl.multiple_of(p * tail, 8), tail), :] = ref[z, piece:]
    misc = rest.shape[0] - 8
    factor = 1.0 / rest[misc + tasks : misc + tasks + 1, tasks + 1 : tasks + 2]
    factor_out[...] = factor
    for s, ref in enumerate(held):
        for z in range(4):
            p = (s * 4 + z) ^ me
            gw2[p // 4, pl.ds(pl.multiple_of((p % 4) * piece, 8), piece), :] = ref[z, 0:piece] * factor
    rest[...] = rest[...] * factor
    gtf[0] = rest[0:width, 0:tower]
    gtf[1] = rest[0:width, tower:]
    gtf[2, 0:tower] = rest[width : width + tower, 0:tower]
    gtf[2, tower:] = rest[width : width + tower, tower:]
    base = width + tower
    mine = rest[pl.ds(pl.multiple_of(base + field * units, 8), units), 0:tower]
    for k in range(tasks):
        ggw[k] = mine[k * experts : (k + 1) * experts]
    gb1[:, 0:tower] = rest[base : base + 8, tower:]
    gb1[:, tower:] = rest[base + 8 : base + 16, tower:]
    base = base + 4 * units
    gb2[...] = rest[base : base + 8, :]
    base = base + 8
    ggb[...] = rest[base : base + domains, 0:units]
    for k in range(tasks):
        at = k
        gtb[k : k + 1] = rest[misc + at // 2 : misc + at // 2 + 1, (at % 2) * tower : (at % 2 + 1) * tower]
        at = tasks + k
        gto[k : k + 1] = rest[misc + at // 2 : misc + at // 2 + 1, (at % 2) * tower : (at % 2 + 1) * tower]
    gtob[...] = rest[misc + tasks : misc + tasks + 1, 0:tasks]
    loss[...] = rest[misc + tasks : misc + tasks + 1, tasks : tasks + 1]


def finish_first_kernel(place, factor, a0, a1, a2, a3, b, out):
    for z, ref in enumerate((a0, a1, a2, a3)):
        out[z ^ place[0]] = ref[...] * factor[...]
        out[(4 + z) ^ place[0]] = b[z] * factor[...]


def finish_inputs_kernel(place, factor, g0, g1, g2, g3, out):
    field = place[0]
    rows = g0.shape[0]
    for k, ref in enumerate((g0, g1, g2, g3)):
        out[pl.ds(pl.multiple_of((field ^ k) * rows, 8), rows), :] = ref[...] * factor[...]


def whole():
    return pl.BlockSpec(memory_space=VMEM)


def anywhere():
    return pl.BlockSpec(memory_space=pl.ANY)


def scalars():
    return pl.BlockSpec(memory_space=pltpu.SMEM)


def like(shape, dtype=F32):
    return jax.ShapeDtypeStruct(shape, dtype)


def after(value, *others):
    return lax.optimization_barrier((value, others))[0]


def per_device(
    n_dp,
    examples,
    domain,
    labels,
    row_counts,
    gate_weight,
    gate_bias,
    w_first,
    b_first,
    w_second,
    b_second,
    tower_first,
    tower_bias,
    tower_out,
    tower_out_bias,
):
    all_rows, cols = examples.shape
    rows = all_rows // 4
    experts, _, hidden = w_first.shape
    tasks = gate_weight.shape[0]
    width = w_second.shape[2]
    tower = tower_first.shape[2]
    domains = gate_bias.shape[0]
    units = tasks * experts
    field = lax.axis_index("field").astype(jnp.int32)
    group = lax.axis_index("dp").astype(jnp.int32)

    def move(value, dp_mask, field_mask):
        pairs = []
        for d in range(n_dp):
            for f in range(4):
                pairs.append((d * 4 + f, (d ^ dp_mask) * 4 + (f ^ field_mask)))
        return lax.ppermute(value, ("dp", "field"), pairs)

    def over_rest(value):
        mask = 8
        while mask < n_dp:
            value = value + move(value, mask, 0)
            mask *= 2
        return value

    core, chip_y = field & 1, field >> 1
    chip_x, chip_z = group & 1, (group >> 1) & 3
    me5 = core * 16 + chip_x * 8 + chip_y * 4 + chip_z
    me3 = chip_x * 4 + chip_z
    corner = group & 3

    count = row_counts[0]

    gate_rows = jnp.transpose(gate_weight, (0, 2, 1)).reshape(units, cols)
    quarter = experts // 4
    far = move(lax.dynamic_slice(w_first, (corner * quarter, 0, 0), (quarter, cols, hidden)), 0, 2)
    near = move(w_first, 0, 1)
    blocks = []
    for k in range(4):
        mine = lax.dynamic_slice(examples, ((field ^ k) * rows, 0), (rows, cols))
        blocks.append(mine if k == 0 else jnp.concatenate([mine, gate_rows], axis=0))
    blocks[1] = move(blocks[1], 0, 1)
    blocks[2] = move(after(blocks[2], far), 0, 2)
    blocks[3] = move(after(blocks[3], far), 0, 3)
    far_a = [far] + [move(far, r, 0) for r in (1, 2, 3)]
    far_b = [move(piece, 0, 1) for piece in far_a]

    my_domain = lax.dynamic_slice(domain, (field * rows,), (rows,)).reshape(1, rows)
    my_labels = lax.dynamic_slice(labels, (field * rows, 0), (rows, tasks)).T

    place = jnp.stack([field * rows, count, me5, field, corner]).astype(jnp.int32)
    outs = pl.pallas_call(
        middle_kernel,
        name="middle",
        out_shape=(
            like((4 * cols, rows), BF16),
            like((4 * cols, rows), BF16),
            like((experts, hidden, rows), BF16),
            like((experts, hidden, rows), BF16),
            like((experts, 4 * cols, hidden), BF16),
            like((experts, 4 * cols, hidden), BF16),
            like((units, 4 * cols)),
            like((units, rows)),
            like((16, 80, width)),
            like((16, 80, width)),
        ),
        in_specs=[scalars()] * 2
        + [whole()] * 5
        + [anywhere()] * 10
        + [whole()] * 4
        + [anywhere()]
        + [whole()] * 4,
        out_specs=[anywhere()] * 6 + [whole()] * 2 + [anywhere()] * 2,
        scratch_shapes=[
            VMEM((experts, 4 * cols, hidden), F32),
            VMEM((experts, hidden, width), F32),
            VMEM((4 * cols, rows), BF16),
            VMEM((4 * cols, rows), BF16),
            VMEM((experts, hidden, rows), BF16),
            VMEM((experts, hidden, rows), BF16),
            VMEM((experts, 4 * cols, hidden), BF16),
            VMEM((experts, 4 * cols, hidden), BF16),
            VMEM((experts, hidden, rows), BF16),
            VMEM((experts, hidden, rows), BF16),
            VMEM((experts, hidden, rows), F32),
            VMEM((experts, width, rows), F32),
            VMEM((units, rows), F32),
            VMEM((tasks, width, rows), F32),
            VMEM((tasks, width, rows), F32),
            VMEM((units, rows), F32),
            VMEM((hidden, 128), F32),
            VMEM((width, 128), F32),
            VMEM((32, 80, width), F32),
            VMEM((512, width), F32),
            pltpu.SemaphoreType.DMA((5 * experts,)),
        ],
        compiler_params=PARAMS,
    )(
        place,
        tower_out_bias,
        *blocks,
        gate_rows,
        w_first,
        near,
        *far_a,
        *far_b,
        my_domain,
        my_labels,
        gate_bias,
        b_first,
        w_second,
        b_second,
        tower_first,
        tower_bias,
        tower_out,
    )
    xt_high, xt_low, gf_high, gf_low, w_high, w_low, gate_all, glog, s_keep, s_send = outs

    got = move(s_send, 0, 1)
    s_parts = [s_keep[4 * q : 4 * q + 4] + got[4 * q : 4 * q + 4] for q in range(4)]
    s_parts = lax.optimization_barrier(s_parts)
    s_got = [move(s_parts[q], q >> 1, (q & 1) * 2) for q in (1, 2, 3)]

    place3 = me3.reshape(1)
    expert = lambda i: (i, 0, 0)
    w_keep, w_send, g0, g1, g2, g3 = pl.pallas_call(
        first_kernel,
        name="first",
        grid=(experts,),
        out_shape=(like((2, 8, cols, hidden)), like((2, 8, cols, hidden))) + (like((rows, cols)),) * 4,
        in_specs=[scalars()]
        + [whole()] * 4
        + [pl.BlockSpec((1, hidden, rows), expert)] * 2
        + [pl.BlockSpec((1, 4 * cols, hidden), expert)] * 2,
        out_specs=[whole()] * 6,
        scratch_shapes=[VMEM((4 * cols, rows), F32)],
        compiler_params=PARAMS,
        cost_estimate=pl.CostEstimate(flops=0, bytes_accessed=1 << 20, transcendentals=0),
    )(place3, xt_high, xt_low, gate_all, glog, after(gf_high, *s_parts), gf_low, w_high, w_low)

    got = move(after(w_send, *s_got), 0, 1)
    w_parts = [w_keep[q & 1, (q >> 1) * 4 : (q >> 1) * 4 + 4] + got[q & 1, (q >> 1) * 4 : (q >> 1) * 4 + 4] for q in range(4)]
    w_parts = lax.optimization_barrier(w_parts)
    w_got = [move(w_parts[q], q >> 1, (q & 1) * 2) for q in (1, 2, 3)]

    s_mine = s_parts[0] + s_got[0] + s_got[1] + s_got[2]
    s_got = [move(s_mine[z], 2 * z, 0) for z in (1, 2, 3)]
    s_piece = over_rest(s_mine[0] + s_got[0] + s_got[1] + s_got[2])
    s_line = jnp.stack([s_piece] + [move(s_piece, 2 * z, 0) for z in (1, 2, 3)])

    w_mine = w_parts[0] + w_got[0] + w_got[1] + w_got[2]
    w_mine, s_line = lax.optimization_barrier((w_mine, s_line))
    w_got = [move(w_mine[z], 2 * z, 0) for z in (1, 2, 3)]
    s_near = [s_line] + [move(s_line, q >> 1, (q & 1) * 2) for q in (1, 2, 3)]
    s_far = [move(part, 0, 1) for part in s_near]
    w_piece = over_rest(w_mine[0] + w_got[0] + w_got[1] + w_got[2])
    w_line = [w_piece] + [move(w_piece, 2 * z, 0) for z in (1, 2, 3)]
    w_other = move(jnp.stack(w_line), 1, 0)

    back = [g0] + [move(after(g, w_piece) if k > 1 else g, 0, k) for k, g in ((1, g1), (2, g2), (3, g3))]
    seconds = pl.pallas_call(
        finish_second_kernel,
        name="finish_second",
        out_shape=(
            like((experts, hidden, width)),
            like((tasks, width, tower)),
            like((tasks, experts, cols)),
            like((domains, units)),
            like((experts, hidden)),
            like((experts, width)),
            like((tasks, tower)),
            like((tasks, tower)),
            like((1, tasks)),
            like((1, 1)),
            like((1, 1)),
        ),
        in_specs=[scalars()] + [whole()] * 8,
        out_specs=[whole()] * 11,
        scratch_shapes=[VMEM((512, width), F32)],
        compiler_params=PARAMS,
    )(jnp.stack([me5, field]), *s_near, *s_far)
    grad_w_second, grad_tower_first, grad_gate_weight, grad_gate_bias = seconds[:4]
    grad_b_first, grad_b_second, grad_tower_bias, grad_tower_out, grad_out_bias, loss, factor = seconds[4:]

    grad_examples = pl.pallas_call(
        finish_inputs_kernel,
        name="finish_inputs",
        out_shape=like((all_rows, cols)),
        in_specs=[scalars()] + [whole()] * 5,
        out_specs=whole(),
        compiler_params=PARAMS,
    )(field.reshape(1), factor, *back)

    grad_w_first = pl.pallas_call(
        finish_first_kernel,
        name="finish_first",
        out_shape=like((experts, cols, hidden)),
        in_specs=[scalars()] + [whole()] * 6,
        out_specs=whole(),
        compiler_params=PARAMS,
    )(place3, factor, *w_line, w_other)

    return (
        loss[0, 0],
        grad_examples,
        jnp.transpose(grad_gate_weight, (0, 2, 1)),
        grad_gate_bias,
        grad_w_first,
        grad_b_first,
        grad_w_second,
        grad_b_second,
        grad_tower_first,
        grad_tower_bias,
        grad_tower_out,
        grad_out_bias[0],
    )


def solution(mesh):
    placed = (
        P("dp", "field"),
        P("dp"),
        P("dp", None),
        P("dp"),
        P(None, "field", None),
        P(),
        P(None, "field", None),
        P(),
        P(),
        P(),
        P(),
        P(),
        P(),
        P(),
    )
    return jax.shard_map(
        functools.partial(per_device, mesh.shape["dp"]),
        mesh=mesh,
        in_specs=placed,
        out_specs=(
            P(),
            P("dp", "field"),
            P(None, "field", None),
            P(),
            P(None, "field", None),
            P(),
            P(),
            P(),
            P(),
            P(),
            P(),
            P(),
        ),
        check_vma=False,
    )
```

```python
import functools

import jax
import jax.numpy as jnp
from jax import lax
from jax.experimental import pallas as pl
from jax.experimental.pallas import tpu as pltpu
from jax.sharding import PartitionSpec as P

F32 = jnp.float32
BF16 = jnp.bfloat16
ROOT_HALF = 0.7071067811865476
DENSITY = 0.3989422804014327
VMEM = pltpu.VMEM
PARAMS = pltpu.CompilerParams(vmem_limit_bytes=58 * 1024 * 1024)
SMALL = pltpu.CompilerParams(vmem_limit_bytes=12 * 1024 * 1024)
NN, TN, NT = (1, 0), (0, 0), (1, 1)


def split(x):
    high = x.astype(BF16)
    return high, (x - high.astype(F32)).astype(BF16)


def one_dot(a, b, dims):
    return lax.dot_general(a, b, (((dims[0],), (dims[1],)), ((), ())), preferred_element_type=F32)


def dot3(a, b, dims):
    return one_dot(a[0], b[0], dims) + (one_dot(a[0], b[1], dims) + one_dot(a[1], b[0], dims))


def gelu_parts(v):
    cdf = 0.5 + 0.5 * lax.erf(v * ROOT_HALF)
    return v * cdf, cdf + v * (DENSITY * jnp.exp(-0.5 * v * v))


def middle_kernel(
    place,
    out_bias,
    x0,
    x1,
    x2,
    x3,
    gate_rows,
    near0,
    near1,
    fa0,
    fa1,
    fa2,
    fa3,
    fb0,
    fb1,
    fb2,
    fb3,
    domain,
    labels,
    gate_bias,
    b_first,
    w_second,
    b_second,
    t_first,
    t_bias,
    t_out,
    xt_high_out,
    xt_low_out,
    gf_high_out,
    gf_low_out,
    w_high_out,
    w_low_out,
    gate_all,
    glog_out,
    s_keep,
    s_send,
    w_in,
    w2_in,
    xt_high,
    xt_low,
    gf_high,
    gf_low,
    w_high,
    w_low,
    hid_high,
    hid_low,
    slope,
    e_out,
    gates,
    soft_rows,
    bias_rows,
    mix,
    gmix,
    ggate,
    scores,
    targets,
    summed,
    rest,
    sems,
):
    experts = w_second.shape[0]
    tasks, width, tower = t_first.shape
    hidden = w_second.shape[1]
    rows = domain.shape[1]
    domains = gate_bias.shape[0]
    cols = near0.shape[1]
    start, count, me, field, corner = place[0], place[1], place[2], place[3], place[4]
    units = tasks * experts
    quarter = experts // 4
    order = [(r ^ corner) * quarter + i for r in range(4) for i in range(quarter)]

    loads = []
    for n, e in enumerate(order):
        far_a, far_b = ((fa0, fb0), (fa1, fb1), (fa2, fb2), (fa3, fb3))[n // quarter]
        sources = (near0.at[e], near1.at[e], far_a.at[n % quarter], far_b.at[n % quarter])
        for k, source in enumerate(sources):
            target = w_in.at[n, k * cols : (k + 1) * cols]
            loads.append(pltpu.make_async_copy(source, target, sems.at[5 * n + k]))
        loads.append(pltpu.make_async_copy(w_second.at[e], w2_in.at[n], sems.at[5 * n + 4]))
    for load in loads:
        load.start()

    wide = tasks * experts
    starts = (0, 0, 0, rows)
    gate_starts = (0, rows, 2 * rows, 2 * rows)
    for k, ref in enumerate((x0, x1, x2, x3)):
        block = slice(k * cols, (k + 1) * cols)
        high, low = split(ref[starts[k] : starts[k] + rows, :].T)
        xt_high[block, :] = high
        xt_low[block, :] = low
        gate_all[:, block] = gate_rows[...] if k == 0 else ref[gate_starts[k] : gate_starts[k] + wide, :]
    hot = lax.broadcasted_iota(jnp.int32, (domains, rows), 0) == domain[pl.ds(field, 1), :]
    onehot = jnp.where(hot, 1.0, 0.0).astype(BF16)
    bias_high, bias_low = split(gate_bias[...])
    logits = dot3(split(gate_all[...]), (xt_high[...], xt_low[...]), NN)
    logits = logits + (one_dot(bias_high, onehot, TN) + one_dot(bias_low, onehot, TN))
    logits = logits.reshape(tasks, experts, rows)
    raised = jnp.exp(logits - jnp.max(logits, axis=1, keepdims=True))
    soft = raised / jnp.sum(raised, axis=1, keepdims=True)
    soft_rows[...] = soft.reshape(units, rows)
    for n, e in enumerate(order):
        for k in range(tasks):
            gates[k * experts + n : k * experts + n + 1, :] = soft_rows[pl.ds(k * experts + e, 1), :]
        bias_rows[n : n + 1, :] = b_first[pl.ds(e, 1), :]
        bias_rows[experts + n : experts + n + 1, :] = b_second[pl.ds(e, 1), :]
    targets[...] = jnp.zeros_like(targets)
    targets[0:tasks, :] = labels[:, pl.ds(pl.multiple_of(field * rows, 128), rows)].astype(F32)
    mix[...] = jnp.zeros_like(mix)
    bias_cols = bias_rows[...].T
    rest[...] = jnp.zeros_like(rest)
    eye = lax.broadcasted_iota(jnp.int32, (tasks, tower), 0) == lax.broadcasted_iota(jnp.int32, (tasks, tower), 1)
    eye = jnp.where(eye, 1.0, 0.0)
    tb_in = lax.dot_general(t_bias[...], eye, (((0,), (0,)), ((), ())), precision=lax.Precision.HIGHEST)
    to_in = lax.dot_general(t_out[...], eye, (((0,), (0,)), ((), ())), precision=lax.Precision.HIGHEST)
    for load in loads:
        load.wait()

    def first_layer(n):
        weight = split(w_in[n])
        w_high[n], w_low[n] = weight
        return dot3(weight, (xt_high[...], xt_low[...]), TN)

    pre = first_layer(0)
    value = None
    for n in range(experts + 1):
        following = first_layer(n + 1) if n + 1 < experts else None
        if n < experts:
            raw, steep = gelu_parts(pre + bias_cols[:, n : n + 1])
            slope[n] = steep
        if n > 0:
            at = experts + n - 1
            result = dot3(split(w2_in[n - 1]), value, TN) + bias_cols[:, at : at + 1]
            e_out[n - 1] = result
            for k in range(tasks):
                mix[k] += gates[k * experts + n - 1 : k * experts + n, :] * result
        if n < experts:
            value = split(raw)
            hid_high[n], hid_low[n] = value
        pre = following

    stores = [
        pltpu.make_async_copy(xt_high, xt_high_out, sems.at[0]),
        pltpu.make_async_copy(xt_low, xt_low_out, sems.at[1]),
    ]
    for n, e in enumerate(order):
        stores.append(pltpu.make_async_copy(w_high.at[n], w_high_out.at[e], sems.at[2 + 2 * n]))
        stores.append(pltpu.make_async_copy(w_low.at[n], w_low_out.at[e], sems.at[3 + 2 * n]))
    for store in stores:
        store.start()

    position = start + lax.broadcasted_iota(jnp.int32, (1, rows), 1)
    live = jnp.where(position < count, 1.0, 0.0)
    row_of = lax.broadcasted_iota(jnp.int32, (8, rows), 0)
    misc = rest.shape[0] - 8
    scores[...] = jnp.zeros_like(scores)
    acts, steeps, mixed, weights = [], [], [], []
    for k in range(tasks):
        mixed.append(split(mix[k]))
        weights.append(split(t_first[k]))
        value, steep = gelu_parts(dot3(weights[k], mixed[k], TN) + tb_in[:, k : k + 1])
        out_column = to_in[:, k : k + 1]
        scores[k : k + 1, :] = jnp.sum(value * out_column, axis=0, keepdims=True) + out_bias[k]
        acts.append(value)
        steeps.append(out_column * steep)
    score = scores[...]
    target = targets[...]
    task_live = jnp.where(row_of < tasks, live, 0.0)
    per_item = jnp.maximum(score, 0.0) + jnp.log1p(jnp.exp(-jnp.abs(score))) - target * score
    gscores = task_live * (jax.nn.sigmoid(score) - target)
    sums = jnp.sum(gscores, axis=1, keepdims=True)
    losses = jnp.sum(per_item * task_live, axis=(0, 1), keepdims=True)
    t_sums = []
    for k in range(tasks):
        gpre = gscores[k : k + 1, :] * steeps[k]
        t_sums.append(jnp.sum(gpre, axis=1, keepdims=True))
        t_sums.append(jnp.sum(gscores[k : k + 1, :] * acts[k], axis=1, keepdims=True))
        gpre = split(gpre)
        gmix[k] = dot3(weights[k], gpre, NN)
        gweight = dot3(mixed[k], gpre, NT)
        if k < 2:
            rest[0:width, k * tower : (k + 1) * tower] = gweight
        else:
            rest[width : width + tower, 0:tower] = gweight[0:tower]
            rest[width : width + tower, tower:] = gweight[tower:]
        rest[misc + tasks : misc + tasks + 1, k : k + 1] = sums[k : k + 1, :]
    rest[misc + tasks : misc + tasks + 1, tasks : tasks + 1] = losses

    grads = []
    b1_sums, b2_sums = [], []
    for n, e in enumerate(order):
        result = e_out[n]
        total = None
        for k in range(tasks):
            down = gmix[k]
            at = k * experts + n
            ggate[at : at + 1, :] = jnp.sum(down * result, axis=0, keepdims=True)
            part = gates[at : at + 1, :] * down
            total = part if total is None else total + part
        b2_sums.append(jnp.sum(total, axis=1, keepdims=True))
        total = split(total)
        gweight = dot3((hid_high[n], hid_low[n]), total, NT)
        piece = hidden // 4
        for i in range(4):
            slot = (4 * e + i) ^ me
            summed[slot, 0:piece, :] = gweight[i * piece : (i + 1) * piece]
        gfirst = dot3(split(w2_in[n]), total, NN) * slope[n]
        b1_sums.append(jnp.sum(gfirst, axis=1, keepdims=True))
        high, low = split(gfirst)
        gf_high[n] = high
        gf_low[n] = low
        grads.append(pltpu.make_async_copy(gf_high.at[n], gf_high_out.at[e], sems.at[20 + 2 * n]))
        grads.append(pltpu.make_async_copy(gf_low.at[n], gf_low_out.at[e], sems.at[21 + 2 * n]))
        if n % 2 == 1:
            for copy in grads[-4:]:
                copy.start()

    piece = hidden // 4
    last = [
        pltpu.make_async_copy(summed.at[16:32, 0:piece], s_send.at[:, 0:piece], sems.at[36]),
        pltpu.make_async_copy(summed.at[0:16, 0:piece], s_keep.at[:, 0:piece], sems.at[37]),
        pltpu.make_async_copy(summed.at[16:32, piece:], s_send.at[:, piece:], sems.at[38]),
        pltpu.make_async_copy(summed.at[0:16, piece:], s_keep.at[:, piece:], sems.at[39]),
    ]
    last[0].start()
    last[1].start()

    lane = lax.broadcasted_iota(jnp.int32, (width, 128), 1)
    lane_t = lax.broadcasted_iota(jnp.int32, (tower, tower), 1)
    t_cols = jnp.zeros((tower, tower), F32)
    for n, column in enumerate(t_sums):
        t_cols = jnp.where(lane_t == n, column, t_cols)
    t_cols = t_cols.T
    for k in range(tasks):
        for at, n in ((k, 2 * k), (tasks + k, 2 * k + 1)):
            side = slice((at % 2) * tower, (at % 2 + 1) * tower)
            rest[misc + at // 2 : misc + at // 2 + 1, side] = t_cols[n : n + 1, :]
    sums = jnp.zeros((width, 128), F32)
    for n in range(experts):
        sums = jnp.where(lane == n, b1_sums[n], sums)
        sums = jnp.where(lane == experts + n, b2_sums[n], sums)
    sums = sums.T
    soft = gates[...].reshape(tasks, experts, rows)
    gsoft = ggate[...].reshape(tasks, experts, rows)
    glog = soft * (gsoft - jnp.sum(soft * gsoft, axis=1, keepdims=True))
    gates[...] = glog.reshape(units, rows)
    base = 2 * tower + tower + 2 * units
    for n, e in enumerate(order):
        for k in range(tasks):
            glog_out[pl.ds(k * experts + e, 1), :] = gates[k * experts + n : k * experts + n + 1, :]
        rest[pl.ds(base + e, 1), :] = sums[n : n + 1, :]
        rest[pl.ds(base + experts + e, 1), :] = sums[experts + n : experts + n + 1, :]
    glog_parts = split(glog_out[...])
    ggw = dot3(glog_parts, (xt_high[...], xt_low[...]), NT)
    base = width + tower
    for k in range(4):
        at = pl.multiple_of(base + ((field ^ k) >> 1) * units, 8)
        part = ggw[:, k * cols : (k + 1) * cols]
        low_side = ((field ^ k) & 1) == 0
        rest[pl.ds(at, units), 0:tower] = jnp.where(low_side, part, rest[pl.ds(at, units), 0:tower])
        rest[pl.ds(at, units), tower:] = jnp.where(low_side, rest[pl.ds(at, units), tower:], part)
    base = base + 2 * units + 2 * experts
    rest[base : base + domains, 0:units] = one_dot(onehot, glog_parts[0], NT) + one_dot(onehot, glog_parts[1], NT)
    alive = jnp.broadcast_to(jnp.sum(live, axis=1, keepdims=True), (1, width))
    tail = rest.shape[0] // 32
    for p in range(32):
        slot = p ^ me
        summed[slot, hidden // 4 :, :] = jnp.concatenate([rest[p * tail : (p + 1) * tail, :], alive], axis=0)
    last[2].start()
    last[3].start()
    for copy in stores + grads + last:
        copy.wait()


def first_kernel(
    place,
    xt_high_in,
    xt_low_in,
    gf_high_in,
    gf_low_in,
    keep_a,
    send_a,
    keep_b,
    send_b,
    xt_high,
    xt_low,
    gf_high,
    gf_low,
    keep,
    send,
    sems,
):
    experts, cols = keep.shape[0], keep.shape[2]
    loads = [
        pltpu.make_async_copy(xt_high_in, xt_high, sems.at[0]),
        pltpu.make_async_copy(xt_low_in, xt_low, sems.at[1]),
    ]
    for n in range(experts):
        loads.append(pltpu.make_async_copy(gf_high_in.at[n], gf_high.at[n], sems.at[2 + 2 * n]))
        loads.append(pltpu.make_async_copy(gf_low_in.at[n], gf_low.at[n], sems.at[3 + 2 * n]))
    for copy in loads:
        copy.start()
    for copy in loads[0:2]:
        copy.wait()
    stores = []
    for n in range(experts):
        if n % 2 == 0:
            for copy in loads[2 + 2 * n : 6 + 2 * n]:
                copy.wait()
        gweight = dot3((xt_high[...], xt_low[...]), (gf_high[n], gf_low[n]), NT)
        slot = n ^ place[0]
        for k in range(4):
            held, outs = ((keep, (keep_a, keep_b)), (send, (send_a, send_b)))[k % 2]
            held[n, k // 2] = gweight[k * cols : (k + 1) * cols]
            for h, out in enumerate(outs):
                at = sems.at[2 + 2 * experts + 8 * n + 2 * k + h]
                part = held.at[n, k // 2, h * (cols // 2) : (h + 1) * (cols // 2)]
                stores.append(pltpu.make_async_copy(part, out.at[k // 2, slot], at))
        if n % 2 == 1:
            for copy in stores[-16:]:
                copy.start()
    for copy in stores:
        copy.wait()


def inputs_kernel(
    gate_all, glog, gf_high_in, gf_low_in, w_high_in, w_low_in, g0, gc, gy, gf_high, gf_low, w_high, w_low, total, sems
):
    experts = gf_high.shape[0]
    rows, cols = g0.shape
    loads = []
    sources = ((gf_high_in, gf_high), (gf_low_in, gf_low), (w_high_in, w_high), (w_low_in, w_low))
    for n in range(experts):
        for m, (source, target) in enumerate(sources):
            loads.append(pltpu.make_async_copy(source.at[n], target.at[n], sems.at[4 * n + m]))
    for copy in loads:
        copy.start()
    total[...] = dot3(split(gate_all[...]), split(glog[...]), TN)
    for n in range(experts):
        if n % 2 == 0:
            for copy in loads[4 * n : 4 * n + 8]:
                copy.wait()
        total[...] += dot3((w_high[n], w_low[n]), (gf_high[n], gf_low[n]), NN)
    g0[...] = total[0:cols, :].T
    gc[0:rows, :] = total[cols : 2 * cols, :].T
    gc[rows:, :] = total[3 * cols :, :].T
    gy[...] = total[2 * cols : 3 * cols, :].T


def finish_second_kernel(
    place, a0, a1, a2, a3, b0, b1, b2, b3, gw2, gtf, ggw, ggb, gb1, gb2, gtb, gto, gtob, loss, parts, rest
):
    me, field = place[0], place[1]
    hidden = gw2.shape[1]
    piece = hidden // 4
    tasks, width, tower = gtf.shape
    experts = ggw.shape[1]
    units = tasks * experts
    domains = ggb.shape[0]
    tail = rest.shape[0] // 32
    half = (piece + tail + 1) // 2
    for s, (ref_a, ref_b) in enumerate(((a0, a1), (a2, a3), (b0, b1), (b2, b3))):
        for i in range(2):
            for z in range(4):
                p = ((s // 2) * 16 + ((s % 2) * 2 + i) * 4 + z) ^ me
                gw2[p // 4, pl.ds(pl.multiple_of((p % 4) * piece, 8), half), :] = ref_a[i, z]
                p = ((s // 2) * 16 + ((s % 2) + 2 * i) * 4 + z) ^ me
                at = pl.multiple_of((p % 4) * piece + half, 8)
                gw2[p // 4, pl.ds(at, piece - half), :] = ref_b[i, z, 0 : piece - half]
                parts[p] = ref_b[i, z, piece - half :]
    for p in range(32):
        rest[p * tail : (p + 1) * tail, :] = parts[p, 0:tail]
    gtf[0] = rest[0:width, 0:tower]
    gtf[1] = rest[0:width, tower:]
    gtf[2, 0:tower] = rest[width : width + tower, 0:tower]
    gtf[2, tower:] = rest[width : width + tower, tower:]
    base = width + tower
    mine = rest[pl.ds(pl.multiple_of(base + (field >> 1) * units, 8), units), :]
    mine = jnp.where((field & 1) == 0, mine[:, 0:tower], mine[:, tower:])
    for k in range(tasks):
        ggw[k] = mine[k * experts : (k + 1) * experts]
    base = base + 2 * units
    gb1[...] = rest[base : base + experts, :]
    gb2[...] = rest[base + experts : base + 2 * experts, :]
    base = base + 2 * experts
    ggb[...] = rest[base : base + domains, 0:units]
    misc = rest.shape[0] - 8
    for k in range(tasks):
        at = k
        gtb[k : k + 1] = rest[misc + at // 2 : misc + at // 2 + 1, (at % 2) * tower : (at % 2 + 1) * tower]
        at = tasks + k
        gto[k : k + 1] = rest[misc + at // 2 : misc + at // 2 + 1, (at % 2) * tower : (at % 2 + 1) * tower]
    gtob[...] = rest[misc + tasks : misc + tasks + 1, 0:tasks]
    loss[...] = rest[misc + tasks : misc + tasks + 1, tasks : tasks + 1]


def place_near_kernel(place, a0, a1, a2, a3, out, sems):
    copies = [
        pltpu.make_async_copy(ref, out.at[z ^ place[0]], sems.at[z]) for z, ref in enumerate((a0, a1, a2, a3))
    ]
    for copy in copies:
        copy.start()
    for copy in copies:
        copy.wait()


def place_far_kernel(place, b, begun, out, sems):
    copies = [pltpu.make_async_copy(b.at[z], out.at[(4 + z) ^ place[0]], sems.at[z]) for z in range(4)]
    for copy in copies:
        copy.start()
    for copy in copies:
        copy.wait()


def finish_inputs_kernel(place, factor, g0, gc, gy, out):
    field = place[0]
    rows = g0.shape[0]
    for k, ref in enumerate((g0, gc, gy, gy)):
        at = rows if k == 3 else 0
        out[pl.ds(pl.multiple_of((field ^ k) * rows, 8), rows), :] = ref[at : at + rows, :] * factor[...]


def whole():
    return pl.BlockSpec(memory_space=VMEM)


def anywhere():
    return pl.BlockSpec(memory_space=pl.ANY)


def scalars():
    return pl.BlockSpec(memory_space=pltpu.SMEM)


def like(shape, dtype=F32):
    return jax.ShapeDtypeStruct(shape, dtype)


def after(value, *others):
    return lax.optimization_barrier((value, others))[0]


def per_device(
    n_dp,
    examples,
    domain,
    labels,
    row_counts,
    gate_weight,
    gate_bias,
    w_first,
    b_first,
    w_second,
    b_second,
    tower_first,
    tower_bias,
    tower_out,
    tower_out_bias,
):
    all_rows, cols = examples.shape
    rows = all_rows // 4
    experts, _, hidden = w_first.shape
    tasks = gate_weight.shape[0]
    width = w_second.shape[2]
    tower = tower_first.shape[2]
    domains = gate_bias.shape[0]
    units = tasks * experts
    field = lax.axis_index("field").astype(jnp.int32)
    group = lax.axis_index("dp").astype(jnp.int32)

    def move(value, dp_mask, field_mask):
        pairs = []
        for d in range(n_dp):
            for f in range(4):
                pairs.append((d * 4 + f, (d ^ dp_mask) * 4 + (f ^ field_mask)))
        return lax.ppermute(value, ("dp", "field"), pairs)

    def over_rest(value):
        mask = 8
        while mask < n_dp:
            value = value + move(value, mask, 0)
            mask *= 2
        return value

    core, chip_y = field & 1, field >> 1
    chip_x, chip_z = group & 1, (group >> 1) & 3
    me5 = core * 16 + chip_x * 8 + chip_y * 4 + chip_z
    me3 = chip_x * 4 + chip_z
    corner = group & 3

    count = row_counts[0]

    gate_rows = jnp.transpose(gate_weight, (0, 2, 1)).reshape(units, cols)
    quarter = experts // 4

    def rows_for(k):
        return lax.dynamic_slice(examples, ((field ^ k) * rows, 0), (rows, cols))

    far = move(lax.dynamic_slice(w_first, (corner * quarter, 0, 0), (quarter, cols, hidden)), 0, 2)
    near = move(w_first, 0, 1)
    place = jnp.stack([field * rows, count, me5, field, corner]).astype(jnp.int32)
    domain = domain.reshape(4, rows)
    x0 = rows_for(0)
    near_rows = jnp.concatenate([rows_for(1), gate_rows], axis=0)
    y_rows = jnp.concatenate([rows_for(2), rows_for(3), gate_rows], axis=0)
    early = (far, near, near_rows, y_rows, x0, place, domain)
    far, near, near_rows, y_rows, x0, place, domain = lax.optimization_barrier(early)

    x2 = move(y_rows, 0, 2)
    x1 = move(near_rows, 0, 1)
    far_a = [far] + [move(far, r, 0) for r in (1, 2, 3)]
    x1, x2, far_a = lax.optimization_barrier((x1, x2, far_a))

    x3 = move(x2, 0, 1)
    far_b = [move(piece, 0, 1) for piece in far_a]

    outs = pl.pallas_call(
        middle_kernel,
        name="middle",
        out_shape=(
            like((4 * cols, rows), BF16),
            like((4 * cols, rows), BF16),
            like((experts, hidden, rows), BF16),
            like((experts, hidden, rows), BF16),
            like((experts, 4 * cols, hidden), BF16),
            like((experts, 4 * cols, hidden), BF16),
            like((units, 4 * cols)),
            like((units, rows)),
            like((16, 80, width)),
            like((16, 80, width)),
        ),
        in_specs=[scalars()] * 2
        + [whole()] * 5
        + [anywhere()] * 10
        + [whole()] * 4
        + [anywhere()]
        + [whole()] * 4,
        out_specs=[anywhere()] * 6 + [whole()] * 2 + [anywhere()] * 2,
        scratch_shapes=[
            VMEM((experts, 4 * cols, hidden), F32),
            VMEM((experts, hidden, width), F32),
            VMEM((4 * cols, rows), BF16),
            VMEM((4 * cols, rows), BF16),
            VMEM((experts, hidden, rows), BF16),
            VMEM((experts, hidden, rows), BF16),
            VMEM((experts, 4 * cols, hidden), BF16),
            VMEM((experts, 4 * cols, hidden), BF16),
            VMEM((experts, hidden, rows), BF16),
            VMEM((experts, hidden, rows), BF16),
            VMEM((experts, hidden, rows), F32),
            VMEM((experts, width, rows), F32),
            VMEM((units, rows), F32),
            VMEM((units, rows), F32),
            VMEM((2 * experts, hidden), F32),
            VMEM((tasks, width, rows), F32),
            VMEM((tasks, width, rows), F32),
            VMEM((units, rows), F32),
            VMEM((8, rows), F32),
            VMEM((8, rows), F32),
            VMEM((32, 80, width), F32),
            VMEM((480, width), F32),
            pltpu.SemaphoreType.DMA((5 * experts,)),
        ],
        compiler_params=PARAMS,
    )(
        place,
        tower_out_bias,
        x0,
        x1,
        x2,
        x3,
        gate_rows,
        w_first,
        near,
        *far_a,
        *far_b,
        domain,
        labels.T,
        gate_bias,
        b_first,
        w_second,
        b_second,
        tower_first,
        tower_bias,
        tower_out,
    )
    xt_high, xt_low, gf_high, gf_low, w_high, w_low, gate_all, glog, s_keep, s_send = outs

    place3 = me3.reshape(1)
    cheap = pl.CostEstimate(flops=0, bytes_accessed=1 << 20, transcendentals=0)

    def fold(keep, got, axis):
        held = keep + got
        return lax.index_in_dim(held, 0, axis, False), lax.index_in_dim(held, 1, axis, False)

    s_keep = s_keep.reshape(2, 2, 4, 80, width)
    s_got = move(s_send, 0, 1).reshape(2, 2, 4, 80, width)
    sa, sa_out = fold(s_keep[:, :, :, 0:40], s_got[:, :, :, 0:40], 0)
    sb, sb_out = fold(s_keep[:, :, :, 40:80], s_got[:, :, :, 40:80], 1)
    sa, sa_out, sb, sb_out, gf_high = lax.optimization_barrier((sa, sa_out, sb, sb_out, gf_high))

    sa_got, sb_got = move(sa_out, 1, 0), move(sb_out, 0, 2)
    wa_keep, wa_send, wb_keep, wb_send = pl.pallas_call(
        first_kernel,
        name="first",
        out_shape=tuple(like((2, 8, cols // 2, hidden)) for _ in range(4)),
        in_specs=[scalars()] + [anywhere()] * 4,
        out_specs=[anywhere()] * 4,
        scratch_shapes=[
            VMEM((4 * cols, rows), BF16),
            VMEM((4 * cols, rows), BF16),
            VMEM((experts, hidden, rows), BF16),
            VMEM((experts, hidden, rows), BF16),
            VMEM((experts, 2, cols, hidden), F32),
            VMEM((experts, 2, cols, hidden), F32),
            pltpu.SemaphoreType.DMA((10 * experts + 2,)),
        ],
        compiler_params=PARAMS,
        cost_estimate=cheap,
    )(place3, xt_high, xt_low, gf_high, gf_low)
    wa_got, wb_got = move(wa_send, 0, 1), move(wb_send, 0, 1)
    sa, sa_out = fold(sa, sa_got, 0)
    sb, sb_out = fold(sb, sb_got, 0)
    sa_got, sb_got = move(sa_out, 0, 2), move(sb_out, 1, 0)
    s_mine = jnp.concatenate([sa + sa_got, sb + sb_got], axis=1)
    slots = (2, 2, 4, cols // 2, hidden)
    wa, wa_out = fold(wa_keep.reshape(slots), wa_got.reshape(slots), 0)
    wb, wb_out = fold(wb_keep.reshape(slots), wb_got.reshape(slots), 1)
    stage = (wa, wa_out, wb, wb_out, s_mine, gf_low)
    wa, wa_out, wb, wb_out, s_mine, gf_low = lax.optimization_barrier(stage)

    wa_got, wb_got = move(wa_out, 0, 2), move(wb_out, 1, 0)
    s_got = [move(s_mine[z], 2 * z, 0) for z in (1, 2, 3)]
    wa, wa_out = fold(wa, wa_got, 0)
    wb, wb_out = fold(wb, wb_got, 0)
    wa_got, wb_got = move(wa_out, 1, 0), move(wb_out, 0, 2)
    s_piece = over_rest(s_mine[0] + s_got[0] + s_got[1] + s_got[2])
    factor = 1.0 / s_piece[79:80, 0:1]
    s_piece = s_piece * factor
    s_line = jnp.stack([s_piece] + [move(s_piece, 2 * z, 0) for z in (1, 2, 3)])
    w_mine = jnp.concatenate([wa + wa_got, wb + wb_got], axis=1)
    w_mine, s_line, gf_low = lax.optimization_barrier((w_mine, s_line, gf_low))

    g0, gc, gy = pl.pallas_call(
        inputs_kernel,
        name="inputs",
        out_shape=(like((rows, cols)), like((2 * rows, cols)), like((rows, cols))),
        in_specs=[whole()] * 2 + [anywhere()] * 4,
        out_specs=[whole()] * 3,
        scratch_shapes=[
            VMEM((experts, hidden, rows), BF16),
            VMEM((experts, hidden, rows), BF16),
            VMEM((experts, 4 * cols, hidden), BF16),
            VMEM((experts, 4 * cols, hidden), BF16),
            VMEM((4 * cols, rows), F32),
            pltpu.SemaphoreType.DMA((4 * experts,)),
        ],
        compiler_params=PARAMS,
        cost_estimate=cheap,
    )(gate_all, glog, gf_high, gf_low, w_high, w_low)
    w_got = [move(w_mine[z], 2 * z, 0) for z in (1, 2, 3)]
    sa, sb = s_line[:, 0:40], s_line[:, 40:80]
    sa = jnp.stack([sa, move(sa, 0, 2)])
    sb = jnp.stack([sb, move(sb, 1, 0)])
    w_piece = over_rest(w_mine[0] + w_got[0] + w_got[1] + w_got[2]) * factor
    w_piece, sa, sb, g0, gc, gy = lax.optimization_barrier((w_piece, sa, sb, g0, gc, gy))

    gc = move(gc, 0, 1)
    w_line = [w_piece] + [move(w_piece, 2 * z, 0) for z in (1, 2, 3)]
    s_near = [sa, sb, move(sa, 1, 0), move(sb, 0, 2)]
    gy = jnp.concatenate([gy, gc[rows:]], axis=0)
    w_line, s_near, gy = lax.optimization_barrier((w_line, s_near, gy))

    w_other = move(jnp.stack(w_line), 1, 0)
    gy = move(gy, 0, 2)
    s_far = [move(part, 0, 1) for part in s_near]

    seconds = pl.pallas_call(
        finish_second_kernel,
        name="finish_second",
        out_shape=(
            like((experts, hidden, width)),
            like((tasks, width, tower)),
            like((tasks, experts, cols)),
            like((domains, units)),
            like((experts, hidden)),
            like((experts, width)),
            like((tasks, tower)),
            like((tasks, tower)),
            like((1, tasks)),
            like((1, 1)),
        ),
        in_specs=[scalars()] + [whole()] * 8,
        out_specs=[whole()] * 10,
        scratch_shapes=[VMEM((32, 16, width), F32), VMEM((480, width), F32)],
        compiler_params=SMALL,
    )(jnp.stack([me5, field]), *s_near, *s_far)
    grad_w_second, grad_tower_first, grad_gate_weight, grad_gate_bias = seconds[:4]
    grad_b_first, grad_b_second, grad_tower_bias, grad_tower_out, grad_out_bias, loss = seconds[4:]

    grad_examples = pl.pallas_call(
        finish_inputs_kernel,
        name="finish_inputs",
        out_shape=like((all_rows, cols)),
        in_specs=[scalars()] + [whole()] * 4,
        out_specs=whole(),
        compiler_params=SMALL,
    )(field.reshape(1), factor, g0, gc, gy)

    begun = pl.pallas_call(
        place_near_kernel,
        name="place_near",
        out_shape=like((experts, cols, hidden)),
        in_specs=[scalars()] + [anywhere()] * 4,
        out_specs=anywhere(),
        scratch_shapes=[pltpu.SemaphoreType.DMA((4,))],
        compiler_params=SMALL,
    )(place3, *w_line)
    grad_w_first = pl.pallas_call(
        place_far_kernel,
        name="place_far",
        out_shape=like((experts, cols, hidden)),
        in_specs=[scalars(), anywhere(), anywhere()],
        out_specs=anywhere(),
        scratch_shapes=[pltpu.SemaphoreType.DMA((4,))],
        input_output_aliases={2: 0},
        compiler_params=SMALL,
    )(place3, w_other, after(begun, grad_examples, grad_w_second))

    return (
        loss[0, 0],
        grad_examples,
        jnp.transpose(grad_gate_weight, (0, 2, 1)),
        grad_gate_bias,
        grad_w_first,
        grad_b_first,
        grad_w_second,
        grad_b_second,
        grad_tower_first,
        grad_tower_bias,
        grad_tower_out,
        grad_out_bias[0],
    )


def solution(mesh):
    placed = (
        P("dp", "field"),
        P("dp"),
        P("dp", None),
        P("dp"),
        P(None, "field", None),
        P(),
        P(None, "field", None),
        P(),
        P(),
        P(),
        P(),
        P(),
        P(),
        P(),
    )
    return jax.shard_map(
        functools.partial(per_device, mesh.shape["dp"]),
        mesh=mesh,
        in_specs=placed,
        out_specs=(
            P(),
            P("dp", "field"),
            P(None, "field", None),
            P(),
            P(None, "field", None),
            P(),
            P(),
            P(),
            P(),
            P(),
            P(),
            P(),
        ),
        check_vma=False,
    )
```

```python
import functools

import jax
import jax.numpy as jnp
from jax import lax
from jax.experimental import pallas as pl
from jax.experimental.pallas import tpu as pltpu
from jax.sharding import PartitionSpec as P

F32 = jnp.float32
BF16 = jnp.bfloat16
ROOT_HALF = 0.7071067811865476
DENSITY = 0.3989422804014327
VMEM = pltpu.VMEM
PARAMS = pltpu.CompilerParams(vmem_limit_bytes=58 * 1024 * 1024)
MEDIUM = pltpu.CompilerParams(vmem_limit_bytes=24 * 1024 * 1024)
SMALL = pltpu.CompilerParams(vmem_limit_bytes=12 * 1024 * 1024)
NN, TN, NT = (1, 0), (0, 0), (1, 1)


def split(x):
    high = x.astype(BF16)
    return high, (x - high.astype(F32)).astype(BF16)


def one_dot(a, b, dims):
    return lax.dot_general(a, b, (((dims[0],), (dims[1],)), ((), ())), preferred_element_type=F32)


def dot3(a, b, dims):
    return one_dot(a[0], b[0], dims) + (one_dot(a[0], b[1], dims) + one_dot(a[1], b[0], dims))


def gelu_parts(v):
    cdf = 0.5 + 0.5 * lax.erf(v * ROOT_HALF)
    return v * cdf, cdf + v * (DENSITY * jnp.exp(-0.5 * v * v))


def middle_kernel(
    place,
    out_bias,
    x0,
    x1,
    x2,
    x3,
    gate_rows,
    near0,
    near1,
    fa0,
    fa1,
    fa2,
    fa3,
    fb0,
    fb1,
    fb2,
    fb3,
    domain,
    labels,
    gate_bias,
    b_first,
    w_second,
    b_second,
    t_first,
    t_bias,
    t_out,
    xt_high_out,
    xt_low_out,
    gf_high_out,
    gf_low_out,
    gate_all,
    glog_out,
    s_keep,
    s_send,
    x_in,
    near_in,
    far_in,
    w2_in,
    xt_high,
    xt_low,
    gf_high,
    gf_low,
    hid_high,
    hid_low,
    slope,
    e_out,
    gates,
    soft_rows,
    bias_rows,
    mix,
    gmix,
    ggate,
    scores,
    targets,
    tower_rows,
    summed,
    rest,
    sems,
):
    experts = w_second.shape[0]
    tasks, width, tower = t_first.shape
    hidden = w_second.shape[1]
    rows = domain.shape[1]
    domains = gate_bias.shape[0]
    cols = near0.shape[1]
    start, count, me, field, corner = place[0], place[1], place[2], place[3], place[4]
    units = tasks * experts
    quarter = experts // 4
    order = [(r ^ corner) * quarter + i for r in range(4) for i in range(quarter)]

    loads = [
        pltpu.make_async_copy(near0, near_in.at[:, 0:cols], sems.at[0]),
        pltpu.make_async_copy(near1, near_in.at[:, cols : 2 * cols], sems.at[1]),
        pltpu.make_async_copy(w_second, w2_in, sems.at[2]),
    ]
    for r, (far_a, far_b) in enumerate(((fa0, fb0), (fa1, fb1), (fa2, fb2), (fa3, fb3))):
        target = far_in.at[r * quarter : (r + 1) * quarter]
        loads.append(pltpu.make_async_copy(far_a, target.at[:, 0:cols], sems.at[3 + 2 * r]))
        loads.append(pltpu.make_async_copy(far_b, target.at[:, cols : 2 * cols], sems.at[4 + 2 * r]))
    x_loads = [
        pltpu.make_async_copy(x0, x_in.at[0, 0:rows], sems.at[11]),
        pltpu.make_async_copy(x1, x_in.at[1], sems.at[12]),
        pltpu.make_async_copy(x2.at[0:rows], x_in.at[2, 0:rows], sems.at[13]),
        pltpu.make_async_copy(x2.at[2 * rows :], x_in.at[2, rows:], sems.at[14]),
        pltpu.make_async_copy(x3.at[rows:], x_in.at[3], sems.at[15]),
    ]
    for load in x_loads + loads:
        load.start()

    wide = tasks * experts
    for copy in x_loads:
        copy.wait()
    for k, ref in enumerate((x_in.at[0], x_in.at[1], x_in.at[2], x_in.at[3])):
        block = slice(k * cols, (k + 1) * cols)
        high, low = split(ref[0:rows, :].T)
        xt_high[block, :] = high
        xt_low[block, :] = low
        gate_all[:, block] = gate_rows[...] if k == 0 else ref[rows : rows + wide, :]
    hot = lax.broadcasted_iota(jnp.int32, (domains, rows), 0) == domain[pl.ds(field, 1), :]
    onehot = jnp.where(hot, 1.0, 0.0).astype(BF16)
    bias_high, bias_low = split(gate_bias[...])
    logits = dot3(split(gate_all[...]), (xt_high[...], xt_low[...]), NN)
    logits = logits + (one_dot(bias_high, onehot, TN) + one_dot(bias_low, onehot, TN))
    logits = logits.reshape(tasks, experts, rows)
    raised = jnp.exp(logits - jnp.max(logits, axis=1, keepdims=True))
    soft = raised / jnp.sum(raised, axis=1, keepdims=True)
    soft_rows[...] = soft.reshape(units, rows)
    for n, e in enumerate(order):
        for k in range(tasks):
            gates[k * experts + n : k * experts + n + 1, :] = soft_rows[pl.ds(k * experts + e, 1), :]
        bias_rows[n : n + 1, :] = b_first[pl.ds(e, 1), :]
        bias_rows[experts + n : experts + n + 1, :] = b_second[pl.ds(e, 1), :]
    targets[...] = jnp.zeros_like(targets)
    targets[0:tasks, :] = labels[:, pl.ds(pl.multiple_of(field * rows, 128), rows)].astype(F32)
    bias_cols = bias_rows[...].T
    rest[...] = jnp.zeros_like(rest)
    tower_rows[...] = jnp.zeros_like(tower_rows)
    tower_rows[0:tasks, :] = t_bias[...]
    tower_rows[tasks : 2 * tasks, :] = t_out[...]
    tower_cols = tower_rows[...].T
    for load in loads:
        load.wait()

    def first_layer(n):
        e = order[n]
        weight = split(jnp.concatenate([near_in[e], far_in[n]], axis=0))
        return dot3(weight, (xt_high[...], xt_low[...]), TN)

    pre = first_layer(0)
    value = None
    for n in range(experts + 1):
        following = first_layer(n + 1) if n + 1 < experts else None
        if n < experts:
            raw, steep = gelu_parts(pre + bias_cols[:, n : n + 1])
            slope[n] = steep
        if n > 0:
            at = experts + n - 1
            result = dot3(split(w2_in[order[n - 1]]), value, TN) + bias_cols[:, at : at + 1]
            e_out[n - 1] = result
            if n % 4 == 0:
                for k in range(tasks):
                    part = gates[k * experts + n - 1 : k * experts + n, :] * result
                    for m in range(n - 4, n - 1):
                        part = part + gates[k * experts + m : k * experts + m + 1, :] * e_out[m]
                    mix[k] = part if n == 4 else mix[k] + part
        if n < experts:
            value = split(raw)
            hid_high[n], hid_low[n] = value
        pre = following

    stores = [
        pltpu.make_async_copy(xt_high, xt_high_out, sems.at[0]),
        pltpu.make_async_copy(xt_low, xt_low_out, sems.at[1]),
    ]
    for store in stores:
        store.start()

    position = start + lax.broadcasted_iota(jnp.int32, (1, rows), 1)
    live = jnp.where(position < count, 1.0, 0.0)
    row_of = lax.broadcasted_iota(jnp.int32, (8, rows), 0)
    misc = rest.shape[0] - 8
    scores[...] = jnp.zeros_like(scores)
    acts, steeps, mixed, weights = [], [], [], []
    for k in range(tasks):
        mixed.append(split(mix[k]))
        weights.append(split(t_first[k]))
        value, steep = gelu_parts(dot3(weights[k], mixed[k], TN) + tower_cols[:, k : k + 1])
        out_column = tower_cols[:, tasks + k : tasks + k + 1]
        scores[k : k + 1, :] = jnp.sum(value * out_column, axis=0, keepdims=True) + out_bias[k]
        acts.append(value)
        steeps.append(out_column * steep)
    score = scores[...]
    target = targets[...]
    task_live = jnp.where(row_of < tasks, live, 0.0)
    per_item = jnp.maximum(score, 0.0) + jnp.log1p(jnp.exp(-jnp.abs(score))) - target * score
    gscores = task_live * (jax.nn.sigmoid(score) - target)
    sums = jnp.sum(gscores, axis=1, keepdims=True)
    losses = jnp.sum(per_item * task_live, axis=(0, 1), keepdims=True)
    t_sums = []
    for k in range(tasks):
        gpre = gscores[k : k + 1, :] * steeps[k]
        t_sums.append(jnp.sum(gpre, axis=1, keepdims=True))
        t_sums.append(jnp.sum(gscores[k : k + 1, :] * acts[k], axis=1, keepdims=True))
        gpre = split(gpre)
        gmix[k] = dot3(weights[k], gpre, NN)
        gweight = dot3(mixed[k], gpre, NT)
        if k < 2:
            rest[0:width, k * tower : (k + 1) * tower] = gweight
        else:
            rest[width : width + tower, 0:tower] = gweight[0:tower]
            rest[width : width + tower, tower:] = gweight[tower:]
        rest[misc + tasks : misc + tasks + 1, k : k + 1] = sums[k : k + 1, :]
    rest[misc + tasks : misc + tasks + 1, tasks : tasks + 1] = losses

    grads = []
    b1_sums, b2_sums = [], []
    for n, e in enumerate(order):
        result = e_out[n]
        total = None
        for k in range(tasks):
            down = gmix[k]
            at = k * experts + n
            ggate[at : at + 1, :] = jnp.sum(down * result, axis=0, keepdims=True)
            part = gates[at : at + 1, :] * down
            total = part if total is None else total + part
        b2_sums.append(jnp.sum(total, axis=1, keepdims=True))
        total = split(total)
        gweight = dot3((hid_high[n], hid_low[n]), total, NT)
        piece = hidden // 4
        for i in range(4):
            slot = (4 * e + i) ^ me
            summed[slot, 0:piece, :] = gweight[i * piece : (i + 1) * piece]
        gfirst = dot3(split(w2_in[e]), total, NN) * slope[n]
        b1_sums.append(jnp.sum(gfirst, axis=1, keepdims=True))
        high, low = split(gfirst)
        gf_high[e] = high
        gf_low[e] = low
        if n % 4 == 3:
            half = pl.ds(((corner >> 1) ^ (n // 4)) * 4, 4)
            grads.append(pltpu.make_async_copy(gf_high.at[half], gf_high_out.at[half], sems.at[4 + n // 2]))
            grads.append(pltpu.make_async_copy(gf_low.at[half], gf_low_out.at[half], sems.at[5 + n // 2]))
            grads[-2].start()
            grads[-1].start()

    piece = hidden // 4
    last = [
        pltpu.make_async_copy(summed.at[16:32, 0:piece], s_send.at[:, 0:piece], sems.at[8]),
        pltpu.make_async_copy(summed.at[0:16, 0:piece], s_keep.at[:, 0:piece], sems.at[9]),
        pltpu.make_async_copy(summed.at[16:32, piece:], s_send.at[:, piece:], sems.at[10]),
        pltpu.make_async_copy(summed.at[0:16, piece:], s_keep.at[:, piece:], sems.at[11]),
    ]
    last[0].start()
    last[1].start()

    lane = lax.broadcasted_iota(jnp.int32, (width, 128), 1)
    lane_t = lax.broadcasted_iota(jnp.int32, (tower, tower), 1)
    t_cols = jnp.zeros((tower, tower), F32)
    for n, column in enumerate(t_sums):
        t_cols = jnp.where(lane_t == n, column, t_cols)
    t_cols = t_cols.T
    for k in range(tasks):
        for at, n in ((k, 2 * k), (tasks + k, 2 * k + 1)):
            side = slice((at % 2) * tower, (at % 2 + 1) * tower)
            rest[misc + at // 2 : misc + at // 2 + 1, side] = t_cols[n : n + 1, :]
    sums = jnp.zeros((width, 128), F32)
    for n in range(experts):
        sums = jnp.where(lane == n, b1_sums[n], sums)
        sums = jnp.where(lane == experts + n, b2_sums[n], sums)
    sums = sums.T
    soft = gates[...].reshape(tasks, experts, rows)
    gsoft = ggate[...].reshape(tasks, experts, rows)
    glog = soft * (gsoft - jnp.sum(soft * gsoft, axis=1, keepdims=True))
    gates[...] = glog.reshape(units, rows)
    base = 2 * tower + tower + 2 * units
    for n, e in enumerate(order):
        for k in range(tasks):
            glog_out[pl.ds(k * experts + e, 1), :] = gates[k * experts + n : k * experts + n + 1, :]
        rest[pl.ds(base + e, 1), :] = sums[n : n + 1, :]
        rest[pl.ds(base + experts + e, 1), :] = sums[experts + n : experts + n + 1, :]
    glog_parts = split(glog_out[...])
    ggw = dot3(glog_parts, (xt_high[...], xt_low[...]), NT)
    base = width + tower
    for k in range(4):
        at = pl.multiple_of(base + ((field ^ k) >> 1) * units, 8)
        part = ggw[:, k * cols : (k + 1) * cols]
        low_side = ((field ^ k) & 1) == 0
        rest[pl.ds(at, units), 0:tower] = jnp.where(low_side, part, rest[pl.ds(at, units), 0:tower])
        rest[pl.ds(at, units), tower:] = jnp.where(low_side, rest[pl.ds(at, units), tower:], part)
    base = base + 2 * units + 2 * experts
    rest[base : base + domains, 0:units] = one_dot(onehot, glog_parts[0], NT) + one_dot(onehot, glog_parts[1], NT)
    alive = jnp.broadcast_to(jnp.sum(live, axis=1, keepdims=True), (1, width))
    tail = rest.shape[0] // 32
    for p in range(32):
        slot = p ^ me
        summed[slot, hidden // 4 :, :] = jnp.concatenate([rest[p * tail : (p + 1) * tail, :], alive], axis=0)
    last[2].start()
    last[3].start()
    for copy in stores + grads + last:
        copy.wait()


def first_kernel(
    place,
    xt_high_in,
    xt_low_in,
    gf_high_in,
    gf_low_in,
    keep_a,
    send_a,
    keep_b,
    send_b,
    xt_high,
    xt_low,
    gf_high,
    gf_low,
    keep,
    send,
    sems,
):
    experts, cols = keep.shape[1], keep.shape[2]
    half = experts // 2
    first_part, second_part = slice(0, half), slice(half, experts)
    loads = [
        pltpu.make_async_copy(xt_high_in, xt_high, sems.at[0]),
        pltpu.make_async_copy(xt_low_in, xt_low, sems.at[1]),
        pltpu.make_async_copy(gf_high_in.at[first_part], gf_high.at[first_part], sems.at[2]),
        pltpu.make_async_copy(gf_low_in.at[first_part], gf_low.at[first_part], sems.at[3]),
        pltpu.make_async_copy(gf_high_in.at[second_part], gf_high.at[second_part], sems.at[4]),
        pltpu.make_async_copy(gf_low_in.at[second_part], gf_low.at[second_part], sems.at[5]),
    ]
    for copy in loads:
        copy.start()
    for copy in loads[0:4]:
        copy.wait()
    stores = []
    for n in range(experts):
        if n == half:
            for copy in loads[4:6]:
                copy.wait()
        gweight = dot3((xt_high[...], xt_low[...]), (gf_high[n], gf_low[n]), NT)
        slot = n ^ place[0]
        for k in range(4):
            held = (keep, send)[k % 2]
            held[k // 2, slot] = gweight[k * cols : (k + 1) * cols]
        if n % half == half - 1:
            done = pl.ds(((place[0] >> 2) ^ (n // half)) * half, half)
            lower, upper = slice(0, cols // 2), slice(cols // 2, cols)
            pairs = ((send, send_a, lower), (send, send_b, upper), (keep, keep_a, lower), (keep, keep_b, upper))
            for held, out, part in pairs:
                at = sems.at[6 + len(stores)]
                stores.append(pltpu.make_async_copy(held.at[:, done, part], out.at[:, done], at))
                stores[-1].start()
    for copy in stores:
        copy.wait()


def inputs_kernel(
    place,
    gate_all,
    glog,
    gf_high_in,
    gf_low_in,
    near0,
    near1,
    fa0,
    fa1,
    fa2,
    fa3,
    fb0,
    fb1,
    fb2,
    fb3,
    g0,
    g1,
    g2,
    g3,
    gf_high,
    gf_low,
    near_in,
    far_in,
    total,
    sems,
):
    experts = gf_high.shape[0]
    rows, cols = g0.shape
    quarter = experts // 4
    corner = place[4]
    order = [(r ^ corner) * quarter + i for r in range(4) for i in range(quarter)]
    loads = [
        pltpu.make_async_copy(gf_high_in, gf_high, sems.at[0]),
        pltpu.make_async_copy(gf_low_in, gf_low, sems.at[1]),
        pltpu.make_async_copy(near0, near_in.at[:, 0:cols], sems.at[2]),
        pltpu.make_async_copy(near1, near_in.at[:, cols : 2 * cols], sems.at[3]),
    ]
    for r, (far_a, far_b) in enumerate(((fa0, fb0), (fa1, fb1), (fa2, fb2), (fa3, fb3))):
        target = far_in.at[r * quarter : (r + 1) * quarter]
        loads.append(pltpu.make_async_copy(far_a, target.at[:, 0:cols], sems.at[4 + 2 * r]))
        loads.append(pltpu.make_async_copy(far_b, target.at[:, cols : 2 * cols], sems.at[5 + 2 * r]))
    for copy in loads:
        copy.start()
    total[...] = dot3(split(gate_all[...]), split(glog[...]), TN)
    for copy in loads:
        copy.wait()
    for n, e in enumerate(order):
        weight = split(jnp.concatenate([near_in[e], far_in[n]], axis=0))
        total[...] += dot3(weight, (gf_high[e], gf_low[e]), NN)
    for k, ref in enumerate((g0, g1, g2, g3)):
        ref[...] = total[k * cols : (k + 1) * cols, :].T


def finish_second_kernel(
    place, a0, a1, a2, a3, b0, b1, b2, b3, gw2, gtf, ggw, ggb, gb1, gb2, gtb, gto, gtob, loss, parts, rest
):
    me, field = place[0], place[1]
    hidden = gw2.shape[1]
    piece = hidden // 4
    tasks, width, tower = gtf.shape
    experts = ggw.shape[1]
    units = tasks * experts
    domains = ggb.shape[0]
    tail = rest.shape[0] // 32
    half = (piece + tail + 1) // 2
    for s, (ref_a, ref_b) in enumerate(((a0, a1), (a2, a3), (b0, b1), (b2, b3))):
        for i in range(2):
            for z in range(4):
                p = ((s // 2) * 16 + ((s % 2) * 2 + i) * 4 + z) ^ me
                gw2[p // 4, pl.ds(pl.multiple_of((p % 4) * piece, 8), half), :] = ref_a[i, z]
                p = ((s // 2) * 16 + ((s % 2) + 2 * i) * 4 + z) ^ me
                at = pl.multiple_of((p % 4) * piece + half, 8)
                gw2[p // 4, pl.ds(at, piece - half), :] = ref_b[i, z, 0 : piece - half]
                parts[p] = ref_b[i, z, piece - half :]
    for p in range(32):
        rest[p * tail : (p + 1) * tail, :] = parts[p, 0:tail]
    gtf[0] = rest[0:width, 0:tower]
    gtf[1] = rest[0:width, tower:]
    gtf[2, 0:tower] = rest[width : width + tower, 0:tower]
    gtf[2, tower:] = rest[width : width + tower, tower:]
    base = width + tower
    mine = rest[pl.ds(pl.multiple_of(base + (field >> 1) * units, 8), units), :]
    mine = jnp.where((field & 1) == 0, mine[:, 0:tower], mine[:, tower:])
    for k in range(tasks):
        ggw[k] = mine[k * experts : (k + 1) * experts]
    base = base + 2 * units
    gb1[...] = rest[base : base + experts, :]
    gb2[...] = rest[base + experts : base + 2 * experts, :]
    base = base + 2 * experts
    ggb[...] = rest[base : base + domains, 0:units]
    misc = rest.shape[0] - 8
    for k in range(tasks):
        at = k
        gtb[k : k + 1] = rest[misc + at // 2 : misc + at // 2 + 1, (at % 2) * tower : (at % 2 + 1) * tower]
        at = tasks + k
        gto[k : k + 1] = rest[misc + at // 2 : misc + at // 2 + 1, (at % 2) * tower : (at % 2 + 1) * tower]
    gtob[...] = rest[misc + tasks : misc + tasks + 1, 0:tasks]
    loss[...] = rest[misc + tasks : misc + tasks + 1, tasks : tasks + 1]


def place_near_kernel(place, a0, a1, a2, a3, out, sems):
    copies = [
        pltpu.make_async_copy(ref, out.at[z ^ place[0]], sems.at[z]) for z, ref in enumerate((a0, a1, a2, a3))
    ]
    for copy in copies:
        copy.start()
    for copy in copies:
        copy.wait()


def place_far_kernel(place, b, begun, out, sems):
    copies = [pltpu.make_async_copy(b.at[z], out.at[(4 + z) ^ place[0]], sems.at[z]) for z in range(4)]
    for copy in copies:
        copy.start()
    for copy in copies:
        copy.wait()


def finish_inputs_kernel(place, factor, g0, g1, g2, g3, out):
    field = place[0]
    rows = g0.shape[0]
    for k, ref in enumerate((g0, g1, g2, g3)):
        out[pl.ds(pl.multiple_of((field ^ k) * rows, 8), rows), :] = ref[...] * factor[...]


def whole():
    return pl.BlockSpec(memory_space=VMEM)


def anywhere():
    return pl.BlockSpec(memory_space=pl.ANY)


def scalars():
    return pl.BlockSpec(memory_space=pltpu.SMEM)


def like(shape, dtype=F32):
    return jax.ShapeDtypeStruct(shape, dtype)


def after(value, *others):
    return lax.optimization_barrier((value, others))[0]


def per_device(
    n_dp,
    examples,
    domain,
    labels,
    row_counts,
    gate_weight,
    gate_bias,
    w_first,
    b_first,
    w_second,
    b_second,
    tower_first,
    tower_bias,
    tower_out,
    tower_out_bias,
):
    all_rows, cols = examples.shape
    rows = all_rows // 4
    experts, _, hidden = w_first.shape
    tasks = gate_weight.shape[0]
    width = w_second.shape[2]
    tower = tower_first.shape[2]
    domains = gate_bias.shape[0]
    units = tasks * experts
    field = lax.axis_index("field").astype(jnp.int32)
    group = lax.axis_index("dp").astype(jnp.int32)

    def move(value, dp_mask, field_mask):
        pairs = []
        for d in range(n_dp):
            for f in range(4):
                pairs.append((d * 4 + f, (d ^ dp_mask) * 4 + (f ^ field_mask)))
        return lax.ppermute(value, ("dp", "field"), pairs)

    def over_rest(value):
        mask = 8
        while mask < n_dp:
            value = value + move(value, mask, 0)
            mask *= 2
        return value

    core, chip_y = field & 1, field >> 1
    chip_x, chip_z = group & 1, (group >> 1) & 3
    me5 = core * 16 + chip_x * 8 + chip_y * 4 + chip_z
    me3 = chip_x * 4 + chip_z
    corner = group & 3

    count = row_counts[0]

    gate_rows = jnp.transpose(gate_weight, (0, 2, 1)).reshape(units, cols)
    quarter = experts // 4

    def rows_for(k):
        return lax.dynamic_slice(examples, ((field ^ k) * rows, 0), (rows, cols))

    far = move(lax.dynamic_slice(w_first, (corner * quarter, 0, 0), (quarter, cols, hidden)), 0, 2)
    near = move(w_first, 0, 1)
    place = jnp.stack([field * rows, count, me5, field, corner]).astype(jnp.int32)
    domain = domain.reshape(4, rows)
    x0 = rows_for(0)
    near_rows = jnp.concatenate([rows_for(1), gate_rows], axis=0)
    y_rows = jnp.concatenate([rows_for(2), rows_for(3), gate_rows], axis=0)
    early = (far, near, near_rows, y_rows, x0, place, domain)
    far, near, near_rows, y_rows, x0, place, domain = lax.optimization_barrier(early)

    x2 = move(y_rows, 0, 2)
    x1 = move(near_rows, 0, 1)
    far_a = [far] + [move(far, r, 0) for r in (1, 2, 3)]
    x1, x2, far_a = lax.optimization_barrier((x1, x2, far_a))

    x3 = move(x2, 0, 1)
    far_b = [move(piece, 0, 1) for piece in far_a]

    outs = pl.pallas_call(
        middle_kernel,
        name="middle",
        out_shape=(
            like((4 * cols, rows), BF16),
            like((4 * cols, rows), BF16),
            like((experts, hidden, rows), BF16),
            like((experts, hidden, rows), BF16),
            like((units, 4 * cols)),
            like((units, rows)),
            like((16, 80, width)),
            like((16, 80, width)),
        ),
        in_specs=[scalars()] * 2
        + [anywhere()] * 4
        + [whole()]
        + [anywhere()] * 10
        + [whole()] * 4
        + [anywhere()]
        + [whole()] * 4,
        out_specs=[anywhere()] * 4 + [whole()] * 2 + [anywhere()] * 2,
        scratch_shapes=[
            VMEM((4, rows + units, cols), F32),
            VMEM((experts, 2 * cols, hidden), F32),
            VMEM((experts, 2 * cols, hidden), F32),
            VMEM((experts, hidden, width), F32),
            VMEM((4 * cols, rows), BF16),
            VMEM((4 * cols, rows), BF16),
            VMEM((experts, hidden, rows), BF16),
            VMEM((experts, hidden, rows), BF16),
            VMEM((experts, hidden, rows), BF16),
            VMEM((experts, hidden, rows), BF16),
            VMEM((experts, hidden, rows), F32),
            VMEM((experts, width, rows), F32),
            VMEM((units, rows), F32),
            VMEM((units, rows), F32),
            VMEM((2 * experts, hidden), F32),
            VMEM((tasks, width, rows), F32),
            VMEM((tasks, width, rows), F32),
            VMEM((units, rows), F32),
            VMEM((8, rows), F32),
            VMEM((8, rows), F32),
            VMEM((8, tower), F32),
            VMEM((32, 80, width), F32),
            VMEM((480, width), F32),
            pltpu.SemaphoreType.DMA((16,)),
        ],
        compiler_params=PARAMS,
    )(
        place,
        tower_out_bias,
        x0,
        x1,
        x2,
        x3,
        gate_rows,
        w_first,
        near,
        *far_a,
        *far_b,
        domain,
        labels.T,
        gate_bias,
        b_first,
        w_second,
        b_second,
        tower_first,
        tower_bias,
        tower_out,
    )
    xt_high, xt_low, gf_high, gf_low, gate_all, glog, s_keep, s_send = outs

    place3 = me3.reshape(1)
    cheap = pl.CostEstimate(flops=0, bytes_accessed=1 << 20, transcendentals=0)

    def fold(keep, got, axis):
        held = keep + got
        return lax.index_in_dim(held, 0, axis, False), lax.index_in_dim(held, 1, axis, False)

    s_keep = s_keep.reshape(2, 2, 4, 80, width)
    s_got = move(s_send, 0, 1).reshape(2, 2, 4, 80, width)
    sa, sa_out = fold(s_keep[:, :, :, 0:40], s_got[:, :, :, 0:40], 0)
    sb, sb_out = fold(s_keep[:, :, :, 40:80], s_got[:, :, :, 40:80], 1)
    sa, sa_out, sb, sb_out, gf_high = lax.optimization_barrier((sa, sa_out, sb, sb_out, gf_high))

    sa_got, sb_got = move(sa_out, 1, 0), move(sb_out, 0, 2)
    wa_keep, wa_send, wb_keep, wb_send = pl.pallas_call(
        first_kernel,
        name="first",
        out_shape=tuple(like((2, 8, cols // 2, hidden)) for _ in range(4)),
        in_specs=[scalars()] + [anywhere()] * 4,
        out_specs=[anywhere()] * 4,
        scratch_shapes=[
            VMEM((4 * cols, rows), BF16),
            VMEM((4 * cols, rows), BF16),
            VMEM((experts, hidden, rows), BF16),
            VMEM((experts, hidden, rows), BF16),
            VMEM((2, experts, cols, hidden), F32),
            VMEM((2, experts, cols, hidden), F32),
            pltpu.SemaphoreType.DMA((14,)),
        ],
        compiler_params=PARAMS,
        cost_estimate=cheap,
    )(place3, xt_high, xt_low, gf_high, gf_low)
    wa_got, wb_got = move(wa_send, 0, 1), move(wb_send, 0, 1)
    sa, sa_out = fold(sa, sa_got, 0)
    sb, sb_out = fold(sb, sb_got, 0)
    sa_got, sb_got = move(sa_out, 0, 2), move(sb_out, 1, 0)
    s_mine = jnp.concatenate([sa + sa_got, sb + sb_got], axis=1)
    slots = (2, 2, 4, cols // 2, hidden)
    wa, wa_out = fold(wa_keep.reshape(slots), wa_got.reshape(slots), 0)
    wb, wb_out = fold(wb_keep.reshape(slots), wb_got.reshape(slots), 1)
    stage = (wa, wa_out, wb, wb_out, s_mine, gf_low)
    wa, wa_out, wb, wb_out, s_mine, gf_low = lax.optimization_barrier(stage)

    wa_got, wb_got = move(wa_out, 0, 2), move(wb_out, 1, 0)
    s_got = [move(s_mine[z], 2 * z, 0) for z in (1, 2, 3)]
    wa, wa_out = fold(wa, wa_got, 0)
    wb, wb_out = fold(wb, wb_got, 0)
    wa_got, wb_got = move(wa_out, 1, 0), move(wb_out, 0, 2)
    s_piece = over_rest(s_mine[0] + s_got[0] + s_got[1] + s_got[2])
    factor = 1.0 / s_piece[79:80, 0:1]
    s_piece = s_piece * factor
    s_line = jnp.stack([s_piece] + [move(s_piece, 2 * z, 0) for z in (1, 2, 3)])
    w_mine = jnp.concatenate([wa + wa_got, wb + wb_got], axis=1)
    w_mine, s_line, gf_low = lax.optimization_barrier((w_mine, s_line, gf_low))

    g0, g1, g2, g3 = pl.pallas_call(
        inputs_kernel,
        name="inputs",
        out_shape=tuple(like((rows, cols)) for _ in range(4)),
        in_specs=[scalars()] + [whole()] * 2 + [anywhere()] * 12,
        out_specs=[whole()] * 4,
        scratch_shapes=[
            VMEM((experts, hidden, rows), BF16),
            VMEM((experts, hidden, rows), BF16),
            VMEM((experts, 2 * cols, hidden), F32),
            VMEM((experts, 2 * cols, hidden), F32),
            VMEM((4 * cols, rows), F32),
            pltpu.SemaphoreType.DMA((12,)),
        ],
        compiler_params=MEDIUM,
        cost_estimate=cheap,
    )(place, gate_all, glog, gf_high, gf_low, w_first, near, *far_a, *far_b)
    w_got = [move(w_mine[z], 2 * z, 0) for z in (1, 2, 3)]
    sa, sb = s_line[:, 0:40], s_line[:, 40:80]
    sa = jnp.stack([sa, move(sa, 0, 2)])
    sb = jnp.stack([sb, move(sb, 1, 0)])
    w_piece = over_rest(w_mine[0] + w_got[0] + w_got[1] + w_got[2]) * factor
    w_piece, sa, sb, g0, g1, g2, g3 = lax.optimization_barrier((w_piece, sa, sb, g0, g1, g2, g3))

    g1 = move(g1, 0, 1)
    w_line = [w_piece] + [move(w_piece, 2 * z, 0) for z in (1, 2, 3)]
    s_near = [sa, sb, move(sa, 1, 0), move(sb, 0, 2)]
    tick = move(w_line[1][0:8] + w_line[2][0:8] + w_line[3][0:8], 0, 1)
    s_near, g2, g3, tick = lax.optimization_barrier((s_near, g2, g3, tick))

    w_other = move(jnp.stack(w_line), 1, 0)
    g2 = move(g2, 0, 2)
    g3 = move(g3, 0, 3)
    s_far = [move(part, 0, 1) for part in s_near]

    seconds = pl.pallas_call(
        finish_second_kernel,
        name="finish_second",
        out_shape=(
            like((experts, hidden, width)),
            like((tasks, width, tower)),
            like((tasks, experts, cols)),
            like((domains, units)),
            like((experts, hidden)),
            like((experts, width)),
            like((tasks, tower)),
            like((tasks, tower)),
            like((1, tasks)),
            like((1, 1)),
        ),
        in_specs=[scalars()] + [whole()] * 8,
        out_specs=[whole()] * 10,
        scratch_shapes=[VMEM((32, 16, width), F32), VMEM((480, width), F32)],
        compiler_params=SMALL,
    )(jnp.stack([me5, field]), *s_near, *s_far)
    grad_w_second, grad_tower_first, grad_gate_weight, grad_gate_bias = seconds[:4]
    grad_b_first, grad_b_second, grad_tower_bias, grad_tower_out, grad_out_bias, loss = seconds[4:]

    grad_examples = pl.pallas_call(
        finish_inputs_kernel,
        name="finish_inputs",
        out_shape=like((all_rows, cols)),
        in_specs=[scalars()] + [whole()] * 5,
        out_specs=whole(),
        compiler_params=SMALL,
    )(field.reshape(1), factor, g0, g1, g2, g3)

    begun = pl.pallas_call(
        place_near_kernel,
        name="place_near",
        out_shape=like((experts, cols, hidden)),
        in_specs=[scalars()] + [anywhere()] * 4,
        out_specs=anywhere(),
        scratch_shapes=[pltpu.SemaphoreType.DMA((4,))],
        compiler_params=SMALL,
    )(place3, *w_line)
    grad_w_first = pl.pallas_call(
        place_far_kernel,
        name="place_far",
        out_shape=like((experts, cols, hidden)),
        in_specs=[scalars(), anywhere(), anywhere()],
        out_specs=anywhere(),
        scratch_shapes=[pltpu.SemaphoreType.DMA((4,))],
        input_output_aliases={2: 0},
        compiler_params=SMALL,
    )(place3, w_other, after(begun, grad_examples, grad_w_second))

    return (
        loss[0, 0],
        grad_examples,
        jnp.transpose(grad_gate_weight, (0, 2, 1)),
        grad_gate_bias,
        grad_w_first,
        grad_b_first,
        grad_w_second,
        grad_b_second,
        grad_tower_first,
        grad_tower_bias,
        grad_tower_out,
        grad_out_bias[0],
    )


def solution(mesh):
    placed = (
        P("dp", "field"),
        P("dp"),
        P("dp", None),
        P("dp"),
        P(None, "field", None),
        P(),
        P(None, "field", None),
        P(),
        P(),
        P(),
        P(),
        P(),
        P(),
        P(),
    )
    return jax.shard_map(
        functools.partial(per_device, mesh.shape["dp"]),
        mesh=mesh,
        in_specs=placed,
        out_specs=(
            P(),
            P("dp", "field"),
            P(None, "field", None),
            P(),
            P(None, "field", None),
            P(),
            P(),
            P(),
            P(),
            P(),
            P(),
            P(),
        ),
        check_vma=False,
    )
```

```python
import functools

import jax
import jax.numpy as jnp
from jax import lax
from jax.experimental import pallas as pl
from jax.experimental.pallas import tpu as pltpu
from jax.sharding import PartitionSpec as P

F32 = jnp.float32
BF16 = jnp.bfloat16
ROOT_HALF = 0.7071067811865476
DENSITY = 0.3989422804014327
VMEM = pltpu.VMEM
PARAMS = pltpu.CompilerParams(vmem_limit_bytes=58 * 1024 * 1024)
MEDIUM = pltpu.CompilerParams(vmem_limit_bytes=24 * 1024 * 1024)
SMALL = pltpu.CompilerParams(vmem_limit_bytes=12 * 1024 * 1024)
NN, TN, NT = (1, 0), (0, 0), (1, 1)


def split(x):
    high = x.astype(BF16)
    return high, (x - high.astype(F32)).astype(BF16)


def one_dot(a, b, dims):
    return lax.dot_general(a, b, (((dims[0],), (dims[1],)), ((), ())), preferred_element_type=F32)


def dot3(a, b, dims):
    return one_dot(a[0], b[0], dims) + (one_dot(a[0], b[1], dims) + one_dot(a[1], b[0], dims))


def gelu_parts(v):
    cdf = 0.5 + 0.5 * lax.erf(v * ROOT_HALF)
    return v * cdf, cdf + v * (DENSITY * jnp.exp(-0.5 * v * v))


def middle_kernel(
    place,
    out_bias,
    x0,
    x1,
    x2,
    x3,
    gate_rows,
    near0,
    near1,
    fa0,
    fa1,
    fa2,
    fa3,
    fb0,
    fb1,
    fb2,
    fb3,
    domain,
    labels,
    gate_bias,
    b_first,
    w_second,
    b_second,
    t_first,
    t_bias,
    t_out,
    xt_high_out,
    xt_low_out,
    gf_high_out,
    gf_low_out,
    gate_all,
    glog_out,
    sa_keep,
    sa_send,
    sb_keep,
    sb_send,
    begun,
    x_in,
    near_in,
    far_in,
    w2_in,
    xt_high,
    xt_low,
    gf_high,
    gf_low,
    hid_high,
    hid_low,
    slope,
    e_out,
    gates,
    soft_rows,
    bias_rows,
    mix,
    gmix,
    ggate,
    scores,
    targets,
    tower_rows,
    summed,
    rest,
    sems,
):
    experts = w_second.shape[0]
    tasks, width, tower = t_first.shape
    hidden = w_second.shape[1]
    rows = domain.shape[1]
    domains = gate_bias.shape[0]
    cols = near0.shape[1]
    start, count, me, field, corner = place[0], place[1], place[2], place[3], place[4]
    units = tasks * experts
    quarter = experts // 4
    order = [(r ^ corner) * quarter + i for r in range(4) for i in range(quarter)]

    loads = [
        pltpu.make_async_copy(near0, near_in.at[:, 0:cols], sems.at[0]),
        pltpu.make_async_copy(near1, near_in.at[:, cols : 2 * cols], sems.at[1]),
        pltpu.make_async_copy(w_second, w2_in, sems.at[2]),
    ]
    for r, (far_a, far_b) in enumerate(((fa0, fb0), (fa1, fb1), (fa2, fb2), (fa3, fb3))):
        target = far_in.at[r * quarter : (r + 1) * quarter]
        loads.append(pltpu.make_async_copy(far_a, target.at[:, 0:cols], sems.at[3 + 2 * r]))
        loads.append(pltpu.make_async_copy(far_b, target.at[:, cols : 2 * cols], sems.at[4 + 2 * r]))
    x_loads = [
        pltpu.make_async_copy(x0, x_in.at[0, 0:rows], sems.at[11]),
        pltpu.make_async_copy(x1, x_in.at[1], sems.at[12]),
        pltpu.make_async_copy(x2.at[0:rows], x_in.at[2, 0:rows], sems.at[13]),
        pltpu.make_async_copy(x2.at[2 * rows :], x_in.at[2, rows:], sems.at[14]),
        pltpu.make_async_copy(x3.at[rows:], x_in.at[3], sems.at[15]),
    ]
    for load in x_loads + loads:
        load.start()

    wide = tasks * experts
    for copy in x_loads:
        copy.wait()
    for k, ref in enumerate((x_in.at[0], x_in.at[1], x_in.at[2], x_in.at[3])):
        block = slice(k * cols, (k + 1) * cols)
        high, low = split(ref[0:rows, :].T)
        xt_high[block, :] = high
        xt_low[block, :] = low
        gate_all[:, block] = gate_rows[...] if k == 0 else ref[rows : rows + wide, :]
    hot = lax.broadcasted_iota(jnp.int32, (domains, rows), 0) == domain[pl.ds(field, 1), :]
    onehot = jnp.where(hot, 1.0, 0.0).astype(BF16)
    bias_high, bias_low = split(gate_bias[...])
    logits = dot3(split(gate_all[...]), (xt_high[...], xt_low[...]), NN)
    logits = logits + (one_dot(bias_high, onehot, TN) + one_dot(bias_low, onehot, TN))
    logits = logits.reshape(tasks, experts, rows)
    raised = jnp.exp(logits - jnp.max(logits, axis=1, keepdims=True))
    soft = raised / jnp.sum(raised, axis=1, keepdims=True)
    soft_rows[...] = soft.reshape(units, rows)
    for n, e in enumerate(order):
        for k in range(tasks):
            gates[k * experts + n : k * experts + n + 1, :] = soft_rows[pl.ds(k * experts + e, 1), :]
        bias_rows[n : n + 1, :] = b_first[pl.ds(e, 1), :]
        bias_rows[experts + n : experts + n + 1, :] = b_second[pl.ds(e, 1), :]
    targets[...] = jnp.zeros_like(targets)
    targets[0:tasks, :] = labels[:, pl.ds(pl.multiple_of(field * rows, 128), rows)].astype(F32)
    bias_cols = bias_rows[...].T
    rest[...] = jnp.zeros_like(rest)
    tower_rows[...] = jnp.zeros_like(tower_rows)
    tower_rows[0:tasks, :] = t_bias[...]
    tower_rows[tasks : 2 * tasks, :] = t_out[...]
    tower_cols = tower_rows[...].T
    for load in loads[0:2]:
        load.wait()
    ahead = 4
    for n in range(ahead):
        begun[n] = dot3(split(near_in[order[n]]), (xt_high[0 : 2 * cols], xt_low[0 : 2 * cols]), TN)
    for load in loads[2:]:
        load.wait()

    def first_layer(n):
        e = order[n]
        if n < ahead:
            weight = split(far_in[n])
            return begun[n] + dot3(weight, (xt_high[2 * cols :], xt_low[2 * cols :]), TN)
        weight = split(jnp.concatenate([near_in[e], far_in[n]], axis=0))
        return dot3(weight, (xt_high[...], xt_low[...]), TN)

    pre = first_layer(0)
    value = None
    for n in range(experts + 1):
        following = first_layer(n + 1) if n + 1 < experts else None
        if n < experts:
            raw, steep = gelu_parts(pre + bias_cols[:, n : n + 1])
            slope[n] = steep
        if n > 0:
            at = experts + n - 1
            result = dot3(split(w2_in[order[n - 1]]), value, TN) + bias_cols[:, at : at + 1]
            e_out[n - 1] = result
            if n % 4 == 0:
                for k in range(tasks):
                    part = gates[k * experts + n - 1 : k * experts + n, :] * result
                    for m in range(n - 4, n - 1):
                        part = part + gates[k * experts + m : k * experts + m + 1, :] * e_out[m]
                    mix[k] = part if n == 4 else mix[k] + part
        if n < experts:
            value = split(raw)
            hid_high[n], hid_low[n] = value
        pre = following

    stores = [
        pltpu.make_async_copy(xt_high, xt_high_out, sems.at[0]),
        pltpu.make_async_copy(xt_low, xt_low_out, sems.at[1]),
    ]
    for store in stores:
        store.start()

    position = start + lax.broadcasted_iota(jnp.int32, (1, rows), 1)
    live = jnp.where(position < count, 1.0, 0.0)
    row_of = lax.broadcasted_iota(jnp.int32, (8, rows), 0)
    misc = rest.shape[0] - 8
    scores[...] = jnp.zeros_like(scores)
    acts, steeps, mixed, weights = [], [], [], []
    for k in range(tasks):
        mixed.append(split(mix[k]))
        weights.append(split(t_first[k]))
        value, steep = gelu_parts(dot3(weights[k], mixed[k], TN) + tower_cols[:, k : k + 1])
        out_column = tower_cols[:, tasks + k : tasks + k + 1]
        scores[k : k + 1, :] = jnp.sum(value * out_column, axis=0, keepdims=True) + out_bias[k]
        acts.append(value)
        steeps.append(out_column * steep)
    score = scores[...]
    target = targets[...]
    task_live = jnp.where(row_of < tasks, live, 0.0)
    per_item = jnp.maximum(score, 0.0) + jnp.log1p(jnp.exp(-jnp.abs(score))) - target * score
    gscores = task_live * (jax.nn.sigmoid(score) - target)
    sums = jnp.sum(gscores, axis=1, keepdims=True)
    losses = jnp.sum(per_item * task_live, axis=(0, 1), keepdims=True)
    t_sums = []
    for k in range(tasks):
        gpre = gscores[k : k + 1, :] * steeps[k]
        t_sums.append(jnp.sum(gpre, axis=1, keepdims=True))
        t_sums.append(jnp.sum(gscores[k : k + 1, :] * acts[k], axis=1, keepdims=True))
        gpre = split(gpre)
        gmix[k] = dot3(weights[k], gpre, NN)
        gweight = dot3(mixed[k], gpre, NT)
        if k < 2:
            rest[0:width, k * tower : (k + 1) * tower] = gweight
        else:
            rest[width : width + tower, 0:tower] = gweight[0:tower]
            rest[width : width + tower, tower:] = gweight[tower:]
        rest[misc + tasks : misc + tasks + 1, k : k + 1] = sums[k : k + 1, :]
    rest[misc + tasks : misc + tasks + 1, tasks : tasks + 1] = losses

    grads = []
    b1_sums, b2_sums = [], []
    for n, e in enumerate(order):
        result = e_out[n]
        total = None
        for k in range(tasks):
            down = gmix[k]
            at = k * experts + n
            ggate[at : at + 1, :] = jnp.sum(down * result, axis=0, keepdims=True)
            part = gates[at : at + 1, :] * down
            total = part if total is None else total + part
        b2_sums.append(jnp.sum(total, axis=1, keepdims=True))
        total = split(total)
        gweight = dot3((hid_high[n], hid_low[n]), total, NT)
        piece = hidden // 4
        for i in range(4):
            slot = (4 * e + i) ^ me
            summed[slot, 0:piece, :] = gweight[i * piece : (i + 1) * piece]
        gfirst = dot3(split(w2_in[e]), total, NN) * slope[n]
        b1_sums.append(jnp.sum(gfirst, axis=1, keepdims=True))
        high, low = split(gfirst)
        gf_high[e] = high
        gf_low[e] = low
        if n % 4 == 3:
            half = pl.ds(((corner >> 1) ^ (n // 4)) * 4, 4)
            grads.append(pltpu.make_async_copy(gf_high.at[half], gf_high_out.at[half], sems.at[4 + n // 2]))
            grads.append(pltpu.make_async_copy(gf_low.at[half], gf_low_out.at[half], sems.at[5 + n // 2]))
            grads[-2].start()
            grads[-1].start()

    piece = hidden // 4
    half = summed.shape[1] // 2
    last = [
        pltpu.make_async_copy(summed.at[16:32, 0:half], sa_send, sems.at[8]),
        pltpu.make_async_copy(summed.at[0:16, 0:half], sa_keep, sems.at[9]),
        pltpu.make_async_copy(summed.at[16:32, half:], sb_send, sems.at[10]),
        pltpu.make_async_copy(summed.at[0:16, half:], sb_keep, sems.at[11]),
    ]
    last[0].start()
    last[1].start()

    lane = lax.broadcasted_iota(jnp.int32, (width, 128), 1)
    lane_t = lax.broadcasted_iota(jnp.int32, (tower, tower), 1)
    t_cols = jnp.zeros((tower, tower), F32)
    for n, column in enumerate(t_sums):
        t_cols = jnp.where(lane_t == n, column, t_cols)
    t_cols = t_cols.T
    for k in range(tasks):
        for at, n in ((k, 2 * k), (tasks + k, 2 * k + 1)):
            side = slice((at % 2) * tower, (at % 2 + 1) * tower)
            rest[misc + at // 2 : misc + at // 2 + 1, side] = t_cols[n : n + 1, :]
    sums = jnp.zeros((width, 128), F32)
    for n in range(experts):
        sums = jnp.where(lane == n, b1_sums[n], sums)
        sums = jnp.where(lane == experts + n, b2_sums[n], sums)
    sums = sums.T
    soft = gates[...].reshape(tasks, experts, rows)
    gsoft = ggate[...].reshape(tasks, experts, rows)
    glog = soft * (gsoft - jnp.sum(soft * gsoft, axis=1, keepdims=True))
    gates[...] = glog.reshape(units, rows)
    base = 2 * tower + tower + 2 * units
    for n, e in enumerate(order):
        for k in range(tasks):
            glog_out[pl.ds(k * experts + e, 1), :] = gates[k * experts + n : k * experts + n + 1, :]
        rest[pl.ds(base + e, 1), :] = sums[n : n + 1, :]
        rest[pl.ds(base + experts + e, 1), :] = sums[experts + n : experts + n + 1, :]
    glog_parts = split(glog_out[...])
    ggw = dot3(glog_parts, (xt_high[...], xt_low[...]), NT)
    base = width + tower
    for k in range(4):
        at = pl.multiple_of(base + ((field ^ k) >> 1) * units, 8)
        part = ggw[:, k * cols : (k + 1) * cols]
        low_side = ((field ^ k) & 1) == 0
        rest[pl.ds(at, units), 0:tower] = jnp.where(low_side, part, rest[pl.ds(at, units), 0:tower])
        rest[pl.ds(at, units), tower:] = jnp.where(low_side, rest[pl.ds(at, units), tower:], part)
    base = base + 2 * units + 2 * experts
    rest[base : base + domains, 0:units] = one_dot(onehot, glog_parts[0], NT) + one_dot(onehot, glog_parts[1], NT)
    alive = jnp.broadcast_to(jnp.sum(live, axis=1, keepdims=True), (1, width))
    tail = rest.shape[0] // 32
    for p in range(32):
        slot = p ^ me
        summed[slot, hidden // 4 :, :] = jnp.concatenate([rest[p * tail : (p + 1) * tail, :], alive], axis=0)
    last[2].start()
    last[3].start()
    for copy in stores + grads + last:
        copy.wait()


def first_kernel(
    place,
    xt_high_in,
    xt_low_in,
    gf_high_in,
    gf_low_in,
    keep_a,
    send_a,
    keep_b,
    send_b,
    xt_high,
    xt_low,
    gf_high,
    gf_low,
    keep,
    send,
    sems,
):
    experts, cols = keep.shape[1], keep.shape[2]
    half = experts // 2
    first_part, second_part = slice(0, half), slice(half, experts)
    loads = [
        pltpu.make_async_copy(xt_high_in, xt_high, sems.at[0]),
        pltpu.make_async_copy(xt_low_in, xt_low, sems.at[1]),
        pltpu.make_async_copy(gf_high_in.at[first_part], gf_high.at[first_part], sems.at[2]),
        pltpu.make_async_copy(gf_low_in.at[first_part], gf_low.at[first_part], sems.at[3]),
        pltpu.make_async_copy(gf_high_in.at[second_part], gf_high.at[second_part], sems.at[4]),
        pltpu.make_async_copy(gf_low_in.at[second_part], gf_low.at[second_part], sems.at[5]),
    ]
    for copy in loads:
        copy.start()
    for copy in loads[0:4]:
        copy.wait()
    stores = []
    for n in range(experts):
        if n == half:
            for copy in loads[4:6]:
                copy.wait()
        gweight = dot3((xt_high[...], xt_low[...]), (gf_high[n], gf_low[n]), NT)
        slot = n ^ place[0]
        for k in range(4):
            held = (keep, send)[k % 2]
            held[k // 2, slot] = gweight[k * cols : (k + 1) * cols]
        if n % half == half - 1:
            done = pl.ds(((place[0] >> 2) ^ (n // half)) * half, half)
            lower, upper = slice(0, cols // 2), slice(cols // 2, cols)
            pairs = ((send, send_a, lower), (send, send_b, upper), (keep, keep_a, lower), (keep, keep_b, upper))
            for held, out, part in pairs:
                at = sems.at[6 + len(stores)]
                stores.append(pltpu.make_async_copy(held.at[:, done, part], out.at[:, done], at))
                stores[-1].start()
    for copy in stores:
        copy.wait()


def inputs_kernel(
    place,
    gate_all,
    glog,
    gf_high_in,
    gf_low_in,
    near0,
    near1,
    fa0,
    fa1,
    fa2,
    fa3,
    fb0,
    fb1,
    fb2,
    fb3,
    g0,
    g1,
    g2,
    g3,
    gf_high,
    gf_low,
    near_in,
    far_in,
    total,
    sems,
):
    experts = gf_high.shape[0]
    rows, cols = g0.shape
    quarter = experts // 4
    corner = place[4]
    order = [(r ^ corner) * quarter + i for r in range(4) for i in range(quarter)]
    loads = [
        pltpu.make_async_copy(gf_high_in, gf_high, sems.at[0]),
        pltpu.make_async_copy(gf_low_in, gf_low, sems.at[1]),
        pltpu.make_async_copy(near0, near_in.at[:, 0:cols], sems.at[2]),
        pltpu.make_async_copy(near1, near_in.at[:, cols : 2 * cols], sems.at[3]),
    ]
    for r, (far_a, far_b) in enumerate(((fa0, fb0), (fa1, fb1), (fa2, fb2), (fa3, fb3))):
        target = far_in.at[r * quarter : (r + 1) * quarter]
        loads.append(pltpu.make_async_copy(far_a, target.at[:, 0:cols], sems.at[4 + 2 * r]))
        loads.append(pltpu.make_async_copy(far_b, target.at[:, cols : 2 * cols], sems.at[5 + 2 * r]))
    for copy in loads:
        copy.start()
    total[...] = dot3(split(gate_all[...]), split(glog[...]), TN)
    for copy in loads:
        copy.wait()
    for n, e in enumerate(order):
        weight = split(jnp.concatenate([near_in[e], far_in[n]], axis=0))
        total[...] += dot3(weight, (gf_high[e], gf_low[e]), NN)
    for k, ref in enumerate((g0, g1, g2, g3)):
        ref[...] = total[k * cols : (k + 1) * cols, :].T


def finish_second_kernel(
    place, a0, a1, a2, a3, b0, b1, b2, b3, gw2, gtf, ggw, ggb, gb1, gb2, gtb, gto, gtob, loss, parts, rest
):
    me, field = place[0], place[1]
    hidden = gw2.shape[1]
    piece = hidden // 4
    tasks, width, tower = gtf.shape
    experts = ggw.shape[1]
    units = tasks * experts
    domains = ggb.shape[0]
    tail = rest.shape[0] // 32
    half = (piece + tail + 1) // 2
    for s, (ref_a, ref_b) in enumerate(((a0, a1), (a2, a3), (b0, b1), (b2, b3))):
        for i in range(2):
            for z in range(4):
                p = ((s // 2) * 16 + ((s % 2) * 2 + i) * 4 + z) ^ me
                gw2[p // 4, pl.ds(pl.multiple_of((p % 4) * piece, 8), half), :] = ref_a[i, z]
                p = ((s // 2) * 16 + ((s % 2) + 2 * i) * 4 + z) ^ me
                at = pl.multiple_of((p % 4) * piece + half, 8)
                gw2[p // 4, pl.ds(at, piece - half), :] = ref_b[i, z, 0 : piece - half]
                parts[p] = ref_b[i, z, piece - half :]
    for p in range(32):
        rest[p * tail : (p + 1) * tail, :] = parts[p, 0:tail]
    gtf[0] = rest[0:width, 0:tower]
    gtf[1] = rest[0:width, tower:]
    gtf[2, 0:tower] = rest[width : width + tower, 0:tower]
    gtf[2, tower:] = rest[width : width + tower, tower:]
    base = width + tower
    mine = rest[pl.ds(pl.multiple_of(base + (field >> 1) * units, 8), units), :]
    mine = jnp.where((field & 1) == 0, mine[:, 0:tower], mine[:, tower:])
    for k in range(tasks):
        ggw[k] = mine[k * experts : (k + 1) * experts]
    base = base + 2 * units
    gb1[...] = rest[base : base + experts, :]
    gb2[...] = rest[base + experts : base + 2 * experts, :]
    base = base + 2 * experts
    ggb[...] = rest[base : base + domains, 0:units]
    misc = rest.shape[0] - 8
    for k in range(tasks):
        at = k
        gtb[k : k + 1] = rest[misc + at // 2 : misc + at // 2 + 1, (at % 2) * tower : (at % 2 + 1) * tower]
        at = tasks + k
        gto[k : k + 1] = rest[misc + at // 2 : misc + at // 2 + 1, (at % 2) * tower : (at % 2 + 1) * tower]
    gtob[...] = rest[misc + tasks : misc + tasks + 1, 0:tasks]
    loss[...] = rest[misc + tasks : misc + tasks + 1, tasks : tasks + 1]


def place_near_kernel(place, a0, a1, a2, a3, out, sems):
    copies = [
        pltpu.make_async_copy(ref, out.at[z ^ place[0]], sems.at[z]) for z, ref in enumerate((a0, a1, a2, a3))
    ]
    for copy in copies:
        copy.start()
    for copy in copies:
        copy.wait()


def place_far_kernel(place, b, begun, out, sems):
    copies = [pltpu.make_async_copy(b.at[z], out.at[(4 + z) ^ place[0]], sems.at[z]) for z in range(4)]
    for copy in copies:
        copy.start()
    for copy in copies:
        copy.wait()


def finish_inputs_kernel(place, factor, g0, g1, g2, g3, out):
    field = place[0]
    rows = g0.shape[0]
    for k, ref in enumerate((g0, g1, g2, g3)):
        out[pl.ds(pl.multiple_of((field ^ k) * rows, 8), rows), :] = ref[...] * factor[...]


def whole():
    return pl.BlockSpec(memory_space=VMEM)


def anywhere():
    return pl.BlockSpec(memory_space=pl.ANY)


def scalars():
    return pl.BlockSpec(memory_space=pltpu.SMEM)


def like(shape, dtype=F32):
    return jax.ShapeDtypeStruct(shape, dtype)


def after(value, *others):
    return lax.optimization_barrier((value, others))[0]


def per_device(
    n_dp,
    examples,
    domain,
    labels,
    row_counts,
    gate_weight,
    gate_bias,
    w_first,
    b_first,
    w_second,
    b_second,
    tower_first,
    tower_bias,
    tower_out,
    tower_out_bias,
):
    all_rows, cols = examples.shape
    rows = all_rows // 4
    experts, _, hidden = w_first.shape
    tasks = gate_weight.shape[0]
    width = w_second.shape[2]
    tower = tower_first.shape[2]
    domains = gate_bias.shape[0]
    units = tasks * experts
    field = lax.axis_index("field").astype(jnp.int32)
    group = lax.axis_index("dp").astype(jnp.int32)

    def move(value, dp_mask, field_mask):
        pairs = []
        for d in range(n_dp):
            for f in range(4):
                pairs.append((d * 4 + f, (d ^ dp_mask) * 4 + (f ^ field_mask)))
        return lax.ppermute(value, ("dp", "field"), pairs)

    def over_rest(value):
        mask = 8
        while mask < n_dp:
            value = value + move(value, mask, 0)
            mask *= 2
        return value

    core, chip_y = field & 1, field >> 1
    chip_x, chip_z = group & 1, (group >> 1) & 3
    me5 = core * 16 + chip_x * 8 + chip_y * 4 + chip_z
    me3 = chip_x * 4 + chip_z
    corner = group & 3

    count = row_counts[0]

    gate_rows = jnp.transpose(gate_weight, (0, 2, 1)).reshape(units, cols)
    quarter = experts // 4

    def rows_for(k):
        return lax.dynamic_slice(examples, ((field ^ k) * rows, 0), (rows, cols))

    far = move(lax.dynamic_slice(w_first, (corner * quarter, 0, 0), (quarter, cols, hidden)), 0, 2)
    near = move(w_first, 0, 1)
    place = jnp.stack([field * rows, count, me5, field, corner]).astype(jnp.int32)
    domain = domain.reshape(4, rows)
    x0 = rows_for(0)
    near_rows = jnp.concatenate([rows_for(1), gate_rows], axis=0)
    y_rows = jnp.concatenate([rows_for(2), rows_for(3), gate_rows], axis=0)
    early = (far, near, near_rows, y_rows, x0, place, domain)
    far, near, near_rows, y_rows, x0, place, domain = lax.optimization_barrier(early)

    x2 = move(y_rows, 0, 2)
    x1 = move(near_rows, 0, 1)
    far_a = [far] + [move(far, r, 0) for r in (1, 2, 3)]
    x1, x2, far_a = lax.optimization_barrier((x1, x2, far_a))

    x3 = move(x2, 0, 1)
    far_b = [move(piece, 0, 1) for piece in far_a]

    outs = pl.pallas_call(
        middle_kernel,
        name="middle",
        out_shape=(
            like((4 * cols, rows), BF16),
            like((4 * cols, rows), BF16),
            like((experts, hidden, rows), BF16),
            like((experts, hidden, rows), BF16),
            like((units, 4 * cols)),
            like((units, rows)),
            like((16, 40, width)),
            like((16, 40, width)),
            like((16, 40, width)),
            like((16, 40, width)),
        ),
        in_specs=[scalars()] * 2
        + [anywhere()] * 4
        + [whole()]
        + [anywhere()] * 10
        + [whole()] * 4
        + [anywhere()]
        + [whole()] * 4,
        out_specs=[anywhere()] * 4 + [whole()] * 2 + [anywhere()] * 4,
        scratch_shapes=[
            VMEM((4, hidden, rows), F32),
            VMEM((4, rows + units, cols), F32),
            VMEM((experts, 2 * cols, hidden), F32),
            VMEM((experts, 2 * cols, hidden), F32),
            VMEM((experts, hidden, width), F32),
            VMEM((4 * cols, rows), BF16),
            VMEM((4 * cols, rows), BF16),
            VMEM((experts, hidden, rows), BF16),
            VMEM((experts, hidden, rows), BF16),
            VMEM((experts, hidden, rows), BF16),
            VMEM((experts, hidden, rows), BF16),
            VMEM((experts, hidden, rows), F32),
            VMEM((experts, width, rows), F32),
            VMEM((units, rows), F32),
            VMEM((units, rows), F32),
            VMEM((2 * experts, hidden), F32),
            VMEM((tasks, width, rows), F32),
            VMEM((tasks, width, rows), F32),
            VMEM((units, rows), F32),
            VMEM((8, rows), F32),
            VMEM((8, rows), F32),
            VMEM((8, tower), F32),
            VMEM((32, 80, width), F32),
            VMEM((480, width), F32),
            pltpu.SemaphoreType.DMA((16,)),
        ],
        compiler_params=PARAMS,
    )(
        place,
        tower_out_bias,
        x0,
        x1,
        x2,
        x3,
        gate_rows,
        w_first,
        near,
        *far_a,
        *far_b,
        domain,
        labels.T,
        gate_bias,
        b_first,
        w_second,
        b_second,
        tower_first,
        tower_bias,
        tower_out,
    )
    xt_high, xt_low, gf_high, gf_low, gate_all, glog, sa_keep, sa_send, sb_keep, sb_send = outs

    place3 = me3.reshape(1)
    cheap = pl.CostEstimate(flops=0, bytes_accessed=1 << 20, transcendentals=0)

    def fold(keep, got, axis):
        held = keep + got
        return lax.index_in_dim(held, 0, axis, False), lax.index_in_dim(held, 1, axis, False)

    slots = (2, 2, 4, 40, width)
    sa, sa_out = fold(sa_keep.reshape(slots), move(sa_send, 0, 1).reshape(slots), 0)
    sb, sb_out = fold(sb_keep.reshape(slots), move(sb_send, 0, 1).reshape(slots), 1)
    sa, sa_out, sb, sb_out, gf_high = lax.optimization_barrier((sa, sa_out, sb, sb_out, gf_high))

    sa_got, sb_got = move(sa_out, 1, 0), move(sb_out, 0, 2)
    wa_keep, wa_send, wb_keep, wb_send = pl.pallas_call(
        first_kernel,
        name="first",
        out_shape=tuple(like((2, 8, cols // 2, hidden)) for _ in range(4)),
        in_specs=[scalars()] + [anywhere()] * 4,
        out_specs=[anywhere()] * 4,
        scratch_shapes=[
            VMEM((4 * cols, rows), BF16),
            VMEM((4 * cols, rows), BF16),
            VMEM((experts, hidden, rows), BF16),
            VMEM((experts, hidden, rows), BF16),
            VMEM((2, experts, cols, hidden), F32),
            VMEM((2, experts, cols, hidden), F32),
            pltpu.SemaphoreType.DMA((14,)),
        ],
        compiler_params=PARAMS,
        cost_estimate=cheap,
    )(place3, xt_high, xt_low, gf_high, gf_low)
    wa_got, wb_got = move(wa_send, 0, 1), move(wb_send, 0, 1)
    sa, sa_out = fold(sa, sa_got, 0)
    sb, sb_out = fold(sb, sb_got, 0)
    sa_got, sb_got = move(sa_out, 0, 2), move(sb_out, 1, 0)
    s_mine = jnp.concatenate([sa + sa_got, sb + sb_got], axis=1)
    slots = (2, 2, 4, cols // 2, hidden)
    wa, wa_out = fold(wa_keep.reshape(slots), wa_got.reshape(slots), 0)
    wb, wb_out = fold(wb_keep.reshape(slots), wb_got.reshape(slots), 1)
    stage = (wa, wa_out, wb, wb_out, s_mine, gf_low)
    wa, wa_out, wb, wb_out, s_mine, gf_low = lax.optimization_barrier(stage)

    wa_got, wb_got = move(wa_out, 0, 2), move(wb_out, 1, 0)
    s_got = [move(s_mine[z], 2 * z, 0) for z in (1, 2, 3)]
    wa, wa_out = fold(wa, wa_got, 0)
    wb, wb_out = fold(wb, wb_got, 0)
    wa_got, wb_got = move(wa_out, 1, 0), move(wb_out, 0, 2)
    s_piece = over_rest(s_mine[0] + s_got[0] + s_got[1] + s_got[2])
    factor = 1.0 / s_piece[79:80, 0:1]
    s_piece = s_piece * factor
    s_line = jnp.stack([s_piece] + [move(s_piece, 2 * z, 0) for z in (1, 2, 3)])
    w_mine = jnp.concatenate([wa + wa_got, wb + wb_got], axis=1)
    w_mine, s_line, gf_low = lax.optimization_barrier((w_mine, s_line, gf_low))

    g0, g1, g2, g3 = pl.pallas_call(
        inputs_kernel,
        name="inputs",
        out_shape=tuple(like((rows, cols)) for _ in range(4)),
        in_specs=[scalars()] + [whole()] * 2 + [anywhere()] * 12,
        out_specs=[whole()] * 4,
        scratch_shapes=[
            VMEM((experts, hidden, rows), BF16),
            VMEM((experts, hidden, rows), BF16),
            VMEM((experts, 2 * cols, hidden), F32),
            VMEM((experts, 2 * cols, hidden), F32),
            VMEM((4 * cols, rows), F32),
            pltpu.SemaphoreType.DMA((12,)),
        ],
        compiler_params=MEDIUM,
        cost_estimate=cheap,
    )(place, gate_all, glog, gf_high, gf_low, w_first, near, *far_a, *far_b)
    w_got = [move(w_mine[z], 2 * z, 0) for z in (1, 2, 3)]
    sa, sb = s_line[:, 0:40], s_line[:, 40:80]
    sa = jnp.stack([sa, move(sa, 0, 2)])
    sb = jnp.stack([sb, move(sb, 1, 0)])
    w_piece = over_rest(w_mine[0] + w_got[0] + w_got[1] + w_got[2]) * factor
    w_piece, sa, sb, g0, g1, g2, g3 = lax.optimization_barrier((w_piece, sa, sb, g0, g1, g2, g3))

    g1 = move(g1, 0, 1)
    w_line = [w_piece] + [move(w_piece, 2 * z, 0) for z in (1, 2, 3)]
    s_near = [sa, sb, move(sa, 1, 0), move(sb, 0, 2)]
    s_near, g2, g3 = lax.optimization_barrier((s_near, g2, g3))

    w_other = move(jnp.stack(w_line), 1, 0)
    g2 = move(g2, 0, 2)
    g3 = move(g3, 0, 3)
    s_far = [move(part, 0, 1) for part in s_near]

    seconds = pl.pallas_call(
        finish_second_kernel,
        name="finish_second",
        out_shape=(
            like((experts, hidden, width)),
            like((tasks, width, tower)),
            like((tasks, experts, cols)),
            like((domains, units)),
            like((experts, hidden)),
            like((experts, width)),
            like((tasks, tower)),
            like((tasks, tower)),
            like((1, tasks)),
            like((1, 1)),
        ),
        in_specs=[scalars()] + [whole()] * 8,
        out_specs=[whole()] * 10,
        scratch_shapes=[VMEM((32, 16, width), F32), VMEM((480, width), F32)],
        compiler_params=SMALL,
    )(jnp.stack([me5, field]), *s_near, *s_far)
    grad_w_second, grad_tower_first, grad_gate_weight, grad_gate_bias = seconds[:4]
    grad_b_first, grad_b_second, grad_tower_bias, grad_tower_out, grad_out_bias, loss = seconds[4:]

    grad_examples = pl.pallas_call(
        finish_inputs_kernel,
        name="finish_inputs",
        out_shape=like((all_rows, cols)),
        in_specs=[scalars()] + [whole()] * 5,
        out_specs=whole(),
        compiler_params=SMALL,
    )(field.reshape(1), factor, g0, g1, g2, g3)

    begun = pl.pallas_call(
        place_near_kernel,
        name="place_near",
        out_shape=like((experts, cols, hidden)),
        in_specs=[scalars()] + [anywhere()] * 4,
        out_specs=anywhere(),
        scratch_shapes=[pltpu.SemaphoreType.DMA((4,))],
        compiler_params=SMALL,
    )(place3, *w_line)
    grad_w_first = pl.pallas_call(
        place_far_kernel,
        name="place_far",
        out_shape=like((experts, cols, hidden)),
        in_specs=[scalars(), anywhere(), anywhere()],
        out_specs=anywhere(),
        scratch_shapes=[pltpu.SemaphoreType.DMA((4,))],
        input_output_aliases={2: 0},
        compiler_params=SMALL,
    )(place3, w_other, after(begun, grad_examples, grad_w_second))

    return (
        loss[0, 0],
        grad_examples,
        jnp.transpose(grad_gate_weight, (0, 2, 1)),
        grad_gate_bias,
        grad_w_first,
        grad_b_first,
        grad_w_second,
        grad_b_second,
        grad_tower_first,
        grad_tower_bias,
        grad_tower_out,
        grad_out_bias[0],
    )


def solution(mesh):
    placed = (
        P("dp", "field"),
        P("dp"),
        P("dp", None),
        P("dp"),
        P(None, "field", None),
        P(),
        P(None, "field", None),
        P(),
        P(),
        P(),
        P(),
        P(),
        P(),
        P(),
    )
    return jax.shard_map(
        functools.partial(per_device, mesh.shape["dp"]),
        mesh=mesh,
        in_specs=placed,
        out_specs=(
            P(),
            P("dp", "field"),
            P(None, "field", None),
            P(),
            P(None, "field", None),
            P(),
            P(),
            P(),
            P(),
            P(),
            P(),
            P(),
        ),
        check_vma=False,
    )
```

```python
import functools

import jax
import jax.numpy as jnp
from jax import lax
from jax.experimental import pallas as pl
from jax.experimental.pallas import tpu as pltpu
from jax.sharding import PartitionSpec as P

F32 = jnp.float32
BF16 = jnp.bfloat16
ROOT_HALF = 0.7071067811865476
DENSITY = 0.3989422804014327
VMEM = pltpu.VMEM
PARAMS = pltpu.CompilerParams(vmem_limit_bytes=58 * 1024 * 1024)
MEDIUM = pltpu.CompilerParams(vmem_limit_bytes=24 * 1024 * 1024)
SMALL = pltpu.CompilerParams(vmem_limit_bytes=14 * 1024 * 1024)
NN, TN, NT = (1, 0), (0, 0), (1, 1)


def split(x):
    high = x.astype(BF16)
    return high, (x - high.astype(F32)).astype(BF16)


def one_dot(a, b, dims):
    return lax.dot_general(a, b, (((dims[0],), (dims[1],)), ((), ())), preferred_element_type=F32)


def dot3(a, b, dims):
    return one_dot(a[0], b[0], dims) + (one_dot(a[0], b[1], dims) + one_dot(a[1], b[0], dims))


def gelu_parts(v):
    cdf = 0.5 + 0.5 * lax.erf(v * ROOT_HALF)
    return v * cdf, cdf + v * (DENSITY * jnp.exp(-0.5 * v * v))


def middle_kernel(
    place,
    out_bias,
    x0,
    x1,
    x2,
    x3,
    gate_rows,
    near0,
    near1,
    fa0,
    fa1,
    fa2,
    fa3,
    fb0,
    fb1,
    fb2,
    fb3,
    domain,
    labels,
    gate_bias,
    b_first,
    w_second,
    b_second,
    t_first,
    t_bias,
    t_out,
    xt_high_out,
    xt_low_out,
    gf_high_out,
    gf_low_out,
    gate_all,
    glog_out,
    sa_keep,
    sa_send,
    sb_keep,
    sb_send,
    begun,
    x_in,
    near_in,
    far_in,
    w2_in,
    xt_high,
    xt_low,
    gf_high,
    gf_low,
    hid_high,
    hid_low,
    slope,
    e_out,
    gates,
    soft_rows,
    bias_rows,
    mix,
    gmix,
    ggate,
    scores,
    targets,
    tower_rows,
    summed,
    rest,
    sems,
):
    experts = w_second.shape[0]
    tasks, width, tower = t_first.shape
    hidden = w_second.shape[1]
    rows = domain.shape[1]
    domains = gate_bias.shape[0]
    cols = near0.shape[1]
    start, count, me, field, corner = place[0], place[1], place[2], place[3], place[4]
    units = tasks * experts
    quarter = experts // 4
    order = [(r ^ corner) * quarter + i for r in range(4) for i in range(quarter)]

    loads = [
        pltpu.make_async_copy(near0, near_in.at[:, 0:cols], sems.at[0]),
        pltpu.make_async_copy(near1, near_in.at[:, cols : 2 * cols], sems.at[1]),
        pltpu.make_async_copy(w_second, w2_in, sems.at[2]),
    ]
    for r, (far_a, far_b) in enumerate(((fa0, fb0), (fa1, fb1), (fa2, fb2), (fa3, fb3))):
        target = far_in.at[r * quarter : (r + 1) * quarter]
        loads.append(pltpu.make_async_copy(far_a, target.at[:, 0:cols], sems.at[3 + 2 * r]))
        loads.append(pltpu.make_async_copy(far_b, target.at[:, cols : 2 * cols], sems.at[4 + 2 * r]))
    x_loads = [
        pltpu.make_async_copy(x0, x_in.at[0, 0:rows], sems.at[11]),
        pltpu.make_async_copy(x1, x_in.at[1], sems.at[12]),
        pltpu.make_async_copy(x2.at[0:rows], x_in.at[2, 0:rows], sems.at[13]),
        pltpu.make_async_copy(x2.at[2 * rows :], x_in.at[2, rows:], sems.at[14]),
        pltpu.make_async_copy(x3.at[rows:], x_in.at[3], sems.at[15]),
    ]
    for load in x_loads + loads:
        load.start()

    wide = tasks * experts
    for copy in x_loads:
        copy.wait()
    for k, ref in enumerate((x_in.at[0], x_in.at[1], x_in.at[2], x_in.at[3])):
        block = slice(k * cols, (k + 1) * cols)
        high, low = split(ref[0:rows, :].T)
        xt_high[block, :] = high
        xt_low[block, :] = low
        gate_all[:, block] = gate_rows[...] if k == 0 else ref[rows : rows + wide, :]
    hot = lax.broadcasted_iota(jnp.int32, (domains, rows), 0) == domain[pl.ds(field, 1), :]
    onehot = jnp.where(hot, 1.0, 0.0).astype(BF16)
    bias_high, bias_low = split(gate_bias[...])
    logits = dot3(split(gate_all[...]), (xt_high[...], xt_low[...]), NN)
    logits = logits + (one_dot(bias_high, onehot, TN) + one_dot(bias_low, onehot, TN))
    logits = logits.reshape(tasks, experts, rows)
    raised = jnp.exp(logits - jnp.max(logits, axis=1, keepdims=True))
    soft = raised / jnp.sum(raised, axis=1, keepdims=True)
    soft_rows[...] = soft.reshape(units, rows)
    for n, e in enumerate(order):
        for k in range(tasks):
            gates[k * experts + n : k * experts + n + 1, :] = soft_rows[pl.ds(k * experts + e, 1), :]
        bias_rows[n : n + 1, :] = b_first[pl.ds(e, 1), :]
        bias_rows[experts + n : experts + n + 1, :] = b_second[pl.ds(e, 1), :]
    targets[...] = jnp.zeros_like(targets)
    targets[0:tasks, :] = labels[:, pl.ds(pl.multiple_of(field * rows, 128), rows)].astype(F32)
    bias_cols = bias_rows[...].T
    rest[...] = jnp.zeros_like(rest)
    tower_rows[...] = jnp.zeros_like(tower_rows)
    tower_rows[0:tasks, :] = t_bias[...]
    tower_rows[tasks : 2 * tasks, :] = t_out[...]
    tower_cols = tower_rows[...].T
    for load in loads[0:2]:
        load.wait()
    ahead = 4
    for n in range(ahead):
        begun[n] = dot3(split(near_in[order[n]]), (xt_high[0 : 2 * cols], xt_low[0 : 2 * cols]), TN)
    for load in loads[2:]:
        load.wait()

    def first_layer(n):
        e = order[n]
        if n < ahead:
            weight = split(far_in[n])
            return begun[n] + dot3(weight, (xt_high[2 * cols :], xt_low[2 * cols :]), TN)
        weight = split(jnp.concatenate([near_in[e], far_in[n]], axis=0))
        return dot3(weight, (xt_high[...], xt_low[...]), TN)

    pre = first_layer(0)
    value = None
    for n in range(experts + 1):
        following = first_layer(n + 1) if n + 1 < experts else None
        if n < experts:
            raw, steep = gelu_parts(pre + bias_cols[:, n : n + 1])
            slope[n] = steep
        if n > 0:
            at = experts + n - 1
            result = dot3(split(w2_in[order[n - 1]]), value, TN) + bias_cols[:, at : at + 1]
            e_out[n - 1] = result
            if n % 4 == 0:
                for k in range(tasks):
                    part = gates[k * experts + n - 1 : k * experts + n, :] * result
                    for m in range(n - 4, n - 1):
                        part = part + gates[k * experts + m : k * experts + m + 1, :] * e_out[m]
                    mix[k] = part if n == 4 else mix[k] + part
        if n < experts:
            value = split(raw)
            hid_high[n], hid_low[n] = value
        pre = following

    stores = [
        pltpu.make_async_copy(xt_high, xt_high_out, sems.at[0]),
        pltpu.make_async_copy(xt_low, xt_low_out, sems.at[1]),
    ]
    for store in stores:
        store.start()

    position = start + lax.broadcasted_iota(jnp.int32, (1, rows), 1)
    live = jnp.where(position < count, 1.0, 0.0)
    row_of = lax.broadcasted_iota(jnp.int32, (8, rows), 0)
    misc = rest.shape[0] - 8
    scores[...] = jnp.zeros_like(scores)
    acts, steeps, mixed, weights = [], [], [], []
    for k in range(tasks):
        mixed.append(split(mix[k]))
        weights.append(split(t_first[k]))
        value, steep = gelu_parts(dot3(weights[k], mixed[k], TN) + tower_cols[:, k : k + 1])
        out_column = tower_cols[:, tasks + k : tasks + k + 1]
        scores[k : k + 1, :] = jnp.sum(value * out_column, axis=0, keepdims=True) + out_bias[k]
        acts.append(value)
        steeps.append(out_column * steep)
    score = scores[...]
    target = targets[...]
    task_live = jnp.where(row_of < tasks, live, 0.0)
    per_item = jnp.maximum(score, 0.0) + jnp.log1p(jnp.exp(-jnp.abs(score))) - target * score
    gscores = task_live * (jax.nn.sigmoid(score) - target)
    sums = jnp.sum(gscores, axis=1, keepdims=True)
    losses = jnp.sum(per_item * task_live, axis=(0, 1), keepdims=True)
    t_sums = []
    for k in range(tasks):
        gpre = gscores[k : k + 1, :] * steeps[k]
        t_sums.append(jnp.sum(gpre, axis=1, keepdims=True))
        t_sums.append(jnp.sum(gscores[k : k + 1, :] * acts[k], axis=1, keepdims=True))
        gpre = split(gpre)
        gmix[k] = dot3(weights[k], gpre, NN)
        gweight = dot3(mixed[k], gpre, NT)
        if k < 2:
            rest[0:width, k * tower : (k + 1) * tower] = gweight
        else:
            rest[width : width + tower, 0:tower] = gweight[0:tower]
            rest[width : width + tower, tower:] = gweight[tower:]
        rest[misc + tasks : misc + tasks + 1, k : k + 1] = sums[k : k + 1, :]
    rest[misc + tasks : misc + tasks + 1, tasks : tasks + 1] = losses

    grads = []
    b1_sums, b2_sums = [], []
    for n, e in enumerate(order):
        result = e_out[n]
        total = None
        for k in range(tasks):
            down = gmix[k]
            at = k * experts + n
            ggate[at : at + 1, :] = jnp.sum(down * result, axis=0, keepdims=True)
            part = gates[at : at + 1, :] * down
            total = part if total is None else total + part
        b2_sums.append(jnp.sum(total, axis=1, keepdims=True))
        total = split(total)
        gweight = dot3((hid_high[n], hid_low[n]), total, NT)
        piece = hidden // 4
        for i in range(4):
            slot = (4 * e + i) ^ me
            summed[slot, 0:piece, :] = gweight[i * piece : (i + 1) * piece]
        gfirst = dot3(split(w2_in[e]), total, NN) * slope[n]
        b1_sums.append(jnp.sum(gfirst, axis=1, keepdims=True))
        high, low = split(gfirst)
        gf_high[e] = high
        gf_low[e] = low
        if n % 4 == 3:
            half = pl.ds(((corner >> 1) ^ (n // 4)) * 4, 4)
            grads.append(pltpu.make_async_copy(gf_high.at[half], gf_high_out.at[half], sems.at[4 + n // 2]))
            grads.append(pltpu.make_async_copy(gf_low.at[half], gf_low_out.at[half], sems.at[5 + n // 2]))
            grads[-2].start()
            grads[-1].start()

    piece = hidden // 4
    half = summed.shape[1] // 2
    last = [
        pltpu.make_async_copy(summed.at[16:32, 0:half], sa_send, sems.at[8]),
        pltpu.make_async_copy(summed.at[0:16, 0:half], sa_keep, sems.at[9]),
        pltpu.make_async_copy(summed.at[16:32, half:], sb_send, sems.at[10]),
        pltpu.make_async_copy(summed.at[0:16, half:], sb_keep, sems.at[11]),
    ]
    last[0].start()
    last[1].start()

    lane = lax.broadcasted_iota(jnp.int32, (width, 128), 1)
    lane_t = lax.broadcasted_iota(jnp.int32, (tower, tower), 1)
    t_cols = jnp.zeros((tower, tower), F32)
    for n, column in enumerate(t_sums):
        t_cols = jnp.where(lane_t == n, column, t_cols)
    t_cols = t_cols.T
    for k in range(tasks):
        for at, n in ((k, 2 * k), (tasks + k, 2 * k + 1)):
            side = slice((at % 2) * tower, (at % 2 + 1) * tower)
            rest[misc + at // 2 : misc + at // 2 + 1, side] = t_cols[n : n + 1, :]
    sums = jnp.zeros((width, 128), F32)
    for n in range(experts):
        sums = jnp.where(lane == n, b1_sums[n], sums)
        sums = jnp.where(lane == experts + n, b2_sums[n], sums)
    sums = sums.T
    soft = gates[...].reshape(tasks, experts, rows)
    gsoft = ggate[...].reshape(tasks, experts, rows)
    glog = soft * (gsoft - jnp.sum(soft * gsoft, axis=1, keepdims=True))
    gates[...] = glog.reshape(units, rows)
    base = 2 * tower + tower + 2 * units
    for n, e in enumerate(order):
        for k in range(tasks):
            glog_out[pl.ds(k * experts + e, 1), :] = gates[k * experts + n : k * experts + n + 1, :]
        rest[pl.ds(base + e, 1), :] = sums[n : n + 1, :]
        rest[pl.ds(base + experts + e, 1), :] = sums[experts + n : experts + n + 1, :]
    glog_parts = split(glog_out[...])
    ggw = dot3(glog_parts, (xt_high[...], xt_low[...]), NT)
    base = width + tower
    for k in range(4):
        at = pl.multiple_of(base + ((field ^ k) >> 1) * units, 8)
        part = ggw[:, k * cols : (k + 1) * cols]
        low_side = ((field ^ k) & 1) == 0
        rest[pl.ds(at, units), 0:tower] = jnp.where(low_side, part, rest[pl.ds(at, units), 0:tower])
        rest[pl.ds(at, units), tower:] = jnp.where(low_side, rest[pl.ds(at, units), tower:], part)
    base = base + 2 * units + 2 * experts
    rest[base : base + domains, 0:units] = one_dot(onehot, glog_parts[0], NT) + one_dot(onehot, glog_parts[1], NT)
    alive = jnp.broadcast_to(jnp.sum(live, axis=1, keepdims=True), (1, width))
    tail = rest.shape[0] // 32
    for p in range(32):
        slot = p ^ me
        summed[slot, hidden // 4 :, :] = jnp.concatenate([rest[p * tail : (p + 1) * tail, :], alive], axis=0)
    last[2].start()
    last[3].start()
    for copy in stores + grads + last:
        copy.wait()


def first_kernel(
    place,
    xt_high_in,
    xt_low_in,
    gf_high_in,
    gf_low_in,
    keep_a,
    send_a,
    keep_b,
    send_b,
    xt_high,
    xt_low,
    gf_high,
    gf_low,
    keep,
    send,
    sems,
):
    experts, cols = keep.shape[1], keep.shape[2]
    half = experts // 2
    first_part, second_part = slice(0, half), slice(half, experts)
    loads = [
        pltpu.make_async_copy(xt_high_in, xt_high, sems.at[0]),
        pltpu.make_async_copy(xt_low_in, xt_low, sems.at[1]),
        pltpu.make_async_copy(gf_high_in.at[first_part], gf_high.at[first_part], sems.at[2]),
        pltpu.make_async_copy(gf_low_in.at[first_part], gf_low.at[first_part], sems.at[3]),
        pltpu.make_async_copy(gf_high_in.at[second_part], gf_high.at[second_part], sems.at[4]),
        pltpu.make_async_copy(gf_low_in.at[second_part], gf_low.at[second_part], sems.at[5]),
    ]
    for copy in loads:
        copy.start()
    for copy in loads[0:4]:
        copy.wait()
    stores = []
    for n in range(experts):
        if n == half:
            for copy in loads[4:6]:
                copy.wait()
        gweight = dot3((xt_high[...], xt_low[...]), (gf_high[n], gf_low[n]), NT)
        slot = n ^ place[0]
        for k in range(4):
            held = (keep, send)[k % 2]
            held[k // 2, slot] = gweight[k * cols : (k + 1) * cols]
        if n % half == half - 1:
            done = pl.ds(((place[0] >> 2) ^ (n // half)) * half, half)
            lower, upper = slice(0, cols // 2), slice(cols // 2, cols)
            pairs = ((send, send_a, lower), (send, send_b, upper), (keep, keep_a, lower), (keep, keep_b, upper))
            for held, out, part in pairs:
                at = sems.at[6 + len(stores)]
                stores.append(pltpu.make_async_copy(held.at[:, done, part], out.at[:, done], at))
                stores[-1].start()
    for copy in stores:
        copy.wait()


def inputs_kernel(
    place,
    gate_all,
    glog,
    gf_high_in,
    gf_low_in,
    near0,
    near1,
    fa0,
    fa1,
    fa2,
    fa3,
    fb0,
    fb1,
    fb2,
    fb3,
    g0,
    g1,
    g2,
    g3,
    gf_high,
    gf_low,
    near_in,
    far_in,
    total,
    sems,
):
    experts = gf_high.shape[0]
    rows, cols = g0.shape
    quarter = experts // 4
    corner = place[4]
    order = [(r ^ corner) * quarter + i for r in range(4) for i in range(quarter)]
    loads = [
        pltpu.make_async_copy(gf_high_in, gf_high, sems.at[0]),
        pltpu.make_async_copy(gf_low_in, gf_low, sems.at[1]),
        pltpu.make_async_copy(near0, near_in.at[:, 0:cols], sems.at[2]),
        pltpu.make_async_copy(near1, near_in.at[:, cols : 2 * cols], sems.at[3]),
    ]
    for r, (far_a, far_b) in enumerate(((fa0, fb0), (fa1, fb1), (fa2, fb2), (fa3, fb3))):
        target = far_in.at[r * quarter : (r + 1) * quarter]
        loads.append(pltpu.make_async_copy(far_a, target.at[:, 0:cols], sems.at[4 + 2 * r]))
        loads.append(pltpu.make_async_copy(far_b, target.at[:, cols : 2 * cols], sems.at[5 + 2 * r]))
    for copy in loads:
        copy.start()
    total[...] = dot3(split(gate_all[...]), split(glog[...]), TN)
    for copy in loads:
        copy.wait()
    for n, e in enumerate(order):
        weight = split(jnp.concatenate([near_in[e], far_in[n]], axis=0))
        total[...] += dot3(weight, (gf_high[e], gf_low[e]), NN)
    for k, ref in enumerate((g0, g1, g2, g3)):
        ref[...] = total[k * cols : (k + 1) * cols, :].T


def finish_second_kernel(
    place, factor, a0, a1, a2, a3, b0, b1, b2, b3, g0, g1, g2, g3, gw2, gtf, ggw, ggb, gb1, gb2, gtb, gto, gtob, loss, out, parts, rest
):
    me, field = place[0], place[1]
    hidden = gw2.shape[1]
    piece = hidden // 4
    tasks, width, tower = gtf.shape
    experts = ggw.shape[1]
    units = tasks * experts
    domains = ggb.shape[0]
    tail = rest.shape[0] // 32
    half = (piece + tail + 1) // 2
    for s, (ref_a, ref_b) in enumerate(((a0, a1), (a2, a3), (b0, b1), (b2, b3))):
        for i in range(2):
            for z in range(4):
                p = ((s // 2) * 16 + ((s % 2) * 2 + i) * 4 + z) ^ me
                gw2[p // 4, pl.ds(pl.multiple_of((p % 4) * piece, 8), half), :] = ref_a[i, z]
                p = ((s // 2) * 16 + ((s % 2) + 2 * i) * 4 + z) ^ me
                at = pl.multiple_of((p % 4) * piece + half, 8)
                gw2[p // 4, pl.ds(at, piece - half), :] = ref_b[i, z, 0 : piece - half]
                parts[p] = ref_b[i, z, piece - half :]
    for p in range(32):
        rest[p * tail : (p + 1) * tail, :] = parts[p, 0:tail]
    gtf[0] = rest[0:width, 0:tower]
    gtf[1] = rest[0:width, tower:]
    gtf[2, 0:tower] = rest[width : width + tower, 0:tower]
    gtf[2, tower:] = rest[width : width + tower, tower:]
    base = width + tower
    mine = rest[pl.ds(pl.multiple_of(base + (field >> 1) * units, 8), units), :]
    mine = jnp.where((field & 1) == 0, mine[:, 0:tower], mine[:, tower:])
    for k in range(tasks):
        ggw[k] = mine[k * experts : (k + 1) * experts]
    base = base + 2 * units
    gb1[...] = rest[base : base + experts, :]
    gb2[...] = rest[base + experts : base + 2 * experts, :]
    base = base + 2 * experts
    ggb[...] = rest[base : base + domains, 0:units]
    misc = rest.shape[0] - 8
    for k in range(tasks):
        at = k
        gtb[k : k + 1] = rest[misc + at // 2 : misc + at // 2 + 1, (at % 2) * tower : (at % 2 + 1) * tower]
        at = tasks + k
        gto[k : k + 1] = rest[misc + at // 2 : misc + at // 2 + 1, (at % 2) * tower : (at % 2 + 1) * tower]
    gtob[...] = rest[misc + tasks : misc + tasks + 1, 0:tasks]
    loss[...] = rest[misc + tasks : misc + tasks + 1, tasks : tasks + 1]
    rows = g0.shape[0]
    for k, ref in enumerate((g0, g1, g2, g3)):
        out[pl.ds(pl.multiple_of((field ^ k) * rows, 8), rows), :] = ref[...] * factor[...]


def place_near_kernel(place, a0, a1, a2, a3, out, sems):
    copies = [
        pltpu.make_async_copy(ref, out.at[z ^ place[0]], sems.at[z]) for z, ref in enumerate((a0, a1, a2, a3))
    ]
    for copy in copies:
        copy.start()
    for copy in copies:
        copy.wait()


def place_far_kernel(place, b, begun, out, sems):
    copies = [pltpu.make_async_copy(b.at[z], out.at[(4 + z) ^ place[0]], sems.at[z]) for z in range(4)]
    for copy in copies:
        copy.start()
    for copy in copies:
        copy.wait()


def whole():
    return pl.BlockSpec(memory_space=VMEM)


def anywhere():
    return pl.BlockSpec(memory_space=pl.ANY)


def scalars():
    return pl.BlockSpec(memory_space=pltpu.SMEM)


def like(shape, dtype=F32):
    return jax.ShapeDtypeStruct(shape, dtype)


def after(value, *others):
    return lax.optimization_barrier((value, others))[0]


def per_device(
    n_dp,
    examples,
    domain,
    labels,
    row_counts,
    gate_weight,
    gate_bias,
    w_first,
    b_first,
    w_second,
    b_second,
    tower_first,
    tower_bias,
    tower_out,
    tower_out_bias,
):
    all_rows, cols = examples.shape
    rows = all_rows // 4
    experts, _, hidden = w_first.shape
    tasks = gate_weight.shape[0]
    width = w_second.shape[2]
    tower = tower_first.shape[2]
    domains = gate_bias.shape[0]
    units = tasks * experts
    field = lax.axis_index("field").astype(jnp.int32)
    group = lax.axis_index("dp").astype(jnp.int32)

    def move(value, dp_mask, field_mask):
        pairs = []
        for d in range(n_dp):
            for f in range(4):
                pairs.append((d * 4 + f, (d ^ dp_mask) * 4 + (f ^ field_mask)))
        return lax.ppermute(value, ("dp", "field"), pairs)

    def over_rest(value):
        mask = 8
        while mask < n_dp:
            value = value + move(value, mask, 0)
            mask *= 2
        return value

    core, chip_y = field & 1, field >> 1
    chip_x, chip_z = group & 1, (group >> 1) & 3
    me5 = core * 16 + chip_x * 8 + chip_y * 4 + chip_z
    me3 = chip_x * 4 + chip_z
    corner = group & 3

    count = row_counts[0]

    gate_rows = jnp.transpose(gate_weight, (0, 2, 1)).reshape(units, cols)
    quarter = experts // 4

    def rows_for(k):
        return lax.dynamic_slice(examples, ((field ^ k) * rows, 0), (rows, cols))

    far = move(lax.dynamic_slice(w_first, (corner * quarter, 0, 0), (quarter, cols, hidden)), 0, 2)
    near = move(w_first, 0, 1)
    place = jnp.stack([field * rows, count, me5, field, corner]).astype(jnp.int32)
    domain = domain.reshape(4, rows)
    x0 = rows_for(0)
    near_rows = jnp.concatenate([rows_for(1), gate_rows], axis=0)
    y_rows = jnp.concatenate([rows_for(2), rows_for(3), gate_rows], axis=0)
    early = (far, near, near_rows, y_rows, x0, place, domain)
    far, near, near_rows, y_rows, x0, place, domain = lax.optimization_barrier(early)

    x2 = move(y_rows, 0, 2)
    x1 = move(near_rows, 0, 1)
    far_a = [far] + [move(far, r, 0) for r in (1, 2, 3)]
    x1, x2, far_a = lax.optimization_barrier((x1, x2, far_a))

    x3 = move(x2, 0, 1)
    far_b = [move(piece, 0, 1) for piece in far_a]

    outs = pl.pallas_call(
        middle_kernel,
        name="middle",
        out_shape=(
            like((4 * cols, rows), BF16),
            like((4 * cols, rows), BF16),
            like((experts, hidden, rows), BF16),
            like((experts, hidden, rows), BF16),
            like((units, 4 * cols)),
            like((units, rows)),
            like((16, 40, width)),
            like((16, 40, width)),
            like((16, 40, width)),
            like((16, 40, width)),
        ),
        in_specs=[scalars()] * 2
        + [anywhere()] * 4
        + [whole()]
        + [anywhere()] * 10
        + [whole()] * 4
        + [anywhere()]
        + [whole()] * 4,
        out_specs=[anywhere()] * 4 + [whole()] * 2 + [anywhere()] * 4,
        scratch_shapes=[
            VMEM((4, hidden, rows), F32),
            VMEM((4, rows + units, cols), F32),
            VMEM((experts, 2 * cols, hidden), F32),
            VMEM((experts, 2 * cols, hidden), F32),
            VMEM((experts, hidden, width), F32),
            VMEM((4 * cols, rows), BF16),
            VMEM((4 * cols, rows), BF16),
            VMEM((experts, hidden, rows), BF16),
            VMEM((experts, hidden, rows), BF16),
            VMEM((experts, hidden, rows), BF16),
            VMEM((experts, hidden, rows), BF16),
            VMEM((experts, hidden, rows), F32),
            VMEM((experts, width, rows), F32),
            VMEM((units, rows), F32),
            VMEM((units, rows), F32),
            VMEM((2 * experts, hidden), F32),
            VMEM((tasks, width, rows), F32),
            VMEM((tasks, width, rows), F32),
            VMEM((units, rows), F32),
            VMEM((8, rows), F32),
            VMEM((8, rows), F32),
            VMEM((8, tower), F32),
            VMEM((32, 80, width), F32),
            VMEM((480, width), F32),
            pltpu.SemaphoreType.DMA((16,)),
        ],
        compiler_params=PARAMS,
    )(
        place,
        tower_out_bias,
        x0,
        x1,
        x2,
        x3,
        gate_rows,
        w_first,
        near,
        *far_a,
        *far_b,
        domain,
        labels.T,
        gate_bias,
        b_first,
        w_second,
        b_second,
        tower_first,
        tower_bias,
        tower_out,
    )
    xt_high, xt_low, gf_high, gf_low, gate_all, glog, sa_keep, sa_send, sb_keep, sb_send = outs

    place3 = me3.reshape(1)
    cheap = pl.CostEstimate(flops=0, bytes_accessed=1 << 20, transcendentals=0)

    def fold(keep, got, axis):
        held = keep + got
        return lax.index_in_dim(held, 0, axis, False), lax.index_in_dim(held, 1, axis, False)

    slots = (2, 2, 4, 40, width)
    sa, sa_out = fold(sa_keep.reshape(slots), move(sa_send, 0, 1).reshape(slots), 0)
    sb, sb_out = fold(sb_keep.reshape(slots), move(sb_send, 0, 1).reshape(slots), 1)
    sa, sa_out, sb, sb_out, gf_high = lax.optimization_barrier((sa, sa_out, sb, sb_out, gf_high))

    sa_got, sb_got = move(sa_out, 1, 0), move(sb_out, 0, 2)
    wa_keep, wa_send, wb_keep, wb_send = pl.pallas_call(
        first_kernel,
        name="first",
        out_shape=tuple(like((2, 8, cols // 2, hidden)) for _ in range(4)),
        in_specs=[scalars()] + [anywhere()] * 4,
        out_specs=[anywhere()] * 4,
        scratch_shapes=[
            VMEM((4 * cols, rows), BF16),
            VMEM((4 * cols, rows), BF16),
            VMEM((experts, hidden, rows), BF16),
            VMEM((experts, hidden, rows), BF16),
            VMEM((2, experts, cols, hidden), F32),
            VMEM((2, experts, cols, hidden), F32),
            pltpu.SemaphoreType.DMA((14,)),
        ],
        compiler_params=PARAMS,
        cost_estimate=cheap,
    )(place3, xt_high, xt_low, gf_high, gf_low)
    wa_got, wb_got = move(wa_send, 0, 1), move(wb_send, 0, 1)
    sa, sa_out = fold(sa, sa_got, 0)
    sb, sb_out = fold(sb, sb_got, 0)
    sa_got, sb_got = move(sa_out, 0, 2), move(sb_out, 1, 0)
    s_mine = jnp.concatenate([sa + sa_got, sb + sb_got], axis=1)
    slots = (2, 2, 4, cols // 2, hidden)
    wa, wa_out = fold(wa_keep.reshape(slots), wa_got.reshape(slots), 0)
    wb, wb_out = fold(wb_keep.reshape(slots), wb_got.reshape(slots), 1)
    stage = (wa, wa_out, wb, wb_out, s_mine, gf_low)
    wa, wa_out, wb, wb_out, s_mine, gf_low = lax.optimization_barrier(stage)

    wa_got, wb_got = move(wa_out, 0, 2), move(wb_out, 1, 0)
    s_got = [move(s_mine[z], 2 * z, 0) for z in (1, 2, 3)]
    wa, wa_out = fold(wa, wa_got, 0)
    wb, wb_out = fold(wb, wb_got, 0)
    wa_got, wb_got = move(wa_out, 1, 0), move(wb_out, 0, 2)
    s_piece = over_rest(s_mine[0] + s_got[0] + s_got[1] + s_got[2])
    factor = 1.0 / s_piece[79:80, 0:1]
    s_piece = s_piece * factor
    s_line = jnp.stack([s_piece] + [move(s_piece, 2 * z, 0) for z in (1, 2, 3)])
    w_mine = jnp.concatenate([wa + wa_got, wb + wb_got], axis=1)
    w_mine, s_line, gf_low = lax.optimization_barrier((w_mine, s_line, gf_low))

    g0, g1, g2, g3 = pl.pallas_call(
        inputs_kernel,
        name="inputs",
        out_shape=tuple(like((rows, cols)) for _ in range(4)),
        in_specs=[scalars()] + [whole()] * 2 + [anywhere()] * 12,
        out_specs=[whole()] * 4,
        scratch_shapes=[
            VMEM((experts, hidden, rows), BF16),
            VMEM((experts, hidden, rows), BF16),
            VMEM((experts, 2 * cols, hidden), F32),
            VMEM((experts, 2 * cols, hidden), F32),
            VMEM((4 * cols, rows), F32),
            pltpu.SemaphoreType.DMA((12,)),
        ],
        compiler_params=MEDIUM,
        cost_estimate=cheap,
    )(place, gate_all, glog, gf_high, gf_low, w_first, near, *far_a, *far_b)
    w_got = [move(w_mine[z], 2 * z, 0) for z in (1, 2, 3)]
    sa, sb = s_line[:, 0:40], s_line[:, 40:80]
    sa = jnp.stack([sa, move(sa, 0, 2)])
    sb = jnp.stack([sb, move(sb, 1, 0)])
    w_piece = over_rest(w_mine[0] + w_got[0] + w_got[1] + w_got[2]) * factor
    w_piece, sa, sb, g0, g1, g2, g3 = lax.optimization_barrier((w_piece, sa, sb, g0, g1, g2, g3))

    g1 = move(g1, 0, 1)
    w_line = [w_piece] + [move(w_piece, 2 * z, 0) for z in (1, 2, 3)]
    s_near = [sa, sb, move(sa, 1, 0), move(sb, 0, 2)]
    s_near, g2, g3 = lax.optimization_barrier((s_near, g2, g3))

    w_other = move(jnp.stack(w_line), 1, 0)
    g2 = move(g2, 0, 2)
    g3 = move(g3, 0, 3)
    s_far = [move(part, 0, 1) for part in s_near]

    seconds = pl.pallas_call(
        finish_second_kernel,
        name="finish_second",
        out_shape=(
            like((experts, hidden, width)),
            like((tasks, width, tower)),
            like((tasks, experts, cols)),
            like((domains, units)),
            like((experts, hidden)),
            like((experts, width)),
            like((tasks, tower)),
            like((tasks, tower)),
            like((1, tasks)),
            like((1, 1)),
            like((all_rows, cols)),
        ),
        in_specs=[scalars()] + [whole()] * 13,
        out_specs=[whole()] * 11,
        scratch_shapes=[VMEM((32, 16, width), F32), VMEM((480, width), F32)],
        compiler_params=SMALL,
    )(jnp.stack([me5, field]), factor, *s_near, *s_far, g0, g1, g2, g3)
    grad_w_second, grad_tower_first, grad_gate_weight, grad_gate_bias = seconds[:4]
    grad_b_first, grad_b_second, grad_tower_bias, grad_tower_out, grad_out_bias, loss, grad_examples = seconds[4:]

    begun = pl.pallas_call(
        place_near_kernel,
        name="place_near",
        out_shape=like((experts, cols, hidden)),
        in_specs=[scalars()] + [anywhere()] * 4,
        out_specs=anywhere(),
        scratch_shapes=[pltpu.SemaphoreType.DMA((4,))],
        compiler_params=SMALL,
    )(place3, *w_line)
    grad_w_first = pl.pallas_call(
        place_far_kernel,
        name="place_far",
        out_shape=like((experts, cols, hidden)),
        in_specs=[scalars(), anywhere(), anywhere()],
        out_specs=anywhere(),
        scratch_shapes=[pltpu.SemaphoreType.DMA((4,))],
        input_output_aliases={2: 0},
        compiler_params=SMALL,
    )(place3, w_other, after(begun, grad_examples, grad_w_second))

    return (
        loss[0, 0],
        grad_examples,
        jnp.transpose(grad_gate_weight, (0, 2, 1)),
        grad_gate_bias,
        grad_w_first,
        grad_b_first,
        grad_w_second,
        grad_b_second,
        grad_tower_first,
        grad_tower_bias,
        grad_tower_out,
        grad_out_bias[0],
    )


def solution(mesh):
    placed = (
        P("dp", "field"),
        P("dp"),
        P("dp", None),
        P("dp"),
        P(None, "field", None),
        P(),
        P(None, "field", None),
        P(),
        P(),
        P(),
        P(),
        P(),
        P(),
        P(),
    )
    return jax.shard_map(
        functools.partial(per_device, mesh.shape["dp"]),
        mesh=mesh,
        in_specs=placed,
        out_specs=(
            P(),
            P("dp", "field"),
            P(None, "field", None),
            P(),
            P(None, "field", None),
            P(),
            P(),
            P(),
            P(),
            P(),
            P(),
            P(),
        ),
        check_vma=False,
    )
```

```python
import functools

import jax
import jax.numpy as jnp
from jax import lax
from jax.experimental import pallas as pl
from jax.experimental.pallas import tpu as pltpu
from jax.sharding import PartitionSpec as P

F32 = jnp.float32
BF16 = jnp.bfloat16
ROOT_HALF = 0.7071067811865476
DENSITY = 0.3989422804014327
VMEM = pltpu.VMEM
PARAMS = pltpu.CompilerParams(vmem_limit_bytes=58 * 1024 * 1024)
MEDIUM = pltpu.CompilerParams(vmem_limit_bytes=24 * 1024 * 1024)
SMALL = pltpu.CompilerParams(vmem_limit_bytes=12 * 1024 * 1024)
NN, TN, NT = (1, 0), (0, 0), (1, 1)


def split(x):
    high = x.astype(BF16)
    return high, (x - high.astype(F32)).astype(BF16)


def one_dot(a, b, dims):
    return lax.dot_general(a, b, (((dims[0],), (dims[1],)), ((), ())), preferred_element_type=F32)


def dot3(a, b, dims):
    return one_dot(a[0], b[0], dims) + (one_dot(a[0], b[1], dims) + one_dot(a[1], b[0], dims))


def gelu_parts(v):
    cdf = 0.5 + 0.5 * lax.erf(v * ROOT_HALF)
    return v * cdf, cdf + v * (DENSITY * jnp.exp(-0.5 * v * v))


def middle_kernel(
    place,
    out_bias,
    x0,
    x1,
    x2,
    x3,
    gate_rows,
    near0,
    near1,
    fa0,
    fa1,
    fa2,
    fa3,
    fb0,
    fb1,
    fb2,
    fb3,
    domain,
    labels,
    gate_bias,
    b_first,
    w_second,
    b_second,
    t_first,
    t_bias,
    t_out,
    xt_high_out,
    xt_low_out,
    gf_high_out,
    gf_low_out,
    gate_all,
    glog_out,
    sa_keep,
    sa_send,
    sb_keep,
    sb_send,
    begun,
    x_in,
    near_in,
    far_in,
    w2_in,
    xt_high,
    xt_low,
    gf_high,
    gf_low,
    hid_high,
    hid_low,
    slope,
    e_out,
    gates,
    soft_rows,
    bias_rows,
    mix,
    gmix,
    ggate,
    scores,
    targets,
    tower_rows,
    summed,
    rest,
    sems,
):
    experts = w_second.shape[0]
    tasks, width, tower = t_first.shape
    hidden = w_second.shape[1]
    rows = domain.shape[1]
    domains = gate_bias.shape[0]
    cols = near0.shape[1]
    start, count, me, field, corner = place[0], place[1], place[2], place[3], place[4]
    units = tasks * experts
    quarter = experts // 4
    order = [(r ^ corner) * quarter + i for r in range(4) for i in range(quarter)]

    loads = [
        pltpu.make_async_copy(near0, near_in.at[:, 0:cols], sems.at[0]),
        pltpu.make_async_copy(near1, near_in.at[:, cols : 2 * cols], sems.at[1]),
        pltpu.make_async_copy(w_second, w2_in, sems.at[2]),
    ]
    for r, (far_a, far_b) in enumerate(((fa0, fb0), (fa1, fb1), (fa2, fb2), (fa3, fb3))):
        target = far_in.at[r * quarter : (r + 1) * quarter]
        loads.append(pltpu.make_async_copy(far_a, target.at[:, 0:cols], sems.at[3 + 2 * r]))
        loads.append(pltpu.make_async_copy(far_b, target.at[:, cols : 2 * cols], sems.at[4 + 2 * r]))
    x_loads = [
        pltpu.make_async_copy(x0, x_in.at[0, 0:rows], sems.at[11]),
        pltpu.make_async_copy(x1, x_in.at[1], sems.at[12]),
        pltpu.make_async_copy(x2.at[0:rows], x_in.at[2, 0:rows], sems.at[13]),
        pltpu.make_async_copy(x2.at[2 * rows :], x_in.at[2, rows:], sems.at[14]),
        pltpu.make_async_copy(x3.at[rows:], x_in.at[3], sems.at[15]),
    ]
    for load in x_loads + loads:
        load.start()

    wide = tasks * experts
    for copy in x_loads:
        copy.wait()
    for k, ref in enumerate((x_in.at[0], x_in.at[1], x_in.at[2], x_in.at[3])):
        block = slice(k * cols, (k + 1) * cols)
        high, low = split(ref[0:rows, :].T)
        xt_high[block, :] = high
        xt_low[block, :] = low
        gate_all[:, block] = gate_rows[...] if k == 0 else ref[rows : rows + wide, :]
    hot = lax.broadcasted_iota(jnp.int32, (domains, rows), 0) == domain[pl.ds(field, 1), :]
    onehot = jnp.where(hot, 1.0, 0.0).astype(BF16)
    bias_high, bias_low = split(gate_bias[...])
    logits = dot3(split(gate_all[...]), (xt_high[...], xt_low[...]), NN)
    logits = logits + (one_dot(bias_high, onehot, TN) + one_dot(bias_low, onehot, TN))
    logits = logits.reshape(tasks, experts, rows)
    raised = jnp.exp(logits - jnp.max(logits, axis=1, keepdims=True))
    soft = raised / jnp.sum(raised, axis=1, keepdims=True)
    soft_rows[...] = soft.reshape(units, rows)
    for n, e in enumerate(order):
        for k in range(tasks):
            gates[k * experts + n : k * experts + n + 1, :] = soft_rows[pl.ds(k * experts + e, 1), :]
        bias_rows[n : n + 1, :] = b_first[pl.ds(e, 1), :]
        bias_rows[experts + n : experts + n + 1, :] = b_second[pl.ds(e, 1), :]
    targets[...] = jnp.zeros_like(targets)
    targets[0:tasks, :] = labels[:, pl.ds(pl.multiple_of(field * rows, 128), rows)].astype(F32)
    bias_cols = bias_rows[...].T
    rest[...] = jnp.zeros_like(rest)
    tower_rows[...] = jnp.zeros_like(tower_rows)
    tower_rows[0:tasks, :] = t_bias[...]
    tower_rows[tasks : 2 * tasks, :] = t_out[...]
    tower_cols = tower_rows[...].T
    for load in loads[0:2]:
        load.wait()
    ahead = 6
    for n in range(ahead):
        begun[n] = dot3(split(near_in[order[n]]), (xt_high[0 : 2 * cols], xt_low[0 : 2 * cols]), TN)
    for load in loads[2:]:
        load.wait()

    def first_layer(n):
        e = order[n]
        if n < ahead:
            weight = split(far_in[n])
            return begun[n] + dot3(weight, (xt_high[2 * cols :], xt_low[2 * cols :]), TN)
        weight = split(jnp.concatenate([near_in[e], far_in[n]], axis=0))
        return dot3(weight, (xt_high[...], xt_low[...]), TN)

    pre = first_layer(0)
    value = None
    for n in range(experts + 1):
        following = first_layer(n + 1) if n + 1 < experts else None
        if n < experts:
            raw, steep = gelu_parts(pre + bias_cols[:, n : n + 1])
            slope[n] = steep
        if n > 0:
            at = experts + n - 1
            result = dot3(split(w2_in[order[n - 1]]), value, TN) + bias_cols[:, at : at + 1]
            e_out[n - 1] = result
            if n % 4 == 0:
                for k in range(tasks):
                    part = gates[k * experts + n - 1 : k * experts + n, :] * result
                    for m in range(n - 4, n - 1):
                        part = part + gates[k * experts + m : k * experts + m + 1, :] * e_out[m]
                    mix[k] = part if n == 4 else mix[k] + part
        if n < experts:
            value = split(raw)
            hid_high[n], hid_low[n] = value
        pre = following

    stores = [
        pltpu.make_async_copy(xt_high, xt_high_out, sems.at[0]),
        pltpu.make_async_copy(xt_low, xt_low_out, sems.at[1]),
    ]
    for store in stores:
        store.start()

    position = start + lax.broadcasted_iota(jnp.int32, (1, rows), 1)
    live = jnp.where(position < count, 1.0, 0.0)
    row_of = lax.broadcasted_iota(jnp.int32, (8, rows), 0)
    misc = rest.shape[0] - 8
    scores[...] = jnp.zeros_like(scores)
    acts, steeps, mixed, weights = [], [], [], []
    for k in range(tasks):
        mixed.append(split(mix[k]))
        weights.append(split(t_first[k]))
        value, steep = gelu_parts(dot3(weights[k], mixed[k], TN) + tower_cols[:, k : k + 1])
        out_column = tower_cols[:, tasks + k : tasks + k + 1]
        scores[k : k + 1, :] = jnp.sum(value * out_column, axis=0, keepdims=True) + out_bias[k]
        acts.append(value)
        steeps.append(out_column * steep)
    score = scores[...]
    target = targets[...]
    task_live = jnp.where(row_of < tasks, live, 0.0)
    per_item = jnp.maximum(score, 0.0) + jnp.log1p(jnp.exp(-jnp.abs(score))) - target * score
    gscores = task_live * (jax.nn.sigmoid(score) - target)
    sums = jnp.sum(gscores, axis=1, keepdims=True)
    losses = jnp.sum(per_item * task_live, axis=(0, 1), keepdims=True)
    t_sums = []
    for k in range(tasks):
        gpre = gscores[k : k + 1, :] * steeps[k]
        t_sums.append(jnp.sum(gpre, axis=1, keepdims=True))
        t_sums.append(jnp.sum(gscores[k : k + 1, :] * acts[k], axis=1, keepdims=True))
        gpre = split(gpre)
        gmix[k] = dot3(weights[k], gpre, NN)
        gweight = dot3(mixed[k], gpre, NT)
        if k < 2:
            rest[0:width, k * tower : (k + 1) * tower] = gweight
        else:
            rest[width : width + tower, 0:tower] = gweight[0:tower]
            rest[width : width + tower, tower:] = gweight[tower:]
        rest[misc + tasks : misc + tasks + 1, k : k + 1] = sums[k : k + 1, :]
    rest[misc + tasks : misc + tasks + 1, tasks : tasks + 1] = losses

    grads = []
    b1_sums, b2_sums = [], []
    for n, e in enumerate(order):
        result = e_out[n]
        total = None
        for k in range(tasks):
            down = gmix[k]
            at = k * experts + n
            ggate[at : at + 1, :] = jnp.sum(down * result, axis=0, keepdims=True)
            part = gates[at : at + 1, :] * down
            total = part if total is None else total + part
        b2_sums.append(jnp.sum(total, axis=1, keepdims=True))
        total = split(total)
        gweight = dot3((hid_high[n], hid_low[n]), total, NT)
        piece = hidden // 4
        for i in range(4):
            slot = (4 * e + i) ^ me
            summed[slot, 0:piece, :] = gweight[i * piece : (i + 1) * piece]
        gfirst = dot3(split(w2_in[e]), total, NN) * slope[n]
        b1_sums.append(jnp.sum(gfirst, axis=1, keepdims=True))
        high, low = split(gfirst)
        gf_high[e] = high
        gf_low[e] = low
        if n % 4 == 3:
            half = pl.ds(((corner >> 1) ^ (n // 4)) * 4, 4)
            grads.append(pltpu.make_async_copy(gf_high.at[half], gf_high_out.at[half], sems.at[4 + n // 2]))
            grads.append(pltpu.make_async_copy(gf_low.at[half], gf_low_out.at[half], sems.at[5 + n // 2]))
            grads[-2].start()
            grads[-1].start()

    piece = hidden // 4
    half = summed.shape[1] // 2
    last = [
        pltpu.make_async_copy(summed.at[16:32, 0:half], sa_send, sems.at[8]),
        pltpu.make_async_copy(summed.at[0:16, 0:half], sa_keep, sems.at[9]),
        pltpu.make_async_copy(summed.at[16:32, half:], sb_send, sems.at[10]),
        pltpu.make_async_copy(summed.at[0:16, half:], sb_keep, sems.at[11]),
    ]
    last[0].start()
    last[1].start()

    lane = lax.broadcasted_iota(jnp.int32, (width, 128), 1)
    lane_t = lax.broadcasted_iota(jnp.int32, (tower, tower), 1)
    t_cols = jnp.zeros((tower, tower), F32)
    for n, column in enumerate(t_sums):
        t_cols = jnp.where(lane_t == n, column, t_cols)
    t_cols = t_cols.T
    for k in range(tasks):
        for at, n in ((k, 2 * k), (tasks + k, 2 * k + 1)):
            side = slice((at % 2) * tower, (at % 2 + 1) * tower)
            rest[misc + at // 2 : misc + at // 2 + 1, side] = t_cols[n : n + 1, :]
    sums = jnp.zeros((width, 128), F32)
    for n in range(experts):
        sums = jnp.where(lane == n, b1_sums[n], sums)
        sums = jnp.where(lane == experts + n, b2_sums[n], sums)
    sums = sums.T
    soft = gates[...].reshape(tasks, experts, rows)
    gsoft = ggate[...].reshape(tasks, experts, rows)
    glog = soft * (gsoft - jnp.sum(soft * gsoft, axis=1, keepdims=True))
    gates[...] = glog.reshape(units, rows)
    base = 2 * tower + tower + 2 * units
    for n, e in enumerate(order):
        for k in range(tasks):
            glog_out[pl.ds(k * experts + e, 1), :] = gates[k * experts + n : k * experts + n + 1, :]
        rest[pl.ds(base + e, 1), :] = sums[n : n + 1, :]
        rest[pl.ds(base + experts + e, 1), :] = sums[experts + n : experts + n + 1, :]
    glog_parts = split(glog_out[...])
    ggw = dot3(glog_parts, (xt_high[...], xt_low[...]), NT)
    base = width + tower
    for k in range(4):
        at = pl.multiple_of(base + ((field ^ k) >> 1) * units, 8)
        part = ggw[:, k * cols : (k + 1) * cols]
        low_side = ((field ^ k) & 1) == 0
        rest[pl.ds(at, units), 0:tower] = jnp.where(low_side, part, rest[pl.ds(at, units), 0:tower])
        rest[pl.ds(at, units), tower:] = jnp.where(low_side, rest[pl.ds(at, units), tower:], part)
    base = base + 2 * units + 2 * experts
    rest[base : base + domains, 0:units] = one_dot(onehot, glog_parts[0], NT) + one_dot(onehot, glog_parts[1], NT)
    alive = jnp.broadcast_to(jnp.sum(live, axis=1, keepdims=True), (1, width))
    tail = rest.shape[0] // 32
    for p in range(32):
        slot = p ^ me
        summed[slot, hidden // 4 :, :] = jnp.concatenate([rest[p * tail : (p + 1) * tail, :], alive], axis=0)
    last[2].start()
    last[3].start()
    for copy in stores + grads + last:
        copy.wait()


def first_kernel(
    place,
    xt_high_in,
    xt_low_in,
    gf_high_in,
    gf_low_in,
    keep_a,
    send_a,
    keep_b,
    send_b,
    xt_high,
    xt_low,
    gf_high,
    gf_low,
    keep,
    send,
    sems,
):
    experts, cols = keep.shape[1], keep.shape[2]
    half = experts // 2
    first_part, second_part = slice(0, half), slice(half, experts)
    loads = [
        pltpu.make_async_copy(xt_high_in, xt_high, sems.at[0]),
        pltpu.make_async_copy(xt_low_in, xt_low, sems.at[1]),
        pltpu.make_async_copy(gf_high_in.at[first_part], gf_high.at[first_part], sems.at[2]),
        pltpu.make_async_copy(gf_low_in.at[first_part], gf_low.at[first_part], sems.at[3]),
        pltpu.make_async_copy(gf_high_in.at[second_part], gf_high.at[second_part], sems.at[4]),
        pltpu.make_async_copy(gf_low_in.at[second_part], gf_low.at[second_part], sems.at[5]),
    ]
    for copy in loads:
        copy.start()
    for copy in loads[0:4]:
        copy.wait()
    stores = []
    for n in range(experts):
        if n == half:
            for copy in loads[4:6]:
                copy.wait()
        gweight = dot3((xt_high[...], xt_low[...]), (gf_high[n], gf_low[n]), NT)
        slot = n ^ place[0]
        for k in range(4):
            held = (keep, send)[k % 2]
            held[k // 2, slot] = gweight[k * cols : (k + 1) * cols]
        if n % half == half - 1:
            done = pl.ds(((place[0] >> 2) ^ (n // half)) * half, half)
            lower, upper = slice(0, cols // 2), slice(cols // 2, cols)
            pairs = ((send, send_a, lower), (send, send_b, upper), (keep, keep_a, lower), (keep, keep_b, upper))
            for held, out, part in pairs:
                at = sems.at[6 + len(stores)]
                stores.append(pltpu.make_async_copy(held.at[:, done, part], out.at[:, done], at))
                stores[-1].start()
    for copy in stores:
        copy.wait()


def inputs_kernel(
    place,
    gate_all,
    glog,
    gf_high_in,
    gf_low_in,
    near0,
    near1,
    fa0,
    fa1,
    fa2,
    fa3,
    fb0,
    fb1,
    fb2,
    fb3,
    g0,
    g1,
    g2,
    g3,
    gf_high,
    gf_low,
    near_in,
    far_in,
    total,
    sems,
):
    experts = gf_high.shape[0]
    rows, cols = g0.shape
    quarter = experts // 4
    corner = place[4]
    order = [(r ^ corner) * quarter + i for r in range(4) for i in range(quarter)]
    loads = [
        pltpu.make_async_copy(gf_high_in, gf_high, sems.at[0]),
        pltpu.make_async_copy(gf_low_in, gf_low, sems.at[1]),
        pltpu.make_async_copy(near0, near_in.at[:, 0:cols], sems.at[2]),
        pltpu.make_async_copy(near1, near_in.at[:, cols : 2 * cols], sems.at[3]),
    ]
    for r, (far_a, far_b) in enumerate(((fa0, fb0), (fa1, fb1), (fa2, fb2), (fa3, fb3))):
        target = far_in.at[r * quarter : (r + 1) * quarter]
        loads.append(pltpu.make_async_copy(far_a, target.at[:, 0:cols], sems.at[4 + 2 * r]))
        loads.append(pltpu.make_async_copy(far_b, target.at[:, cols : 2 * cols], sems.at[5 + 2 * r]))
    for copy in loads:
        copy.start()
    total[...] = dot3(split(gate_all[...]), split(glog[...]), TN)
    for copy in loads:
        copy.wait()
    for n, e in enumerate(order):
        weight = split(jnp.concatenate([near_in[e], far_in[n]], axis=0))
        total[...] += dot3(weight, (gf_high[e], gf_low[e]), NN)
    for k, ref in enumerate((g0, g1, g2, g3)):
        ref[...] = total[k * cols : (k + 1) * cols, :].T


def finish_second_kernel(
    place, a0, a1, a2, a3, b0, b1, b2, b3, gw2, gtf, ggw, ggb, gb1, gb2, gtb, gto, gtob, loss, parts, rest
):
    me, field = place[0], place[1]
    hidden = gw2.shape[1]
    piece = hidden // 4
    tasks, width, tower = gtf.shape
    experts = ggw.shape[1]
    units = tasks * experts
    domains = ggb.shape[0]
    tail = rest.shape[0] // 32
    half = (piece + tail + 1) // 2
    for s, (ref_a, ref_b) in enumerate(((a0, a1), (a2, a3), (b0, b1), (b2, b3))):
        for i in range(2):
            for z in range(4):
                p = ((s // 2) * 16 + ((s % 2) * 2 + i) * 4 + z) ^ me
                gw2[p // 4, pl.ds(pl.multiple_of((p % 4) * piece, 8), half), :] = ref_a[i, z]
                p = ((s // 2) * 16 + ((s % 2) + 2 * i) * 4 + z) ^ me
                at = pl.multiple_of((p % 4) * piece + half, 8)
                gw2[p // 4, pl.ds(at, piece - half), :] = ref_b[i, z, 0 : piece - half]
                parts[p] = ref_b[i, z, piece - half :]
    for p in range(32):
        rest[p * tail : (p + 1) * tail, :] = parts[p, 0:tail]
    gtf[0] = rest[0:width, 0:tower]
    gtf[1] = rest[0:width, tower:]
    gtf[2, 0:tower] = rest[width : width + tower, 0:tower]
    gtf[2, tower:] = rest[width : width + tower, tower:]
    base = width + tower
    mine = rest[pl.ds(pl.multiple_of(base + (field >> 1) * units, 8), units), :]
    mine = jnp.where((field & 1) == 0, mine[:, 0:tower], mine[:, tower:])
    for k in range(tasks):
        ggw[k] = mine[k * experts : (k + 1) * experts]
    base = base + 2 * units
    gb1[...] = rest[base : base + experts, :]
    gb2[...] = rest[base + experts : base + 2 * experts, :]
    base = base + 2 * experts
    ggb[...] = rest[base : base + domains, 0:units]
    misc = rest.shape[0] - 8
    for k in range(tasks):
        at = k
        gtb[k : k + 1] = rest[misc + at // 2 : misc + at // 2 + 1, (at % 2) * tower : (at % 2 + 1) * tower]
        at = tasks + k
        gto[k : k + 1] = rest[misc + at // 2 : misc + at // 2 + 1, (at % 2) * tower : (at % 2 + 1) * tower]
    gtob[...] = rest[misc + tasks : misc + tasks + 1, 0:tasks]
    loss[...] = rest[misc + tasks : misc + tasks + 1, tasks : tasks + 1]


def place_near_kernel(place, a0, a1, a2, a3, out, sems):
    copies = [
        pltpu.make_async_copy(ref, out.at[z ^ place[0]], sems.at[z]) for z, ref in enumerate((a0, a1, a2, a3))
    ]
    for copy in copies:
        copy.start()
    for copy in copies:
        copy.wait()


def place_far_kernel(place, b, begun, out, sems):
    copies = [pltpu.make_async_copy(b.at[z], out.at[(4 + z) ^ place[0]], sems.at[z]) for z in range(4)]
    for copy in copies:
        copy.start()
    for copy in copies:
        copy.wait()


def finish_inputs_kernel(place, factor, g0, g1, g2, g3, out):
    field = place[0]
    rows = g0.shape[0]
    for k, ref in enumerate((g0, g1, g2, g3)):
        out[pl.ds(pl.multiple_of((field ^ k) * rows, 8), rows), :] = ref[...] * factor[...]


def whole():
    return pl.BlockSpec(memory_space=VMEM)


def anywhere():
    return pl.BlockSpec(memory_space=pl.ANY)


def scalars():
    return pl.BlockSpec(memory_space=pltpu.SMEM)


def like(shape, dtype=F32):
    return jax.ShapeDtypeStruct(shape, dtype)


def after(value, *others):
    return lax.optimization_barrier((value, others))[0]


def per_device(
    n_dp,
    examples,
    domain,
    labels,
    row_counts,
    gate_weight,
    gate_bias,
    w_first,
    b_first,
    w_second,
    b_second,
    tower_first,
    tower_bias,
    tower_out,
    tower_out_bias,
):
    all_rows, cols = examples.shape
    rows = all_rows // 4
    experts, _, hidden = w_first.shape
    tasks = gate_weight.shape[0]
    width = w_second.shape[2]
    tower = tower_first.shape[2]
    domains = gate_bias.shape[0]
    units = tasks * experts
    field = lax.axis_index("field").astype(jnp.int32)
    group = lax.axis_index("dp").astype(jnp.int32)

    def move(value, dp_mask, field_mask):
        pairs = []
        for d in range(n_dp):
            for f in range(4):
                pairs.append((d * 4 + f, (d ^ dp_mask) * 4 + (f ^ field_mask)))
        return lax.ppermute(value, ("dp", "field"), pairs)

    def over_rest(value):
        mask = 8
        while mask < n_dp:
            value = value + move(value, mask, 0)
            mask *= 2
        return value

    core, chip_y = field & 1, field >> 1
    chip_x, chip_z = group & 1, (group >> 1) & 3
    me5 = core * 16 + chip_x * 8 + chip_y * 4 + chip_z
    me3 = chip_x * 4 + chip_z
    corner = group & 3

    count = row_counts[0]

    gate_rows = jnp.transpose(gate_weight, (0, 2, 1)).reshape(units, cols)
    quarter = experts // 4

    def rows_for(k):
        return lax.dynamic_slice(examples, ((field ^ k) * rows, 0), (rows, cols))

    far = move(lax.dynamic_slice(w_first, (corner * quarter, 0, 0), (quarter, cols, hidden)), 0, 2)
    near = move(w_first, 0, 1)
    place = jnp.stack([field * rows, count, me5, field, corner]).astype(jnp.int32)
    domain = domain.reshape(4, rows)
    x0 = rows_for(0)
    near_rows = jnp.concatenate([rows_for(1), gate_rows], axis=0)
    y_rows = jnp.concatenate([rows_for(2), rows_for(3), gate_rows], axis=0)
    early = (far, near, near_rows, y_rows, x0, place, domain)
    far, near, near_rows, y_rows, x0, place, domain = lax.optimization_barrier(early)

    x2 = move(y_rows, 0, 2)
    x1 = move(near_rows, 0, 1)
    far_a = [far] + [move(far, r, 0) for r in (1, 2, 3)]
    x1, x2, far_a = lax.optimization_barrier((x1, x2, far_a))

    x3 = move(x2, 0, 1)
    far_b = [move(piece, 0, 1) for piece in far_a]

    outs = pl.pallas_call(
        middle_kernel,
        name="middle",
        out_shape=(
            like((4 * cols, rows), BF16),
            like((4 * cols, rows), BF16),
            like((experts, hidden, rows), BF16),
            like((experts, hidden, rows), BF16),
            like((units, 4 * cols)),
            like((units, rows)),
            like((16, 40, width)),
            like((16, 40, width)),
            like((16, 40, width)),
            like((16, 40, width)),
        ),
        in_specs=[scalars()] * 2
        + [anywhere()] * 4
        + [whole()]
        + [anywhere()] * 10
        + [whole()] * 4
        + [anywhere()]
        + [whole()] * 4,
        out_specs=[anywhere()] * 4 + [whole()] * 2 + [anywhere()] * 4,
        scratch_shapes=[
            VMEM((8, hidden, rows), F32),
            VMEM((4, rows + units, cols), F32),
            VMEM((experts, 2 * cols, hidden), F32),
            VMEM((experts, 2 * cols, hidden), F32),
            VMEM((experts, hidden, width), F32),
            VMEM((4 * cols, rows), BF16),
            VMEM((4 * cols, rows), BF16),
            VMEM((experts, hidden, rows), BF16),
            VMEM((experts, hidden, rows), BF16),
            VMEM((experts, hidden, rows), BF16),
            VMEM((experts, hidden, rows), BF16),
            VMEM((experts, hidden, rows), F32),
            VMEM((experts, width, rows), F32),
            VMEM((units, rows), F32),
            VMEM((units, rows), F32),
            VMEM((2 * experts, hidden), F32),
            VMEM((tasks, width, rows), F32),
            VMEM((tasks, width, rows), F32),
            VMEM((units, rows), F32),
            VMEM((8, rows), F32),
            VMEM((8, rows), F32),
            VMEM((8, tower), F32),
            VMEM((32, 80, width), F32),
            VMEM((480, width), F32),
            pltpu.SemaphoreType.DMA((16,)),
        ],
        compiler_params=PARAMS,
    )(
        place,
        tower_out_bias,
        x0,
        x1,
        x2,
        x3,
        gate_rows,
        w_first,
        near,
        *far_a,
        *far_b,
        domain,
        labels.T,
        gate_bias,
        b_first,
        w_second,
        b_second,
        tower_first,
        tower_bias,
        tower_out,
    )
    xt_high, xt_low, gf_high, gf_low, gate_all, glog, sa_keep, sa_send, sb_keep, sb_send = outs

    place3 = me3.reshape(1)
    cheap = pl.CostEstimate(flops=0, bytes_accessed=1 << 20, transcendentals=0)

    def fold(keep, got, axis):
        held = keep + got
        return lax.index_in_dim(held, 0, axis, False), lax.index_in_dim(held, 1, axis, False)

    slots = (2, 2, 4, 40, width)
    sa, sa_out = fold(sa_keep.reshape(slots), move(sa_send, 0, 1).reshape(slots), 0)
    sb, sb_out = fold(sb_keep.reshape(slots), move(sb_send, 0, 1).reshape(slots), 1)
    sa, sa_out, sb, sb_out, gf_high = lax.optimization_barrier((sa, sa_out, sb, sb_out, gf_high))

    sa_got, sb_got = move(sa_out, 1, 0), move(sb_out, 0, 2)
    wa_keep, wa_send, wb_keep, wb_send = pl.pallas_call(
        first_kernel,
        name="first",
        out_shape=tuple(like((2, 8, cols // 2, hidden)) for _ in range(4)),
        in_specs=[scalars()] + [anywhere()] * 4,
        out_specs=[anywhere()] * 4,
        scratch_shapes=[
            VMEM((4 * cols, rows), BF16),
            VMEM((4 * cols, rows), BF16),
            VMEM((experts, hidden, rows), BF16),
            VMEM((experts, hidden, rows), BF16),
            VMEM((2, experts, cols, hidden), F32),
            VMEM((2, experts, cols, hidden), F32),
            pltpu.SemaphoreType.DMA((14,)),
        ],
        compiler_params=PARAMS,
        cost_estimate=cheap,
    )(place3, xt_high, xt_low, gf_high, gf_low)
    wa_got, wb_got = move(wa_send, 0, 1), move(wb_send, 0, 1)
    sa, sa_out = fold(sa, sa_got, 0)
    sb, sb_out = fold(sb, sb_got, 0)
    sa_got, sb_got = move(sa_out, 0, 2), move(sb_out, 1, 0)
    s_mine = jnp.concatenate([sa + sa_got, sb + sb_got], axis=1)
    slots = (2, 2, 4, cols // 2, hidden)
    wa, wa_out = fold(wa_keep.reshape(slots), wa_got.reshape(slots), 0)
    wb, wb_out = fold(wb_keep.reshape(slots), wb_got.reshape(slots), 1)
    stage = (wa, wa_out, wb, wb_out, s_mine, gf_low)
    wa, wa_out, wb, wb_out, s_mine, gf_low = lax.optimization_barrier(stage)

    wa_got, wb_got = move(wa_out, 0, 2), move(wb_out, 1, 0)
    s_got = [move(s_mine[z], 2 * z, 0) for z in (1, 2, 3)]
    wa, wa_out = fold(wa, wa_got, 0)
    wb, wb_out = fold(wb, wb_got, 0)
    wa_got, wb_got = move(wa_out, 1, 0), move(wb_out, 0, 2)
    s_piece = over_rest(s_mine[0] + s_got[0] + s_got[1] + s_got[2])
    factor = 1.0 / s_piece[79:80, 0:1]
    s_piece = s_piece * factor
    s_line = jnp.stack([s_piece] + [move(s_piece, 2 * z, 0) for z in (1, 2, 3)])
    w_mine = jnp.concatenate([wa + wa_got, wb + wb_got], axis=1)
    w_mine, s_line, gf_low = lax.optimization_barrier((w_mine, s_line, gf_low))

    g0, g1, g2, g3 = pl.pallas_call(
        inputs_kernel,
        name="inputs",
        out_shape=tuple(like((rows, cols)) for _ in range(4)),
        in_specs=[scalars()] + [whole()] * 2 + [anywhere()] * 12,
        out_specs=[whole()] * 4,
        scratch_shapes=[
            VMEM((experts, hidden, rows), BF16),
            VMEM((experts, hidden, rows), BF16),
            VMEM((experts, 2 * cols, hidden), F32),
            VMEM((experts, 2 * cols, hidden), F32),
            VMEM((4 * cols, rows), F32),
            pltpu.SemaphoreType.DMA((12,)),
        ],
        compiler_params=MEDIUM,
        cost_estimate=cheap,
    )(place, gate_all, glog, gf_high, gf_low, w_first, near, *far_a, *far_b)
    w_got = [move(w_mine[z], 2 * z, 0) for z in (1, 2, 3)]
    sa, sb = s_line[:, 0:40], s_line[:, 40:80]
    sa = jnp.stack([sa, move(sa, 0, 2)])
    sb = jnp.stack([sb, move(sb, 1, 0)])
    w_piece = over_rest(w_mine[0] + w_got[0] + w_got[1] + w_got[2]) * factor
    w_piece, sa, sb, g0, g1, g2, g3 = lax.optimization_barrier((w_piece, sa, sb, g0, g1, g2, g3))

    g1 = move(g1, 0, 1)
    w_line = [w_piece] + [move(w_piece, 2 * z, 0) for z in (1, 2, 3)]
    s_near = [sa, sb, move(sa, 1, 0), move(sb, 0, 2)]
    s_near, g2, g3 = lax.optimization_barrier((s_near, g2, g3))

    w_other = move(jnp.stack(w_line), 1, 0)
    g2 = move(g2, 0, 2)
    g3 = move(g3, 0, 3)
    s_far = [move(part, 0, 1) for part in s_near]

    seconds = pl.pallas_call(
        finish_second_kernel,
        name="finish_second",
        out_shape=(
            like((experts, hidden, width)),
            like((tasks, width, tower)),
            like((tasks, experts, cols)),
            like((domains, units)),
            like((experts, hidden)),
            like((experts, width)),
            like((tasks, tower)),
            like((tasks, tower)),
            like((1, tasks)),
            like((1, 1)),
        ),
        in_specs=[scalars()] + [whole()] * 8,
        out_specs=[whole()] * 10,
        scratch_shapes=[VMEM((32, 16, width), F32), VMEM((480, width), F32)],
        compiler_params=SMALL,
    )(jnp.stack([me5, field]), *s_near, *s_far)
    grad_w_second, grad_tower_first, grad_gate_weight, grad_gate_bias = seconds[:4]
    grad_b_first, grad_b_second, grad_tower_bias, grad_tower_out, grad_out_bias, loss = seconds[4:]

    grad_examples = pl.pallas_call(
        finish_inputs_kernel,
        name="finish_inputs",
        out_shape=like((all_rows, cols)),
        in_specs=[scalars()] + [whole()] * 5,
        out_specs=whole(),
        compiler_params=SMALL,
    )(field.reshape(1), factor, g0, g1, g2, g3)

    begun = pl.pallas_call(
        place_near_kernel,
        name="place_near",
        out_shape=like((experts, cols, hidden)),
        in_specs=[scalars()] + [anywhere()] * 4,
        out_specs=anywhere(),
        scratch_shapes=[pltpu.SemaphoreType.DMA((4,))],
        compiler_params=SMALL,
    )(place3, *w_line)
    grad_w_first = pl.pallas_call(
        place_far_kernel,
        name="place_far",
        out_shape=like((experts, cols, hidden)),
        in_specs=[scalars(), anywhere(), anywhere()],
        out_specs=anywhere(),
        scratch_shapes=[pltpu.SemaphoreType.DMA((4,))],
        input_output_aliases={2: 0},
        compiler_params=SMALL,
    )(place3, w_other, after(begun, grad_examples, grad_w_second))

    return (
        loss[0, 0],
        grad_examples,
        jnp.transpose(grad_gate_weight, (0, 2, 1)),
        grad_gate_bias,
        grad_w_first,
        grad_b_first,
        grad_w_second,
        grad_b_second,
        grad_tower_first,
        grad_tower_bias,
        grad_tower_out,
        grad_out_bias[0],
    )


def solution(mesh):
    placed = (
        P("dp", "field"),
        P("dp"),
        P("dp", None),
        P("dp"),
        P(None, "field", None),
        P(),
        P(None, "field", None),
        P(),
        P(),
        P(),
        P(),
        P(),
        P(),
        P(),
    )
    return jax.shard_map(
        functools.partial(per_device, mesh.shape["dp"]),
        mesh=mesh,
        in_specs=placed,
        out_specs=(
            P(),
            P("dp", "field"),
            P(None, "field", None),
            P(),
            P(None, "field", None),
            P(),
            P(),
            P(),
            P(),
            P(),
            P(),
            P(),
        ),
        check_vma=False,
    )
```
